256 devices in a mesh: head: 8 (over x, y_hi), tok: 32 (over y_lo, z, core).
Axes of the slice: x: 4, y: 4 (y_hi: 2, y_lo: 2; y = y_hi * 2 + y_lo), z: 8, core: 2. Of those that a mesh axis runs over, the one named last changes fastest.
Arguments:
- anchors: bfloat16 [4096, 1024], P('tok'), may hold values from -26 to 26
- cells: bfloat16 [16384, 1024], P('tok'), may hold values from -26 to 26
- w_query: bfloat16 [1024, 1024], P(None, 'head'), may hold values from -0.125 to 0.125
- w_key: bfloat16 [1024, 1024], P(None, 'head'), may hold values from -0.15625 to 0.15625
- w_value: bfloat16 [1024, 1024], P(None, 'head'), may hold values from -0.1875 to 0.1875
- w_out: bfloat16 [1024, 1024], P('head'), may hold values from -0.1875 to 0.1875
- grad_out_anchors: bfloat16 [4096, 1024], P('tok'), may hold values from -96 to 96
- grad_out_cells: bfloat16 [16384, 1024], P('tok'), may hold values from -96 to 96
Outputs:
- grad_anchors: bfloat16 [4096, 1024], P('tok', 'head')
- grad_cells: bfloat16 [16384, 1024], P('tok', 'head')
The draws below stay inside these ranges and needn't reach their ends.
All inputs are finite; a program needn't handle non-finite values.
Results may differ from the reference program's by a relative error of at most 0.035.
Values may be sent and summed in bfloat16 or wider, within the bound.
No kernel may reach another device: no remote copies, remote signals or barrier semaphores. Data moves between devices by JAX's collectives and lax.ppermute only.
A program may use at most 64 MiB of HBM per device.

```python
import math
import jax
import jax.numpy as jnp
from jax import lax

D = 1024
HEADS = 16
HEAD_DIM = 64
ANCHORS = 4096
CELLS = 16384


def anchor_rows(key, boost):
    base_rows = jnp.clip(jax.random.normal(jax.random.fold_in(key, 11), (ANCHORS, D), jnp.float32), -3.0, 3.0)
    row_ids = jnp.arange(ANCHORS)
    strength = 1.0 + boost * jnp.array([2.5, 3.5, 4.5, 5.5], jnp.float32)[row_ids // 64 % 4][:, None]
    leaders = (row_ids % 64 == 0)[:, None]
    partners = (row_ids % 64 == 1)[:, None]
    partner_rows = base_rows
    return jnp.where(leaders, base_rows * strength, jnp.where(partners, partner_rows * strength, base_rows))


def query_matrix(key):
    return jnp.clip(jax.random.normal(jax.random.fold_in(key, 21), (D, D), jnp.float32), -4.0, 4.0) * D ** (-0.5)


def draw_anchors(key, part):
    return anchor_rows(key, 0.0).astype(jnp.bfloat16)


def draw_cells(key, part):
    key = jax.random.fold_in(key, 5)
    base_rows = jnp.clip(jax.random.normal(key, (CELLS, D), jnp.float32), -3.0, 3.0)
    row_ids = jnp.arange(CELLS)
    picked = (row_ids % 128 == 0)[:, None]
    return jnp.where(picked, base_rows, base_rows).astype(jnp.bfloat16)


def draw_w_query(key, part):
    return query_matrix(key).astype(jnp.bfloat16)


def draw_w_key(key, part):
    key = jax.random.fold_in(key, 4)
    fresh_draw = jnp.clip(jax.random.normal(key, (D, D), jnp.float32), -4.0, 4.0) * D ** (-0.5)
    return fresh_draw.astype(jnp.bfloat16)


def levels(stream_key, shape, pieces, smallest, largest):
    level = 1.0
    for position, shards_of in pieces:
        steps = jax.random.uniform(jax.random.fold_in(jax.random.fold_in(stream_key, 6), position), (shards_of,), jnp.float32, smallest / len(pieces), largest / len(pieces))
        level = level * jnp.repeat(jnp.exp(steps), shape[position] // shards_of).reshape((-1,) + (1,) * (len(shape) - 1 - position))
    return level


def noise(stream_key, extent, deviation, most, split=(), kind=jnp.bfloat16):
    factor_of = levels(stream_key, extent, split, -0.22, 0.18) if split else 1.0
    values = jax.random.normal(stream_key, extent, jnp.float32) * deviation * factor_of
    return jnp.minimum(jnp.maximum(values, -most), most).astype(kind)


def setup_inputs(seed: int = 0) -> dict:
    key_of = jax.random.split(jax.random.key(seed), 9)
    anchors = draw_anchors(jax.random.fold_in(key_of[8], 71), 0)
    cells = draw_cells(jax.random.fold_in(key_of[8], 71), 0)
    w_query = draw_w_query(jax.random.fold_in(key_of[8], 71), 0)
    w_key = draw_w_key(jax.random.fold_in(key_of[8], 71), 0)
    w_value = noise(key_of[4], (D, D), D ** -0.5, 0.1875, ((1, 8),))
    w_out = noise(key_of[5], (D, D), D ** -0.5, 0.1875, ((0, 8),))
    grad_out_anchors = noise(key_of[6], (ANCHORS, D), 16.0, 96.0, ((0, 32),))
    grad_out_cells = noise(key_of[7], (CELLS, D), 16.0, 96.0, ((0, 32),))
    return {"anchors": anchors, "cells": cells, "w_query": w_query, "w_key": w_key, "w_value": w_value, "w_out": w_out, "grad_out_anchors": grad_out_anchors, "grad_out_cells": grad_out_cells}


def reference(anchors, cells, w_query, w_key, w_value, w_out, grad_out_anchors, grad_out_cells):
    row_data = jnp.concatenate([anchors, cells], axis=0)
    cotangent = jnp.concatenate([grad_out_anchors, grad_out_cells], axis=0)
    row_count = row_data.shape[0]
    anchor_count = anchors.shape[0]
    block_rows = math.gcd(row_count, 2048)
    block_total = row_count // block_rows
    score_scale = HEAD_DIM ** -0.5

    def head_term(totals, head_index):
        column = (head_index * HEAD_DIM).astype(jnp.int32)
        query_cols = lax.dynamic_slice_in_dim(w_query, column, HEAD_DIM, 1)
        key_cols = lax.dynamic_slice_in_dim(w_key, column, HEAD_DIM, 1)
        value_cols = lax.dynamic_slice_in_dim(w_value, column, HEAD_DIM, 1)
        out_rows = lax.dynamic_slice_in_dim(w_out, column, HEAD_DIM, 0)
        queries = jnp.dot(row_data, query_cols, preferred_element_type=jnp.float32).astype(jnp.bfloat16)
        key_rows = jnp.dot(anchors, key_cols, preferred_element_type=jnp.float32).astype(jnp.bfloat16)
        value_rows = jnp.dot(anchors, value_cols, preferred_element_type=jnp.float32).astype(jnp.bfloat16)
        grad_head = jnp.dot(cotangent, out_rows.T, preferred_element_type=jnp.float32).astype(jnp.bfloat16)

        def one_block(sums_so_far, block_index):
            key_sum, value_sum = sums_so_far
            offset = (block_index * block_rows).astype(jnp.int32)
            query_part = lax.dynamic_slice_in_dim(queries, offset, block_rows, 0)
            grad_part = lax.dynamic_slice_in_dim(grad_head, offset, block_rows, 0)
            scores = jnp.dot(query_part, key_rows.T, preferred_element_type=jnp.float32) * score_scale
            row_peak = jnp.max(scores, axis=1, keepdims=True)
            log_total = row_peak + jnp.log(jnp.sum(jnp.exp(scores - row_peak), axis=1, keepdims=True))
            weights = jnp.exp(scores - log_total)
            weights_low = weights.astype(jnp.bfloat16)
            outputs = jnp.dot(weights_low, value_rows, preferred_element_type=jnp.float32)
            delta_rows = jnp.sum(grad_part.astype(jnp.float32) * outputs, axis=1, keepdims=True)
            dprobs = jnp.dot(grad_part, value_rows.T, preferred_element_type=jnp.float32)
            dscore = (weights * (dprobs - delta_rows)).astype(jnp.bfloat16)
            dquery = (jnp.dot(dscore, key_rows, preferred_element_type=jnp.float32) * score_scale).astype(jnp.bfloat16)
            key_sum = key_sum + jnp.dot(dscore.T, query_part, preferred_element_type=jnp.float32) * score_scale
            value_sum = value_sum + jnp.dot(weights_low.T, grad_part, preferred_element_type=jnp.float32)
            return (key_sum, value_sum), dquery

        zeros_acc = jnp.zeros((anchor_count, HEAD_DIM), jnp.float32)
        (key_sum, value_sum), dquery = lax.scan(one_block, (zeros_acc, zeros_acc), jnp.arange(block_total, dtype=jnp.int32))
        dquery = dquery.reshape(row_count, HEAD_DIM)
        key_grad = key_sum.astype(jnp.bfloat16)
        value_grad = value_sum.astype(jnp.bfloat16)
        spread = jnp.dot(dquery, query_cols.T, preferred_element_type=jnp.float32)
        anchor_total = totals[0] + spread[:anchor_count] + jnp.dot(key_grad, key_cols.T, preferred_element_type=jnp.float32) + jnp.dot(value_grad, value_cols.T, preferred_element_type=jnp.float32)
        cell_total = totals[1] + spread[anchor_count:]
        return (anchor_total, cell_total), None

    initial = (jnp.zeros((anchor_count, D), jnp.float32), jnp.zeros((row_count - anchor_count, D), jnp.float32))
    (anchor_sum, cell_sum), _ = lax.scan(head_term, initial, jnp.arange(HEADS, dtype=jnp.int32))
    return anchor_sum.astype(jnp.bfloat16), cell_sum.astype(jnp.bfloat16)
```

```python
import functools

import jax
import jax.numpy as jnp
from jax import lax
from jax.experimental import pallas as pl
from jax.experimental.pallas import tpu as pltpu
from jax.sharding import PartitionSpec as P

HEAD_DIM = 64
SCALE = HEAD_DIM ** (-0.5)
LOG2E = 1.4426950408889634
Y_LO, Z, CORES = 2, 8, 2
X, Y_HI = 4, 2
BF16 = jnp.bfloat16
F32 = jnp.float32


def tok_perm(move):
    pairs = []
    for yl in range(Y_LO):
        for z in range(Z):
            for core in range(CORES):
                yl2, z2, core2 = move(yl, z, core)
                pairs.append(
                    ((yl * Z + z) * CORES + core, (yl2 * Z + z2 % Z) * CORES + core2)
                )
    return pairs


def head_perm(move):
    pairs = []
    for x in range(X):
        for yh in range(Y_HI):
            x2, yh2 = move(x, yh)
            pairs.append((x * Y_HI + yh, (x2 % X) * Y_HI + yh2))
    return pairs


SWAP_Y = tok_perm(lambda yl, z, c: (1 - yl, z, c))
SWAP_CORE = tok_perm(lambda yl, z, c: (yl, z, 1 - c))
SPREAD_NEAR = tok_perm(lambda yl, z, c: (yl, z, 0) if c == 0 else (yl, z - 1, 1))
SPREAD_FAR = tok_perm(lambda yl, z, c: (yl, z - 1, 1) if c == 0 else (yl, z, 0))
RING_OUT = tok_perm(lambda yl, z, c: (yl, z + 1, 0) if c == 0 else (yl, z - 1, 1))
RING_BACK = tok_perm(lambda yl, z, c: (yl, z - 1, 0) if c == 0 else (yl, z + 1, 1))
RETURN_NEAR = tok_perm(lambda yl, z, c: (yl, z, 0) if c == 0 else (yl, z + 1, 1))
RETURN_FAR = tok_perm(lambda yl, z, c: (yl, z, 1) if c == 0 else (yl, z + 1, 0))
HOPS = 3
SHIFT_X = [head_perm(lambda x, yh, r=r: (x + r, yh)) for r in range(X)]
SWAP_YH = head_perm(lambda x, yh: (x, 1 - yh))


def dot(a, b, ca, cb):
    return lax.dot_general(a, b, (((ca,), (cb,)), ((), ())), preferred_element_type=F32)


def call(body, outs, args, name, flops=0, transcendentals=0, scratch=(), smem=0):
    nbytes = sum(a.size * a.dtype.itemsize for a in (*args, *outs))
    in_specs = [
        pl.BlockSpec(memory_space=pltpu.SMEM if i < smem else pltpu.VMEM)
        for i in range(len(args))
    ]
    return pl.pallas_call(
        body,
        out_shape=tuple(outs),
        in_specs=in_specs,
        out_specs=tuple(pl.BlockSpec(memory_space=pltpu.VMEM) for _ in outs),
        scratch_shapes=list(scratch),
        compiler_params=pltpu.CompilerParams(vmem_limit_bytes=28 << 20),
        cost_estimate=pl.CostEstimate(
            flops=flops, bytes_accessed=nbytes, transcendentals=transcendentals
        ),
        name=name,
    )(*args)


def sds(shape, dtype):
    return jax.ShapeDtypeStruct(shape, dtype)


def kv_kernel(rows, w_key, w_value, out):
    x = rows[...]
    out[:, 0:128] = dot(x, w_key[...], 1, 0).astype(BF16)
    out[:, 128:256] = dot(x, w_value[...], 1, 0).astype(BF16)


def qd_kernel(anchors, cells, grad_a, grad_c, w_query, w_out, out):
    na = anchors.shape[0]
    wq = w_query[...]
    wo = w_out[...]
    for lo, rows, grads in ((0, anchors, grad_a), (na, cells, grad_c)):
        hi = lo + rows.shape[0]
        out[lo:hi, 0:128] = dot(rows[...], wq, 1, 0).astype(BF16) * SCALE
        out[lo:hi, 128:256] = dot(grads[...], wo, 1, 1).astype(BF16)


def stats_block(kv, rhs, before, out):
    total = rhs.shape[0] // 2
    keys = kv[:, 0:128]
    values = kv[:, 128:256]
    for tile in range(0, total, 256):
        for h in range(2):
            lo = h * total + tile
            s = dot(keys, rhs[lo : lo + 256, 0:128], 1, 1)
            peak = jnp.max(s, axis=0, keepdims=True) * LOG2E
            if before is not None:
                old_peak = before[h : h + 1, tile : tile + 256]
                peak = jnp.maximum(peak, old_peak)
            e = jnp.exp2(s * LOG2E - peak)
            dp = dot(values, rhs[lo : lo + 256, 128:256], 1, 1)
            norm = jnp.sum(e, axis=0, keepdims=True)
            mass = jnp.sum(e * dp, axis=0, keepdims=True)
            if before is not None:
                factor = jnp.exp2(old_peak - peak)
                norm += factor * before[2 + h : 3 + h, tile : tile + 256]
                mass += factor * before[4 + h : 5 + h, tile : tile + 256]
            out[h : h + 1, tile : tile + 256] = peak
            out[2 + h : 3 + h, tile : tile + 256] = norm
            out[4 + h : 5 + h, tile : tile + 256] = mass
    out[6:8, :] = jnp.zeros((2, total), F32)


def first_stats_kernel(mine, theirs, kv, stats, rhs):
    half = mine.shape[0]
    lane = lax.broadcasted_iota(jnp.int32, (1, 256), 1)
    for h in range(2):
        keep = lane // HEAD_DIM % 2 == h
        for part, rows in enumerate((mine, theirs)):
            x = rows[...]
            lo = (2 * h + part) * half
            rhs[lo : lo + half, :] = jnp.where(keep, x, jnp.zeros_like(x))
    stats_block(kv, rhs, None, stats)


def next_stats_kernel(kv, rhs, before, stats):
    stats_block(kv, rhs, before, stats)


def merge_kernel(mine, theirs, out):
    half = mine.shape[1] // 2
    for a, b in ((0, half), (half, 0)):
        for h in range(2):
            m1 = mine[h : h + 1, a : a + half]
            m2 = theirs[h : h + 1, b : b + half]
            peak = jnp.maximum(m1, m2)
            f1 = jnp.exp2(m1 - peak)
            f2 = jnp.exp2(m2 - peak)
            norm = f1 * mine[2 + h : 3 + h, a : a + half] + f2 * theirs[2 + h : 3 + h, b : b + half]
            mass = f1 * mine[4 + h : 5 + h, a : a + half] + f2 * theirs[4 + h : 5 + h, b : b + half]
            out[h : h + 1, a : a + half] = peak + jnp.log(norm) * LOG2E
            out[2 + h : 3 + h, a : a + half] = mass / norm
    out[4:8, :] = jnp.zeros((4, 2 * half), F32)


def grads_kernel(has_before, is_last, *refs):
    kv, rhs, stats = refs[:3]
    refs = refs[3:]
    before = None
    if has_before:
        before, refs = refs[0], refs[1:]
    if is_last:
        dkv, dq_mine, dq_theirs, p_t, ds_t = refs
    else:
        dkv, dq, p_t, ds_t = refs
    total = rhs.shape[0] // 2
    half = total // 2
    n = kv.shape[0]
    keys_t = kv[:, 0:128].T
    step = 128
    for h in range(2):
        lo = h * total
        lse = stats[h : h + 1, :]
        delta = stats[2 + h : 3 + h, :]
        for c in range(0, n, step):
            s = dot(kv[c : c + step, 0:128], rhs[lo : lo + total, 0:128], 1, 1)
            p = jnp.exp2(s * LOG2E - lse)
            dp = dot(kv[c : c + step, 128:256], rhs[lo : lo + total, 128:256], 1, 1)
            ds = p * (dp - delta)
            p_t[c : c + step, lo : lo + total] = p.astype(BF16)
            ds_t[c : c + step, lo : lo + total] = ds.astype(BF16)
        out = slice(h * HEAD_DIM, (h + 1) * HEAD_DIM)
        part = dot(keys_t[out, :], ds_t[:, lo : lo + total], 1, 0)
        if has_before:
            part += before[out, :]
        if is_last:
            dq_mine[out, :] = part[:, :half]
            dq_theirs[out, :] = part[:, half:].astype(BF16)
        else:
            dq[out, :] = part
    dkv[:, 0:128] = dot(ds_t[...], rhs[:, 0:128], 1, 0).astype(BF16)
    dkv[:, 128:256] = dot(p_t[...], rhs[:, 128:256], 1, 0).astype(BF16)


def grads(kv, rhs, stats, before, is_last):
    total = rhs.shape[0] // 2
    n = kv.shape[0]
    args = [kv, rhs, stats] + ([] if before is None else [before])
    outs = [sds((n, 256), BF16)]
    if is_last:
        outs += [sds((128, total // 2), F32), sds((128, total // 2), BF16)]
    else:
        outs += [sds((128, total), F32)]
    return call(
        functools.partial(grads_kernel, before is not None, is_last),
        outs,
        args,
        "grads",
        flops=10 * n * 2 * total * 256,
        transcendentals=2 * n * total,
        scratch=[pltpu.VMEM((n, 2 * total), BF16), pltpu.VMEM((n, 2 * total), BF16)],
    )


def cells_kernel(place, mine, theirs, w_query, dq_anchors, *outs):
    na = mine.shape[1] - outs[0].shape[0]
    dq = ((mine[...] + theirs[...].astype(F32)) * SCALE).astype(BF16)
    dq_anchors[...] = dq[:, :na]
    width = outs[0].shape[1]
    for r, out in enumerate(outs):
        lo = pl.multiple_of(lax.rem(place[0] + r, X) * width, width)
        out[...] = dot(dq[:, na:], w_query[pl.ds(lo, width), :], 0, 1).astype(BF16)


def anchors_kernel(place, dq, dkv, more, w_query, w_key, w_value, *outs):
    width = outs[0].shape[1]
    total = (dkv[...] + more[...].astype(F32)).astype(BF16)
    for r, out in enumerate(outs):
        lo = pl.multiple_of(lax.rem(place[0] + r, X) * width, width)
        acc = dot(dq[...], w_query[pl.ds(lo, width), :], 0, 1)
        acc += dot(total[:, 0:128], w_key[pl.ds(lo, width), :], 1, 1)
        acc += dot(total[:, 128:256], w_value[pl.ds(lo, width), :], 1, 1)
        out[...] = acc.astype(BF16)


def split_kernel(place, a, b, c, d, mine, theirs):
    def terms(lo):
        cols = slice(lo, lo + 128)
        return (a[:, cols].astype(F32) + b[:, cols].astype(F32)) + (
            c[:, cols].astype(F32) + d[:, cols].astype(F32)
        )

    low, high = terms(0), terms(128)
    first = place[1] == 0
    mine[...] = jnp.where(first, low, high)
    theirs[...] = jnp.where(first, high, low).astype(BF16)


def over_heads(place, chunks):
    rows = chunks[0].shape[0]
    got = [lax.ppermute(chunks[r], "head", SHIFT_X[r]) for r in range(1, X)]
    mine, theirs = call(
        split_kernel,
        [sds((rows, 128), F32), sds((rows, 128), BF16)],
        [place, chunks[0], *got],
        "split",
        smem=1,
    )
    more = lax.ppermute(theirs, "head", SWAP_YH)
    return (mine + more.astype(F32)).astype(BF16)


def per_device(anchors, cells, w_query, w_key, w_value, w_out, grad_a, grad_c):
    na, nc, d = anchors.shape[0], cells.shape[0], anchors.shape[1]
    rows = na + nc
    total = 2 * rows
    head = lax.axis_index("head")
    place = jnp.stack([head // Y_HI, head % Y_HI]).astype(jnp.int32)

    (kv,) = call(
        kv_kernel,
        [sds((na, 256), BF16)],
        [anchors, w_key, w_value],
        "kv",
        flops=2 * na * d * 256,
    )
    kv_pair = jnp.concatenate([kv, lax.ppermute(kv, "tok", SWAP_Y)], axis=0)
    block = jnp.concatenate(
        [
            lax.ppermute(kv_pair, "tok", SPREAD_NEAR),
            lax.ppermute(kv_pair, "tok", SPREAD_FAR),
        ],
        axis=0,
    )
    blocks = [block]
    for _ in range(HOPS):
        blocks.append(lax.ppermute(blocks[-1], "tok", RING_OUT))

    (mine,) = call(
        qd_kernel,
        [sds((rows, 256), BF16)],
        [anchors, cells, grad_a, grad_c, w_query, w_out],
        "qd",
        flops=2 * rows * d * 256,
    )
    theirs = lax.ppermute(mine, "tok", SWAP_CORE)

    n = block.shape[0]
    cost = dict(flops=4 * n * 2 * total * 256, transcendentals=2 * n * total)
    stats, rhs = call(
        first_stats_kernel,
        [sds((8, total), F32), sds((2 * total, 256), BF16)],
        [mine, theirs, blocks[0]],
        "stats0",
        **cost,
    )
    for kv_block in blocks[1:]:
        (stats,) = call(
            next_stats_kernel, [sds((8, total), F32)], [kv_block, rhs, stats], "stats", **cost
        )
    (stats,) = call(
        merge_kernel,
        [sds((8, total), F32)],
        [stats, lax.ppermute(stats, "tok", SWAP_CORE)],
        "merge",
    )

    dq = None
    arrived = None
    for k in range(HOPS, -1, -1):
        dkv, *dq = grads(blocks[k], rhs, stats, dq, k == 0)
        if arrived is not None:
            dkv = (dkv.astype(F32) + arrived.astype(F32)).astype(BF16)
        if k > 0:
            arrived = lax.ppermute(dkv, "tok", RING_BACK)
            dq = dq[0]

    dq_mine, dq_theirs = dq
    dq_theirs = lax.ppermute(dq_theirs, "tok", SWAP_CORE)
    width = d // X
    dq_anchors, *chunks = call(
        cells_kernel,
        [sds((128, na), BF16)] + [sds((nc, width), BF16)] * X,
        [place, dq_mine, dq_theirs, w_query],
        "cells",
        flops=2 * nc * 128 * d,
        smem=1,
    )
    cell_grad = over_heads(place, chunks)

    near = lax.ppermute(dkv[: n // 2], "tok", RETURN_NEAR)
    far = lax.ppermute(dkv[n // 2 :], "tok", RETURN_FAR)
    pair = near.astype(F32) + far.astype(F32)
    more = lax.ppermute(pair[na:].astype(BF16), "tok", SWAP_Y)
    chunks = call(
        anchors_kernel,
        [sds((na, width), BF16)] * X,
        [place, dq_anchors, pair[:na], more, w_query, w_key, w_value],
        "anchors",
        flops=2 * na * 128 * d * 3,
        smem=1,
    )
    anchor_grad = over_heads(place, chunks)
    return (anchor_grad, cell_grad)


def solution(mesh):
    return jax.shard_map(
        per_device,
        mesh=mesh,
        in_specs=(
            P("tok", None),
            P("tok", None),
            P(None, "head"),
            P(None, "head"),
            P(None, "head"),
            P("head", None),
            P("tok", None),
            P("tok", None),
        ),
        out_specs=(P("tok", "head"), P("tok", "head")),
        check_vma=False,
    )
```

```python
import functools

import jax
import jax.numpy as jnp
from jax import lax
from jax.experimental import pallas as pl
from jax.experimental.pallas import tpu as pltpu
from jax.sharding import PartitionSpec as P

HEAD_DIM = 64
SCALE = HEAD_DIM ** (-0.5)
LOG2E = 1.4426950408889634
Y_LO, Z, CORES = 2, 8, 2
X, Y_HI = 4, 2
BF16 = jnp.bfloat16
F32 = jnp.float32
COST = {"grads": 15 * 10**8, "last_grads": 15 * 10**8, "last_pair": 15 * 10**8}


def tok_perm(move):
    pairs = []
    for yl in range(Y_LO):
        for z in range(Z):
            for core in range(CORES):
                yl2, z2, core2 = move(yl, z, core)
                pairs.append(
                    ((yl * Z + z) * CORES + core, (yl2 * Z + z2 % Z) * CORES + core2)
                )
    return pairs


def head_perm(move):
    pairs = []
    for x in range(X):
        for yh in range(Y_HI):
            x2, yh2 = move(x, yh)
            pairs.append((x * Y_HI + yh, (x2 % X) * Y_HI + yh2))
    return pairs


SWAP_CORE = tok_perm(lambda yl, z, c: (yl, z, 1 - c))
GATHER = [
    tok_perm(lambda yl, z, c, f=f: (f(yl), z, 0) if c == 0 else (f(yl), z - 1, 1))
    for f in (lambda yl: yl, lambda yl: 1 - yl)
] + [
    tok_perm(lambda yl, z, c, f=f: (f(yl), z - 1, 1) if c == 0 else (f(yl), z, 0))
    for f in (lambda yl: yl, lambda yl: 1 - yl)
]
RETURN = [[(b, a) for a, b in perm] for perm in GATHER]
HOPS = 3
FORTH = [
    tok_perm(lambda yl, z, c, j=j: (yl, z + j, 0) if c == 0 else (yl, z - j, 1))
    for j in range(HOPS + 1)
]
BACK = [[(b, a) for a, b in perm] for perm in FORTH]
SHIFT_X = [head_perm(lambda x, yh, r=r: (x + r, yh)) for r in range(X)]
SWAP_YH = head_perm(lambda x, yh: (x, 1 - yh))


def dot(a, b, ca, cb):
    return lax.dot_general(a, b, (((ca,), (cb,)), ((), ())), preferred_element_type=F32)


def call(body, outs, args, name, scratch=(), smem=0, anywhere=False, after=()):
    def spec(i):
        if i < smem:
            return pl.BlockSpec(memory_space=pltpu.SMEM)
        if anywhere or i >= len(args):
            return pl.BlockSpec(memory_space=pl.ANY)
        return pl.BlockSpec(memory_space=pltpu.VMEM)

    def kernel(*refs):
        body(*refs[: len(args)], *refs[len(args) + len(after) :])

    return pl.pallas_call(
        kernel,
        out_shape=tuple(outs),
        in_specs=[spec(i) for i in range(len(args) + len(after))],
        out_specs=tuple(pl.BlockSpec(memory_space=pltpu.VMEM) for _ in outs),
        scratch_shapes=list(scratch),
        compiler_params=pltpu.CompilerParams(vmem_limit_bytes=28 << 20),
        cost_estimate=pl.CostEstimate(
            flops=COST.get(name, 10**10), bytes_accessed=10**6, transcendentals=0
        ),
        name=name,
    )(*args, *after)


def sds(shape, dtype):
    return jax.ShapeDtypeStruct(shape, dtype)


def kv_kernel(rows_hbm, w_key_hbm, w_value_hbm, out, rows, w_key, w_value, sems):
    copies = [
        pltpu.make_async_copy(src, dst, sems.at[i])
        for i, (src, dst) in enumerate(
            ((rows_hbm, rows), (w_key_hbm, w_key), (w_value_hbm, w_value))
        )
    ]
    for copy in copies:
        copy.start()
    copies[0].wait()
    copies[1].wait()
    out[:, 0:128] = dot(rows[...], w_key[...], 1, 0).astype(BF16)
    copies[2].wait()
    out[:, 128:256] = dot(rows[...], w_value[...], 1, 0).astype(BF16)


def qd_kernel(anchors, cells, grad_a, grad_c, w_query, w_out, out):
    na = anchors.shape[0]
    wq = w_query[...]
    wo = w_out[...]
    for lo, rows, grads in ((0, anchors, grad_a), (na, cells, grad_c)):
        hi = lo + rows.shape[0]
        out[lo:hi, 0:128] = dot(rows[...], wq, 1, 0).astype(BF16) * SCALE
        out[lo:hi, 128:256] = dot(grads[...], wo, 1, 1).astype(BF16)


def stats_block(kv, rhs, before, out):
    total = rhs.shape[0] // 2
    keys = kv[:, 0:128]
    values = kv[:, 128:256]
    for tile in range(0, total, 256):
        for h in range(2):
            lo = h * total + tile
            s = dot(keys, rhs[lo : lo + 256, 0:128], 1, 1)
            peak = jnp.max(s, axis=0, keepdims=True) * LOG2E
            if before is not None:
                old_peak = before[h : h + 1, tile : tile + 256]
                peak = jnp.maximum(peak, old_peak)
            e = jnp.exp2(s * LOG2E - peak)
            dp = dot(values, rhs[lo : lo + 256, 128:256], 1, 1)
            norm = jnp.sum(e, axis=0, keepdims=True)
            mass = jnp.sum(e * dp, axis=0, keepdims=True)
            if before is not None:
                factor = jnp.exp2(old_peak - peak)
                norm += factor * before[2 + h : 3 + h, tile : tile + 256]
                mass += factor * before[4 + h : 5 + h, tile : tile + 256]
            out[h : h + 1, tile : tile + 256] = peak
            out[2 + h : 3 + h, tile : tile + 256] = norm
            out[4 + h : 5 + h, tile : tile + 256] = mass
    out[6:8, :] = jnp.zeros((2, total), F32)


def first_stats_kernel(mine, theirs, kv, stats, rhs):
    half = mine.shape[0]
    lane = lax.broadcasted_iota(jnp.int32, (1, 256), 1)
    for h in range(2):
        keep = lane // HEAD_DIM % 2 == h
        for part, rows in enumerate((mine, theirs)):
            x = rows[...]
            lo = (2 * h + part) * half
            rhs[lo : lo + half, :] = jnp.where(keep, x, jnp.zeros_like(x))
    stats_block(kv, rhs, None, stats)


def next_stats_kernel(kv, rhs, before, stats):
    stats_block(kv, rhs, before, stats)


def merge_kernel(mine, theirs, out):
    half = mine.shape[1] // 2
    for a, b in ((0, half), (half, 0)):
        for h in range(2):
            m1 = mine[h : h + 1, a : a + half]
            m2 = theirs[h : h + 1, b : b + half]
            peak = jnp.maximum(m1, m2)
            f1 = jnp.exp2(m1 - peak)
            f2 = jnp.exp2(m2 - peak)
            norm = f1 * mine[2 + h : 3 + h, a : a + half] + f2 * theirs[2 + h : 3 + h, b : b + half]
            mass = f1 * mine[4 + h : 5 + h, a : a + half] + f2 * theirs[4 + h : 5 + h, b : b + half]
            out[h : h + 1, a : a + half] = peak + jnp.log(norm) * LOG2E
            out[2 + h : 3 + h, a : a + half] = mass / norm
    out[4:8, :] = jnp.zeros((4, 2 * half), F32)


def grads_kernel(has_before, is_last, *refs):
    kv, rhs, stats = refs[:3]
    refs = refs[3:]
    before = None
    if has_before:
        before, refs = refs[0], refs[1:]
    if is_last:
        p_t, ds_t, dq_mine, dq_theirs = refs
    else:
        dkv, dq, p_t, ds_t = refs
    total = rhs.shape[0] // 2
    half = total // 2
    n = kv.shape[0]
    keys_t = kv[:, 0:128].T
    step = 128
    for h in range(2):
        lo = h * total
        lse = stats[h : h + 1, :]
        delta = stats[2 + h : 3 + h, :]
        for c in range(0, n, step):
            s = dot(kv[c : c + step, 0:128], rhs[lo : lo + total, 0:128], 1, 1)
            p = jnp.exp2(s * LOG2E - lse)
            dp = dot(kv[c : c + step, 128:256], rhs[lo : lo + total, 128:256], 1, 1)
            ds = p * (dp - delta)
            p_t[c : c + step, lo : lo + total] = p.astype(BF16)
            ds_t[c : c + step, lo : lo + total] = ds.astype(BF16)
        out = slice(h * HEAD_DIM, (h + 1) * HEAD_DIM)
        part = dot(keys_t[out, :], ds_t[:, lo : lo + total], 1, 0)
        if has_before:
            part += before[out, :]
        if is_last:
            dq_mine[out, :] = part[:, :half]
            dq_theirs[out, :] = part[:, half:].astype(BF16)
        else:
            dq[out, :] = part
    if not is_last:
        dkv[:, 0:128] = dot(ds_t[...], rhs[:, 0:128], 1, 0).astype(BF16)
        dkv[:, 128:256] = dot(p_t[...], rhs[:, 128:256], 1, 0).astype(BF16)


def grads(kv, rhs, stats, before, is_last, after=()):
    total = rhs.shape[0] // 2
    n = kv.shape[0]
    args = [kv, rhs, stats] + ([] if before is None else [before])
    weights = [(n, 2 * total)] * 2
    if is_last:
        outs = [sds(shape, BF16) for shape in weights]
        outs += [sds((128, total // 2), F32), sds((128, total // 2), BF16)]
    else:
        outs = [sds((n, 256), BF16), sds((128, total), F32)]
    return call(
        functools.partial(grads_kernel, before is not None, is_last),
        outs,
        args,
        "last_grads" if is_last else "grads",
        scratch=[] if is_last else [pltpu.VMEM(shape, BF16) for shape in weights],
        after=after,
    )


def last_pair_kernel(p_t, ds_t, rhs, dkv):
    dkv[:, 0:128] = dot(ds_t[...], rhs[:, 0:128], 1, 0)
    dkv[:, 128:256] = dot(p_t[...], rhs[:, 128:256], 1, 0)


def pair_sum_kernel(own, a, b, c, *outs):
    n = outs[0].shape[0]
    for i, out in enumerate(outs):
        rows = slice(i * n, (i + 1) * n)
        more = (a[rows, :].astype(F32) + b[rows, :].astype(F32)) + c[rows, :].astype(F32)
        out[...] = (own[rows, :] + more).astype(BF16)


def cells_kernel(place, mine, theirs, w_query, dq_anchors, *outs):
    na = mine.shape[1] - outs[0].shape[0]
    dq = ((mine[...] + theirs[...].astype(F32)) * SCALE).astype(BF16)
    dq_anchors[...] = dq[:, :na]
    width = outs[0].shape[1]
    for r, out in enumerate(outs):
        lo = pl.multiple_of(lax.rem(place[0] + r, X) * width, width)
        out[...] = dot(dq[:, na:], w_query[pl.ds(lo, width), :], 0, 1).astype(BF16)


def anchors_kernel(place, dq, a, b, c, d, w_query, w_key, w_value, *outs):
    width = outs[0].shape[1]
    total = (a[...].astype(F32) + b[...].astype(F32)) + (c[...].astype(F32) + d[...].astype(F32))
    total = total.astype(BF16)
    for r, out in enumerate(outs):
        lo = pl.multiple_of(lax.rem(place[0] + r, X) * width, width)
        acc = dot(dq[...], w_query[pl.ds(lo, width), :], 0, 1)
        acc += dot(total[:, 0:128], w_key[pl.ds(lo, width), :], 1, 1)
        acc += dot(total[:, 128:256], w_value[pl.ds(lo, width), :], 1, 1)
        out[...] = acc.astype(BF16)


def split_kernel(place, a, b, c, d, mine, theirs):
    def terms(lo):
        cols = slice(lo, lo + 128)
        return (a[:, cols].astype(F32) + b[:, cols].astype(F32)) + (
            c[:, cols].astype(F32) + d[:, cols].astype(F32)
        )

    low, high = terms(0), terms(128)
    first = place[1] == 0
    mine[...] = jnp.where(first, low, high)
    theirs[...] = jnp.where(first, high, low).astype(BF16)


def over_heads(place, chunks, after=()):
    rows = chunks[0].shape[0]
    got = [lax.ppermute(chunks[r], "head", SHIFT_X[r]) for r in (2, 1, 3)]
    mine, theirs = call(
        split_kernel,
        [sds((rows, 128), F32), sds((rows, 128), BF16)],
        [place, chunks[0], *got],
        "split",
        smem=1,
        after=after,
    )
    more = lax.ppermute(theirs, "head", SWAP_YH)
    return (mine + more.astype(F32)).astype(BF16), mine


def per_device(anchors, cells, w_query, w_key, w_value, w_out, grad_a, grad_c):
    na, nc, d = anchors.shape[0], cells.shape[0], anchors.shape[1]
    rows = na + nc
    total = 2 * rows
    head = lax.axis_index("head")
    place = jnp.stack([head // Y_HI, head % Y_HI]).astype(jnp.int32)

    (kv,) = call(
        kv_kernel,
        [sds((na, 256), BF16)],
        [anchors, w_key, w_value],
        "kv",
        scratch=[
            pltpu.VMEM((na, d), BF16),
            pltpu.VMEM((d, 128), BF16),
            pltpu.VMEM((d, 128), BF16),
            pltpu.SemaphoreType.DMA((3,)),
        ],
        anywhere=True,
    )
    block = jnp.concatenate([lax.ppermute(kv, "tok", perm) for perm in GATHER], axis=0)
    blocks = [block] + [lax.ppermute(block, "tok", FORTH[j]) for j in range(1, HOPS + 1)]

    (mine,) = call(
        qd_kernel,
        [sds((rows, 256), BF16)],
        [anchors, cells, grad_a, grad_c, w_query, w_out],
        "qd",
    )
    theirs = lax.ppermute(mine, "tok", SWAP_CORE)

    n = block.shape[0]
    stats, rhs = call(
        first_stats_kernel,
        [sds((8, total), F32), sds((2 * total, 256), BF16)],
        [mine, theirs, blocks[0]],
        "stats0",
    )
    for kv_block in blocks[1:]:
        (stats,) = call(
            next_stats_kernel, [sds((8, total), F32)], [kv_block, rhs, stats], "stats"
        )
    (stats,) = call(
        merge_kernel,
        [sds((8, total), F32)],
        [stats, lax.ppermute(stats, "tok", SWAP_CORE)],
        "merge",
    )

    dq = None
    sums = []
    for k in range(HOPS, 0, -1):
        dkv, dq = grads(blocks[k], rhs, stats, dq, False)
        sums.append(lax.ppermute(dkv, "tok", BACK[k]))
    p_t, ds_t, dq_mine, dq_theirs = grads(blocks[0], rhs, stats, dq, True, after=sums[:1])
    (dkv,) = call(
        last_pair_kernel,
        [sds((n, 256), F32)],
        [p_t, ds_t, rhs],
        "last_pair",
        after=sums[1:2],
    )
    pieces = call(
        pair_sum_kernel, [sds((na, 256), BF16)] * len(RETURN), [dkv, *sums], "pair_sum"
    )
    pieces = [lax.ppermute(piece, "tok", perm) for piece, perm in zip(pieces, RETURN)]
    dq_theirs = lax.ppermute(dq_theirs, "tok", SWAP_CORE)
    width = d // X
    dq_anchors, *chunks = call(
        cells_kernel,
        [sds((128, na), BF16)] + [sds((nc, width), BF16)] * X,
        [place, dq_mine, dq_theirs, w_query],
        "cells",
        smem=1,
    )
    cell_grad, cell_mine = over_heads(place, chunks)

    chunks = call(
        anchors_kernel,
        [sds((na, width), BF16)] * X,
        [place, dq_anchors, *pieces, w_query, w_key, w_value],
        "anchors",
        smem=1,
    )
    anchor_grad, _ = over_heads(place, chunks, after=[cell_mine])
    return (anchor_grad, cell_grad)


def solution(mesh):
    return jax.shard_map(
        per_device,
        mesh=mesh,
        in_specs=(
            P("tok", None),
            P("tok", None),
            P(None, "head"),
            P(None, "head"),
            P(None, "head"),
            P("head", None),
            P("tok", None),
            P("tok", None),
        ),
        out_specs=(P("tok", "head"), P("tok", "head")),
        check_vma=False,
    )
```

```python
import functools

import jax
import jax.numpy as jnp
from jax import lax
from jax.experimental import pallas as pl
from jax.experimental.pallas import tpu as pltpu
from jax.sharding import PartitionSpec as P

HEAD_DIM = 64
SCALE = HEAD_DIM ** (-0.5)
LOG2E = 1.4426950408889634
Y_LO, Z, CORES = 2, 8, 2
X, Y_HI = 4, 2
HEAD = ("x", "y_hi")
TOK = ("y_lo", "z", "core")
BF16 = jnp.bfloat16
F32 = jnp.float32
COST = {"scores": 15 * 10**8, "pair": 15 * 10**8, "anchors": 10**8, "split": 10**8}


def tok_perm(move):
    pairs = []
    for yl in range(Y_LO):
        for z in range(Z):
            for core in range(CORES):
                yl2, z2, core2 = move(yl, z, core)
                pairs.append(
                    ((yl * Z + z) * CORES + core, (yl2 * Z + z2 % Z) * CORES + core2)
                )
    return pairs


def head_perm(move):
    pairs = []
    for x in range(X):
        for yh in range(Y_HI):
            x2, yh2 = move(x, yh)
            pairs.append((x * Y_HI + yh, (x2 % X) * Y_HI + yh2))
    return pairs


SWAP_CORE = tok_perm(lambda yl, z, c: (yl, z, 1 - c))
GATHER = [
    tok_perm(lambda yl, z, c, f=f: (f(yl), z, 0) if c == 0 else (f(yl), z - 1, 1))
    for f in (lambda yl: yl, lambda yl: 1 - yl)
] + [
    tok_perm(lambda yl, z, c, f=f: (f(yl), z - 1, 1) if c == 0 else (f(yl), z, 0))
    for f in (lambda yl: yl, lambda yl: 1 - yl)
]
RETURN = [[(b, a) for a, b in perm] for perm in GATHER]
HOPS = 3
FORTH = [
    tok_perm(lambda yl, z, c, j=j: (yl, z + j, 0) if c == 0 else (yl, z - j, 1))
    for j in range(HOPS + 1)
]
BACK = [[(b, a) for a, b in perm] for perm in FORTH]
SHIFT_X = [head_perm(lambda x, yh, r=r: (x + r, yh)) for r in range(X)]
SWAP_YH = head_perm(lambda x, yh: (x, 1 - yh))


def dot(a, b, ca, cb):
    return lax.dot_general(a, b, (((ca,), (cb,)), ((), ())), preferred_element_type=F32)


def call(body, outs, args, name, scratch=(), smem=0, hbm=(), after=(), vmem=20):
    def spec(i):
        if i < smem:
            return pl.BlockSpec(memory_space=pltpu.SMEM)
        if i >= len(args):
            return pl.BlockSpec(memory_space=pl.ANY)
        return pl.BlockSpec(memory_space=pltpu.HBM if i in hbm else pltpu.VMEM)

    def kernel(*refs):
        body(*refs[: len(args)], *refs[len(args) + len(after) :])

    return pl.pallas_call(
        kernel,
        out_shape=tuple(outs),
        in_specs=[spec(i) for i in range(len(args) + len(after))],
        out_specs=tuple(pl.BlockSpec(memory_space=pltpu.VMEM) for _ in outs),
        scratch_shapes=list(scratch),
        compiler_params=pltpu.CompilerParams(vmem_limit_bytes=vmem << 20),
        cost_estimate=pl.CostEstimate(
            flops=COST.get(name, 10**10), bytes_accessed=10**6, transcendentals=0
        ),
        name=name,
    )(*args, *after)


def sds(shape, dtype):
    return jax.ShapeDtypeStruct(shape, dtype)


def kv_kernel(rows_hbm, w_key_hbm, w_value_hbm, out, rows, w_key, w_value, sems):
    copies = [
        pltpu.make_async_copy(src, dst, sems.at[i])
        for i, (src, dst) in enumerate(
            ((rows_hbm, rows), (w_key_hbm, w_key), (w_value_hbm, w_value))
        )
    ]
    for copy in copies:
        copy.start()
    copies[0].wait()
    copies[1].wait()
    out[:, 0:128] = dot(rows[...], w_key[...], 1, 0).astype(BF16)
    copies[2].wait()
    out[:, 128:256] = dot(rows[...], w_value[...], 1, 0).astype(BF16)


def qd_kernel(anchors, cells, grad_a, grad_c, w_query, w_out, out):
    na = anchors.shape[0]
    wq = w_query[...]
    wo = w_out[...]
    for lo, rows, grads in ((0, anchors, grad_a), (na, cells, grad_c)):
        hi = lo + rows.shape[0]
        out[lo:hi, 0:128] = dot(rows[...], wq, 1, 0).astype(BF16) * SCALE
        out[lo:hi, 128:256] = dot(grads[...], wo, 1, 1).astype(BF16)


def stats_block(kv, rhs, before, out):
    total = rhs.shape[0] // 2
    keys = kv[:, 0:128]
    values = kv[:, 128:256]
    for tile in range(0, total, 256):
        for h in range(2):
            lo = h * total + tile
            s = dot(keys, rhs[lo : lo + 256, 0:128], 1, 1)
            peak = jnp.max(s, axis=0, keepdims=True) * LOG2E
            if before is not None:
                old_peak = before[h : h + 1, tile : tile + 256]
                peak = jnp.maximum(peak, old_peak)
            e = jnp.exp2(s * LOG2E - peak)
            dp = dot(values, rhs[lo : lo + 256, 128:256], 1, 1)
            norm = jnp.sum(e, axis=0, keepdims=True)
            mass = jnp.sum(e * dp, axis=0, keepdims=True)
            if before is not None:
                factor = jnp.exp2(old_peak - peak)
                norm += factor * before[2 + h : 3 + h, tile : tile + 256]
                mass += factor * before[4 + h : 5 + h, tile : tile + 256]
            out[h : h + 1, tile : tile + 256] = peak
            out[2 + h : 3 + h, tile : tile + 256] = norm
            out[4 + h : 5 + h, tile : tile + 256] = mass
    out[6:8, :] = jnp.zeros((2, total), F32)


def first_stats_kernel(mine, theirs, kv, stats, rhs):
    half = mine.shape[0]
    lane = lax.broadcasted_iota(jnp.int32, (1, 256), 1)
    for h in range(2):
        keep = lane // HEAD_DIM % 2 == h
        for part, rows in enumerate((mine, theirs)):
            x = rows[...]
            lo = (2 * h + part) * half
            rhs[lo : lo + half, :] = jnp.where(keep, x, jnp.zeros_like(x))
    stats_block(kv, rhs, None, stats)


def next_stats_kernel(kv, rhs, before, stats):
    stats_block(kv, rhs, before, stats)


def merge_kernel(mine, theirs, out):
    half = mine.shape[1] // 2
    for a, b in ((0, half), (half, 0)):
        for h in range(2):
            m1 = mine[h : h + 1, a : a + half]
            m2 = theirs[h : h + 1, b : b + half]
            peak = jnp.maximum(m1, m2)
            f1 = jnp.exp2(m1 - peak)
            f2 = jnp.exp2(m2 - peak)
            norm = f1 * mine[2 + h : 3 + h, a : a + half] + f2 * theirs[2 + h : 3 + h, b : b + half]
            mass = f1 * mine[4 + h : 5 + h, a : a + half] + f2 * theirs[4 + h : 5 + h, b : b + half]
            out[h : h + 1, a : a + half] = peak + jnp.log(norm) * LOG2E
            out[2 + h : 3 + h, a : a + half] = mass / norm
    out[4:8, :] = jnp.zeros((4, 2 * half), F32)


def scores_kernel(has_before, is_last, *refs):
    kv, rhs, stats = refs[:3]
    refs = refs[3:]
    before = None
    if has_before:
        before, refs = refs[0], refs[1:]
    p_t, ds_t, *dq = refs
    total = rhs.shape[0] // 2
    half = total // 2
    n = kv.shape[0]
    keys_t = kv[:, 0:128].T
    step = 128
    for h in range(2):
        lo = h * total
        lse = stats[h : h + 1, :]
        delta = stats[2 + h : 3 + h, :]
        for c in range(0, n, step):
            s = dot(kv[c : c + step, 0:128], rhs[lo : lo + total, 0:128], 1, 1)
            p = jnp.exp2(s * LOG2E - lse)
            dp = dot(kv[c : c + step, 128:256], rhs[lo : lo + total, 128:256], 1, 1)
            ds = p * (dp - delta)
            p_t[c : c + step, lo : lo + total] = p.astype(BF16)
            ds_t[c : c + step, lo : lo + total] = ds.astype(BF16)
        out = slice(h * HEAD_DIM, (h + 1) * HEAD_DIM)
        part = dot(keys_t[out, :], ds_t[:, lo : lo + total], 1, 0)
        if has_before:
            part += before[out, :]
        if is_last:
            dq_mine, dq_theirs = dq
            dq_mine[out, :] = part[:, :half]
            dq_theirs[out, :] = part[:, half:].astype(BF16)
        else:
            dq[0][out, :] = part


def scores(kv, rhs, stats, before, is_last, after=()):
    total = rhs.shape[0] // 2
    args = [kv, rhs, stats] + ([] if before is None else [before])
    outs = [sds((kv.shape[0], 2 * total), BF16)] * 2
    if is_last:
        outs += [sds((128, total // 2), F32), sds((128, total // 2), BF16)]
    else:
        outs += [sds((128, total), F32)]
    return call(
        functools.partial(scores_kernel, before is not None, is_last),
        outs,
        args,
        "scores",
        after=after,
    )


def pair_kernel(p_t, ds_t, rhs, dkv):
    dkv[:, 0:128] = dot(ds_t[...], rhs[:, 0:128], 1, 0).astype(dkv.dtype)
    dkv[:, 128:256] = dot(p_t[...], rhs[:, 128:256], 1, 0).astype(dkv.dtype)


def pair(weights, rhs, dtype, after=()):
    (dkv,) = call(
        pair_kernel, [sds((weights[0].shape[0], 256), dtype)], [*weights, rhs], "pair", after=after
    )
    return dkv


def pair_sum_kernel(own, a, b, c, *outs):
    n = outs[0].shape[0]
    for i, out in enumerate(outs):
        rows = slice(i * n, (i + 1) * n)
        more = (a[rows, :].astype(F32) + b[rows, :].astype(F32)) + c[rows, :].astype(F32)
        out[...] = (own[rows, :] + more).astype(BF16)


def cells_kernel(place, mine, theirs, w_query, dq_anchors, *outs):
    na = mine.shape[1] - outs[0].shape[0]
    dq = ((mine[...] + theirs[...].astype(F32)) * SCALE).astype(BF16)
    dq_anchors[...] = dq[:, :na]
    width = outs[0].shape[1]
    for r, out in enumerate(outs):
        lo = pl.multiple_of(lax.rem(place[0] + r, X) * width, width)
        out[...] = dot(dq[:, na:], w_query[pl.ds(lo, width), :], 0, 1).astype(BF16)


def anchors_kernel(place, dq, a, b, c, d, w_query, w_key, w_value, *outs):
    width = outs[0].shape[1]
    total = (a[...].astype(F32) + b[...].astype(F32)) + (c[...].astype(F32) + d[...].astype(F32))
    total = total.astype(BF16)
    for r, out in enumerate(outs):
        lo = pl.multiple_of(lax.rem(place[0] + r, X) * width, width)
        acc = dot(dq[...], w_query[pl.ds(lo, width), :], 0, 1)
        acc += dot(total[:, 0:128], w_key[pl.ds(lo, width), :], 1, 1)
        acc += dot(total[:, 128:256], w_value[pl.ds(lo, width), :], 1, 1)
        out[...] = acc.astype(BF16)


def split_kernel(place, *refs):
    mine, theirs = refs[-2:]
    first = place[1] == 0
    lo = 0
    for own, a, b, c in (refs[0:4], refs[4:8]):
        rows = slice(lo, lo + own.shape[0])
        lo += own.shape[0]
        low, high = (
            (own[:, cols].astype(F32) + a[:, cols].astype(F32))
            + (b[:, cols].astype(F32) + c[:, cols].astype(F32))
            for cols in (slice(0, 128), slice(128, 256))
        )
        mine[rows, :] = jnp.where(first, low, high)
        theirs[rows, :] = jnp.where(first, high, low).astype(BF16)


def last_sum_kernel(mine, theirs, anchors, cells):
    na = anchors.shape[0]
    total = (mine[...] + theirs[...].astype(F32)).astype(BF16)
    anchors[...] = total[:na, :]
    cells[...] = total[na:, :]


def per_device(anchors, cells, w_query, w_key, w_value, w_out, grad_a, grad_c):
    na, nc, d = anchors.shape[0], cells.shape[0], anchors.shape[1]
    rows = na + nc
    total = 2 * rows
    place = jnp.stack([lax.axis_index("x"), lax.axis_index("y_hi")]).astype(jnp.int32)

    (kv,) = call(
        kv_kernel,
        [sds((na, 256), BF16)],
        [anchors, w_key, w_value],
        "kv",
        scratch=[
            pltpu.VMEM((na, d), BF16),
            pltpu.VMEM((d, 128), BF16),
            pltpu.VMEM((d, 128), BF16),
            pltpu.SemaphoreType.DMA((3,)),
        ],
        hbm=(0, 1, 2),
        vmem=60,
    )
    block = jnp.concatenate([lax.ppermute(kv, TOK, perm) for perm in GATHER], axis=0)
    blocks = [block] + [lax.ppermute(block, TOK, FORTH[j]) for j in range(1, HOPS + 1)]

    (mine,) = call(
        qd_kernel,
        [sds((rows, 256), BF16)],
        [anchors, cells, grad_a, grad_c, w_query, w_out],
        "qd",
        after=[place],
    )
    theirs = lax.ppermute(mine, TOK, SWAP_CORE)

    n = block.shape[0]
    stats, rhs = call(
        first_stats_kernel,
        [sds((8, total), F32), sds((2 * total, 256), BF16)],
        [mine, theirs, blocks[0]],
        "stats0",
    )
    for kv_block in blocks[1:]:
        (stats,) = call(
            next_stats_kernel, [sds((8, total), F32)], [kv_block, rhs, stats], "stats"
        )
    (stats,) = call(
        merge_kernel,
        [sds((8, total), F32)],
        [stats, lax.ppermute(stats, TOK, SWAP_CORE)],
        "merge",
    )

    def send_back(k, after=()):
        dkv = pair(weights[k], rhs, BF16, after)
        sums.append(lax.ppermute(dkv, TOK, BACK[k]))
        return dkv

    sums = []
    weights = {}
    dq = None
    after = ()
    for k in range(HOPS, -1, -1):
        p_t, ds_t, *dq = scores(blocks[k], rhs, stats, dq, k == 0, after)
        weights[k] = (p_t, ds_t)
        after = sums[:1]
        if k > 0:
            dq = dq[0]
        if k > 1:
            after = [send_back(k)]
    dq_mine, dq_theirs = dq
    dkv = send_back(1, after=[dq_mine])
    dq_theirs = lax.ppermute(dq_theirs, TOK, SWAP_CORE)
    width = d // X
    dq_anchors, *cell_parts = call(
        cells_kernel,
        [sds((128, na), BF16)] + [sds((nc, width), BF16)] * X,
        [place, dq_mine, dq_theirs, w_query],
        "cells",
        smem=1,
        after=[dkv, sums[1]],
    )
    cell_sums = [lax.ppermute(cell_parts[r], HEAD, SHIFT_X[r]) for r in (1, 3, 2)]
    dkv = pair(weights[0], rhs, F32, after=[dq_anchors])
    pieces = call(
        pair_sum_kernel, [sds((na, 256), BF16)] * len(RETURN), [dkv, *sums], "pair_sum", after=cell_sums[:2]
    )
    pieces = [lax.ppermute(piece, TOK, perm) for piece, perm in zip(pieces, RETURN)]
    parts = call(
        anchors_kernel,
        [sds((na, width), BF16)] * X,
        [place, dq_anchors, *pieces, w_query, w_key, w_value],
        "anchors",
        smem=1,
    )
    anchor_sums = [lax.ppermute(parts[r], HEAD, SHIFT_X[r]) for r in (2, 1, 3)]
    mine, theirs = call(
        split_kernel,
        [sds((rows, 128), F32), sds((rows, 128), BF16)],
        [place, parts[0], *anchor_sums, cell_parts[0], *cell_sums],
        "split",
        smem=1,
    )
    theirs = lax.ppermute(theirs, HEAD, SWAP_YH)
    return tuple(
        call(
            last_sum_kernel,
            [sds((na, 128), BF16), sds((nc, 128), BF16)],
            [mine, theirs],
            "last_sum",
        )
    )


def solution(mesh):
    parts = jax.sharding.Mesh(mesh.devices.reshape(X, Y_HI, Y_LO, Z, CORES), (*HEAD, *TOK))
    return jax.shard_map(
        per_device,
        mesh=parts,
        in_specs=(
            P(TOK, None),
            P(TOK, None),
            P(None, HEAD),
            P(None, HEAD),
            P(None, HEAD),
            P(HEAD, None),
            P(TOK, None),
            P(TOK, None),
        ),
        out_specs=(P(TOK, HEAD), P(TOK, HEAD)),
        check_vma=False,
    )
```

```python
import functools

import jax
import jax.numpy as jnp
from jax import lax
from jax.experimental import pallas as pl
from jax.experimental.pallas import tpu as pltpu
from jax.sharding import PartitionSpec as P

HEAD_DIM = 64
SCALE = HEAD_DIM ** (-0.5)
LOG2E = 1.4426950408889634
Y_LO, Z, CORES = 2, 8, 2
X, Y_HI = 4, 2
HEAD = ("x", "y_hi")
TOK = ("y_lo", "z", "core")
BF16 = jnp.bfloat16
F32 = jnp.float32
COST = {"scores": 15 * 10**8, "pair": 15 * 10**8, "anchors": 10**8, "split": 10**8}


def tok_perm(move):
    pairs = []
    for yl in range(Y_LO):
        for z in range(Z):
            for core in range(CORES):
                yl2, z2, core2 = move(yl, z, core)
                pairs.append(
                    ((yl * Z + z) * CORES + core, (yl2 * Z + z2 % Z) * CORES + core2)
                )
    return pairs


def head_perm(move):
    pairs = []
    for x in range(X):
        for yh in range(Y_HI):
            x2, yh2 = move(x, yh)
            pairs.append((x * Y_HI + yh, (x2 % X) * Y_HI + yh2))
    return pairs


SWAP_CORE = tok_perm(lambda yl, z, c: (yl, z, 1 - c))
GATHER = [
    tok_perm(lambda yl, z, c, f=f: (f(yl), z, 0) if c == 0 else (f(yl), z - 1, 1))
    for f in (lambda yl: yl, lambda yl: 1 - yl)
] + [
    tok_perm(lambda yl, z, c, f=f: (f(yl), z - 1, 1) if c == 0 else (f(yl), z, 0))
    for f in (lambda yl: yl, lambda yl: 1 - yl)
]
RETURN = [[(b, a) for a, b in perm] for perm in GATHER]
HOPS = 3
FORTH = [
    tok_perm(lambda yl, z, c, j=j: (yl, z + j, 0) if c == 0 else (yl, z - j, 1))
    for j in range(HOPS + 1)
]
BACK = [[(b, a) for a, b in perm] for perm in FORTH]
SHIFT_X = [head_perm(lambda x, yh, r=r: (x + r, yh)) for r in range(X)]
SWAP_YH = head_perm(lambda x, yh: (x, 1 - yh))


def dot(a, b, ca, cb):
    return lax.dot_general(a, b, (((ca,), (cb,)), ((), ())), preferred_element_type=F32)


def call(body, outs, args, name, scratch=(), smem=0, hbm=(), after=(), vmem=20):
    def spec(i):
        if i < smem:
            return pl.BlockSpec(memory_space=pltpu.SMEM)
        if i >= len(args):
            return pl.BlockSpec(memory_space=pl.ANY)
        return pl.BlockSpec(memory_space=pltpu.HBM if i in hbm else pltpu.VMEM)

    def kernel(*refs):
        body(*refs[: len(args)], *refs[len(args) + len(after) :])

    return pl.pallas_call(
        kernel,
        out_shape=tuple(outs),
        in_specs=[spec(i) for i in range(len(args) + len(after))],
        out_specs=tuple(pl.BlockSpec(memory_space=pltpu.VMEM) for _ in outs),
        scratch_shapes=list(scratch),
        compiler_params=pltpu.CompilerParams(vmem_limit_bytes=vmem << 20),
        cost_estimate=pl.CostEstimate(
            flops=COST.get(name, 10**10), bytes_accessed=10**6, transcendentals=0
        ),
        name=name,
    )(*args, *after)


def sds(shape, dtype):
    return jax.ShapeDtypeStruct(shape, dtype)


def kv_kernel(rows_hbm, w_key_hbm, w_value_hbm, out, rows, w_key, w_value, sems):
    copies = [
        pltpu.make_async_copy(src, dst, sems.at[i])
        for i, (src, dst) in enumerate(
            ((rows_hbm, rows), (w_key_hbm, w_key), (w_value_hbm, w_value))
        )
    ]
    for copy in copies:
        copy.start()
    copies[0].wait()
    copies[1].wait()
    out[:, 0:128] = dot(rows[...], w_key[...], 1, 0).astype(BF16)
    copies[2].wait()
    out[:, 128:256] = dot(rows[...], w_value[...], 1, 0).astype(BF16)


def qd_kernel(anchors, cells, grad_a, grad_c, w_query, w_out, out):
    na = anchors.shape[0]
    wq = w_query[...]
    wo = w_out[...]
    for lo, rows, grads in ((0, anchors, grad_a), (na, cells, grad_c)):
        hi = lo + rows.shape[0]
        out[lo:hi, 0:128] = dot(rows[...], wq, 1, 0).astype(BF16) * SCALE
        out[lo:hi, 128:256] = dot(grads[...], wo, 1, 1).astype(BF16)


def stats_block(kv, rhs, before, out):
    total = rhs.shape[0] // 2
    keys = kv[:, 0:128]
    values = kv[:, 128:256]
    for tile in range(0, total, 256):
        for h in range(2):
            lo = h * total + tile
            s = dot(keys, rhs[lo : lo + 256, 0:128], 1, 1)
            peak = jnp.max(s, axis=0, keepdims=True) * LOG2E
            if before is not None:
                old_peak = before[h : h + 1, tile : tile + 256]
                peak = jnp.maximum(peak, old_peak)
            e = jnp.exp2(s * LOG2E - peak)
            dp = dot(values, rhs[lo : lo + 256, 128:256], 1, 1)
            norm = jnp.sum(e, axis=0, keepdims=True)
            mass = jnp.sum(e * dp, axis=0, keepdims=True)
            if before is not None:
                factor = jnp.exp2(old_peak - peak)
                norm += factor * before[2 + h : 3 + h, tile : tile + 256]
                mass += factor * before[4 + h : 5 + h, tile : tile + 256]
            out[h : h + 1, tile : tile + 256] = peak
            out[2 + h : 3 + h, tile : tile + 256] = norm
            out[4 + h : 5 + h, tile : tile + 256] = mass
    out[6:8, :] = jnp.zeros((2, total), F32)


def first_stats_kernel(mine, theirs, kv, stats, rhs):
    half = mine.shape[0]
    lane = lax.broadcasted_iota(jnp.int32, (1, 256), 1)
    for h in range(2):
        keep = lane // HEAD_DIM % 2 == h
        for part, rows in enumerate((mine, theirs)):
            x = rows[...]
            lo = (2 * h + part) * half
            rhs[lo : lo + half, :] = jnp.where(keep, x, jnp.zeros_like(x))
    stats_block(kv, rhs, None, stats)


def next_stats_kernel(kv, rhs, before, stats):
    stats_block(kv, rhs, before, stats)


def merge_kernel(mine, theirs, out):
    half = mine.shape[1] // 2
    for a, b in ((0, half), (half, 0)):
        for h in range(2):
            m1 = mine[h : h + 1, a : a + half]
            m2 = theirs[h : h + 1, b : b + half]
            peak = jnp.maximum(m1, m2)
            f1 = jnp.exp2(m1 - peak)
            f2 = jnp.exp2(m2 - peak)
            norm = f1 * mine[2 + h : 3 + h, a : a + half] + f2 * theirs[2 + h : 3 + h, b : b + half]
            mass = f1 * mine[4 + h : 5 + h, a : a + half] + f2 * theirs[4 + h : 5 + h, b : b + half]
            out[h : h + 1, a : a + half] = peak + jnp.log(norm) * LOG2E
            out[2 + h : 3 + h, a : a + half] = mass / norm
    out[4:8, :] = jnp.zeros((4, 2 * half), F32)


def scores_kernel(has_before, is_last, *refs):
    kv, rhs, stats = refs[:3]
    refs = refs[3:]
    before = None
    if has_before:
        before, refs = refs[0], refs[1:]
    p_t, ds_t, *dq = refs
    total = rhs.shape[0] // 2
    half = total // 2
    n = kv.shape[0]
    keys_t = kv[:, 0:128].T
    step = 128
    for h in range(2):
        lo = h * total
        lse = stats[h : h + 1, :]
        delta = stats[2 + h : 3 + h, :]
        for c in range(0, n, step):
            s = dot(kv[c : c + step, 0:128], rhs[lo : lo + total, 0:128], 1, 1)
            p = jnp.exp2(s * LOG2E - lse)
            dp = dot(kv[c : c + step, 128:256], rhs[lo : lo + total, 128:256], 1, 1)
            ds = p * (dp - delta)
            p_t[c : c + step, lo : lo + total] = p.astype(BF16)
            ds_t[c : c + step, lo : lo + total] = ds.astype(BF16)
        out = slice(h * HEAD_DIM, (h + 1) * HEAD_DIM)
        part = dot(keys_t[out, :], ds_t[:, lo : lo + total], 1, 0)
        if has_before:
            part += before[out, :]
        if is_last:
            dq_mine, dq_theirs = dq
            dq_mine[out, :] = part[:, :half]
            dq_theirs[out, :] = part[:, half:].astype(BF16)
        else:
            dq[0][out, :] = part


def scores(kv, rhs, stats, before, is_last, after=()):
    total = rhs.shape[0] // 2
    args = [kv, rhs, stats] + ([] if before is None else [before])
    outs = [sds((kv.shape[0], 2 * total), BF16)] * 2
    if is_last:
        outs += [sds((128, total // 2), F32), sds((128, total // 2), BF16)]
    else:
        outs += [sds((128, total), F32)]
    return call(
        functools.partial(scores_kernel, before is not None, is_last),
        outs,
        args,
        "scores",
        after=after,
    )


def pair_kernel(p_t, ds_t, rhs, dkv):
    dkv[:, 0:128] = dot(ds_t[...], rhs[:, 0:128], 1, 0).astype(dkv.dtype)
    dkv[:, 128:256] = dot(p_t[...], rhs[:, 128:256], 1, 0).astype(dkv.dtype)


def pair(weights, rhs, dtype, after=()):
    (dkv,) = call(
        pair_kernel, [sds((weights[0].shape[0], 256), dtype)], [*weights, rhs], "pair", after=after
    )
    return dkv


def pair_sum_kernel(own, a, b, c, *outs):
    n = outs[0].shape[0]
    for i, out in enumerate(outs):
        rows = slice(i * n, (i + 1) * n)
        more = (a[rows, :].astype(F32) + b[rows, :].astype(F32)) + c[rows, :].astype(F32)
        out[...] = (own[rows, :] + more).astype(BF16)


def weights_kernel(place, w_query, w_key, w_value, *outs):
    width = outs[0].shape[0]
    for r, out in enumerate(outs):
        lo = pl.multiple_of(lax.rem(place[0] + r, X) * width, width)
        for i, w in enumerate((w_query, w_key, w_value)):
            out[:, i * 128 : (i + 1) * 128] = w[pl.ds(lo, width), :]


def dq_sum_kernel(mine, theirs, dq):
    dq[...] = ((mine[...] + theirs[...].astype(F32)) * SCALE).astype(BF16)


def piece_sum_kernel(a, b, c, d, out):
    total = (a[...].astype(F32) + b[...].astype(F32)) + (c[...].astype(F32) + d[...].astype(F32))
    out[...] = total.astype(BF16)


def stack_weights(place, weights, cols, stacked, base):
    for r, w in enumerate(weights):
        for side in range(2):
            y_hi = place[1] if side == 0 else 1 - place[1]
            rows = pl.ds(pl.multiple_of(y_hi * 128, 128), 128)
            width = cols.stop - cols.start
            lo = base + r * width
            stacked[side * 128 : (side + 1) * 128, lo : lo + width] = w[rows, cols]


def cells_kernel(place, *refs):
    dqs, weights, (mine, theirs, dq, stacked) = refs[:X], refs[X : 2 * X], refs[2 * X :]
    na = dqs[0].shape[1] - mine.shape[0]
    for r, part in enumerate(dqs):
        dq[r * 128 : (r + 1) * 128, :] = part[:, na:]
    stack_weights(place, weights, slice(0, 128), stacked, 0)
    out = dot(dq[...], stacked[...], 0, 1)
    mine[...] = out[:, 0:128]
    theirs[...] = out[:, 128:256].astype(BF16)


def anchors_kernel(place, *refs):
    dqs, dkvs, weights = (refs[i * X : (i + 1) * X] for i in range(3))
    mine, theirs, rows, stacked = refs[3 * X :]
    na = mine.shape[0]
    for r, (dq, dkv) in enumerate(zip(dqs, dkvs)):
        rows[:, r * 128 : (r + 1) * 128] = dq[:, :na].T
        lo = X * 128 + r * 256
        rows[:, lo : lo + 256] = dkv[...]
    stack_weights(place, weights, slice(0, 128), stacked, 0)
    stack_weights(place, weights, slice(128, 384), stacked, X * 128)
    out = dot(rows[...], stacked[...], 1, 1)
    mine[...] = out[:, 0:128]
    theirs[...] = out[:, 128:256].astype(BF16)


def last_sum_kernel(mine, theirs, out):
    out[...] = (mine[...] + theirs[...].astype(F32)).astype(BF16)


def over_x(array):
    return [array] + [lax.ppermute(array, HEAD, SHIFT_X[r]) for r in range(1, X)]


def over_y(mine, theirs):
    (out,) = call(
        last_sum_kernel,
        [sds(mine.shape, BF16)],
        [mine, lax.ppermute(theirs, HEAD, SWAP_YH)],
        "last_sum",
    )
    return out


def per_device(anchors, cells, w_query, w_key, w_value, w_out, grad_a, grad_c):
    na, nc, d = anchors.shape[0], cells.shape[0], anchors.shape[1]
    rows = na + nc
    total = 2 * rows
    place = jnp.stack([lax.axis_index("x"), lax.axis_index("y_hi")]).astype(jnp.int32)

    (kv,) = call(
        kv_kernel,
        [sds((na, 256), BF16)],
        [anchors, w_key, w_value],
        "kv",
        scratch=[
            pltpu.VMEM((na, d), BF16),
            pltpu.VMEM((d, 128), BF16),
            pltpu.VMEM((d, 128), BF16),
            pltpu.SemaphoreType.DMA((3,)),
        ],
        hbm=(0, 1, 2),
        vmem=60,
    )
    block = jnp.concatenate([lax.ppermute(kv, TOK, perm) for perm in GATHER], axis=0)
    blocks = [block] + [lax.ppermute(block, TOK, FORTH[j]) for j in range(1, HOPS + 1)]

    (mine,) = call(
        qd_kernel,
        [sds((rows, 256), BF16)],
        [anchors, cells, grad_a, grad_c, w_query, w_out],
        "qd",
        after=[place],
    )
    theirs = lax.ppermute(mine, TOK, SWAP_CORE)

    n = block.shape[0]
    stats, rhs = call(
        first_stats_kernel,
        [sds((8, total), F32), sds((2 * total, 256), BF16)],
        [mine, theirs, blocks[0]],
        "stats0",
    )
    x_weights = call(
        weights_kernel,
        [sds((d // X, 3 * 128), BF16)] * X,
        [place, w_query, w_key, w_value],
        "weights",
        smem=1,
        after=[stats],
    )
    x_weights = x_weights[:1] + tuple(
        lax.ppermute(x_weights[r], HEAD, SHIFT_X[r]) for r in range(1, X)
    )
    for j in range(1, HOPS + 1):
        (stats,) = call(
            next_stats_kernel,
            [sds((8, total), F32)],
            [blocks[j], rhs, stats],
            "stats",
            after=x_weights[1:] if j == HOPS else (),
        )
    (stats,) = call(
        merge_kernel,
        [sds((8, total), F32)],
        [stats, lax.ppermute(stats, TOK, SWAP_CORE)],
        "merge",
    )

    def send_back(k, after=()):
        dkv = pair(weights[k], rhs, BF16, after)
        sums.append(lax.ppermute(dkv, TOK, BACK[k]))
        return dkv

    sums = []
    weights = {}
    dq = None
    after = ()
    for k in range(HOPS, -1, -1):
        p_t, ds_t, *dq = scores(blocks[k], rhs, stats, dq, k == 0, after)
        weights[k] = (p_t, ds_t)
        after = sums[:1]
        if k > 0:
            dq = dq[0]
        if k > 1:
            after = [send_back(k)]
    dq_mine, dq_theirs = dq
    dkv = send_back(1, after=[dq_mine])
    (dq,) = call(
        dq_sum_kernel,
        [sds((128, rows), BF16)],
        [dq_mine, lax.ppermute(dq_theirs, TOK, SWAP_CORE)],
        "dq_sum",
        after=[dkv, sums[1]],
    )
    dqs = over_x(dq)
    dkv = pair(weights[0], rhs, F32, after=[dq])
    pieces = call(
        pair_sum_kernel, [sds((na, 256), BF16)] * len(RETURN), [dkv, *sums], "pair_sum"
    )
    pieces = [lax.ppermute(piece, TOK, perm) for piece, perm in zip(pieces, RETURN)]
    cell_halves = call(
        cells_kernel,
        [sds((nc, 128), F32), sds((nc, 128), BF16)],
        [place, *dqs, *x_weights],
        "cells",
        scratch=[pltpu.VMEM((X * 128, nc), BF16), pltpu.VMEM((256, X * 128), BF16)],
        smem=1,
    )
    (dkv,) = call(piece_sum_kernel, [sds((na, 256), BF16)], pieces, "piece_sum")
    anchor_halves = call(
        anchors_kernel,
        [sds((na, 128), F32), sds((na, 128), BF16)],
        [place, *dqs, *over_x(dkv), *x_weights],
        "anchors",
        scratch=[pltpu.VMEM((na, X * 384), BF16), pltpu.VMEM((256, X * 384), BF16)],
        smem=1,
        after=cell_halves[:1],
    )
    return over_y(*anchor_halves), over_y(*cell_halves)


def solution(mesh):
    parts = jax.sharding.Mesh(mesh.devices.reshape(X, Y_HI, Y_LO, Z, CORES), (*HEAD, *TOK))
    return jax.shard_map(
        per_device,
        mesh=parts,
        in_specs=(
            P(TOK, None),
            P(TOK, None),
            P(None, HEAD),
            P(None, HEAD),
            P(None, HEAD),
            P(HEAD, None),
            P(TOK, None),
            P(TOK, None),
        ),
        out_specs=(P(TOK, HEAD), P(TOK, HEAD)),
        check_vma=False,
    )
```

```python
import functools

import jax
import jax.numpy as jnp
from jax import lax
from jax.experimental import pallas as pl
from jax.experimental.pallas import tpu as pltpu
from jax.sharding import PartitionSpec as P

HEAD_DIM = 64
SCALE = HEAD_DIM ** (-0.5)
LOG2E = 1.4426950408889634
Y_LO, Z, CORES = 2, 8, 2
X, Y_HI = 4, 2
HEAD = ("x", "y_hi")
TOK = ("y_lo", "z", "core")
STEP = 128
BF16 = jnp.bfloat16
F32 = jnp.float32
COST = {"scores": 15 * 10**8, "pair": 15 * 10**8, "anchors": 10**8, "split": 10**8}


def tok_perm(move):
    pairs = []
    for yl in range(Y_LO):
        for z in range(Z):
            for core in range(CORES):
                yl2, z2, core2 = move(yl, z, core)
                pairs.append(
                    ((yl * Z + z) * CORES + core, (yl2 * Z + z2 % Z) * CORES + core2)
                )
    return pairs


def head_perm(move):
    pairs = []
    for x in range(X):
        for yh in range(Y_HI):
            x2, yh2 = move(x, yh)
            pairs.append((x * Y_HI + yh, (x2 % X) * Y_HI + yh2))
    return pairs


SWAP_CORE = tok_perm(lambda yl, z, c: (yl, z, 1 - c))
SWAP_Y = tok_perm(lambda yl, z, c: (1 - yl, z, c))
SWAP_BOTH = tok_perm(lambda yl, z, c: (1 - yl, z, 1 - c))
GATHER = [
    tok_perm(lambda yl, z, c: (yl, z, 0) if c == 0 else (yl, z - 1, 1)),
    tok_perm(lambda yl, z, c: (yl, z - 1, 1) if c == 0 else (yl, z, 0)),
]
RETURN = [[(b, a) for a, b in perm] for perm in GATHER]
HOPS = 3
FORTH = [
    tok_perm(lambda yl, z, c, j=j: (yl, z + j, 0) if c == 0 else (yl, z - j, 1))
    for j in range(HOPS + 1)
]
BACK = [[(b, a) for a, b in perm] for perm in FORTH]
SHIFT_X = [head_perm(lambda x, yh, r=r: (x + r, yh)) for r in range(X)]
SWAP_YH = head_perm(lambda x, yh: (x, 1 - yh))


def dot(a, b, ca, cb):
    return lax.dot_general(a, b, (((ca,), (cb,)), ((), ())), preferred_element_type=F32)


def call(body, outs, args, name, scratch=(), smem=0, hbm=(), after=(), vmem=20):
    def spec(i):
        if i < smem:
            return pl.BlockSpec(memory_space=pltpu.SMEM)
        if i >= len(args):
            return pl.BlockSpec(memory_space=pl.ANY)
        return pl.BlockSpec(memory_space=pltpu.HBM if i in hbm else pltpu.VMEM)

    def kernel(*refs):
        body(*refs[: len(args)], *refs[len(args) + len(after) :])

    return pl.pallas_call(
        kernel,
        out_shape=tuple(outs),
        in_specs=[spec(i) for i in range(len(args) + len(after))],
        out_specs=tuple(pl.BlockSpec(memory_space=pltpu.VMEM) for _ in outs),
        scratch_shapes=list(scratch),
        compiler_params=pltpu.CompilerParams(vmem_limit_bytes=vmem << 20),
        cost_estimate=pl.CostEstimate(
            flops=COST.get(name, 10**10), bytes_accessed=10**6, transcendentals=0
        ),
        name=name,
    )(*args, *after)


def sds(shape, dtype):
    return jax.ShapeDtypeStruct(shape, dtype)


def kv_kernel(rows_hbm, w_key_hbm, w_value_hbm, out, rows, w_key, w_value, sems):
    copies = [
        pltpu.make_async_copy(src, dst, sems.at[i])
        for i, (src, dst) in enumerate(
            ((rows_hbm, rows), (w_key_hbm, w_key), (w_value_hbm, w_value))
        )
    ]
    for copy in copies:
        copy.start()
    copies[0].wait()
    copies[1].wait()
    out[:, 0:128] = dot(rows[...], w_key[...], 1, 0).astype(BF16)
    copies[2].wait()
    out[:, 128:256] = dot(rows[...], w_value[...], 1, 0).astype(BF16)


def qd_kernel(anchors, cells, grad_a, grad_c, w_query, w_out, out):
    na = anchors.shape[0]
    wq = w_query[...]
    wo = w_out[...]
    for lo, rows, grads in ((0, anchors, grad_a), (na, cells, grad_c)):
        hi = lo + rows.shape[0]
        out[lo:hi, 0:128] = dot(rows[...], wq, 1, 0).astype(BF16) * SCALE
        out[lo:hi, 128:256] = dot(grads[...], wo, 1, 1).astype(BF16)


def stats_block(kv, rhs, before, out):
    total = rhs.shape[0] // 2
    keys = kv[:, 0:128]
    values = kv[:, 128:256]
    for tile in range(0, total, 256):
        cols = slice(tile, tile + 256)
        for h in range(2):
            lo = h * total + tile
            s = dot(keys, rhs[lo : lo + 256, 0:128], 1, 1)
            peak = jnp.max(s, axis=0, keepdims=True) * LOG2E
            if before is not None:
                old_peak = before[h : h + 1, cols]
                peak = jnp.maximum(peak, old_peak)
            e = jnp.exp2(s * LOG2E - peak)
            dp = dot(values, rhs[lo : lo + 256, 128:256], 1, 1)
            norm = jnp.sum(e, axis=0, keepdims=True)
            mass = jnp.sum(e * dp, axis=0, keepdims=True)
            if before is not None:
                factor = jnp.exp2(old_peak - peak)
                norm += factor * before[2 + h : 3 + h, cols]
                mass += factor * before[4 + h : 5 + h, cols]
            out[h : h + 1, cols] = peak
            out[2 + h : 3 + h, cols] = norm
            out[4 + h : 5 + h, cols] = mass
    out[6:8, :] = jnp.zeros((2, total), F32)


def first_stats_kernel(count, *refs):
    first, second = refs[:2]
    blocks = refs[2 : 2 + count]
    stats, rhs = refs[2 + count :]
    half = first.shape[0]
    lane = lax.broadcasted_iota(jnp.int32, (1, 256), 1)
    for h in range(2):
        keep = lane // HEAD_DIM % 2 == h
        for part, rows in enumerate((first, second)):
            x = rows[...]
            lo = (2 * h + part) * half
            rhs[lo : lo + half, :] = jnp.where(keep, x, jnp.zeros_like(x))
    for i, kv in enumerate(blocks):
        stats_block(kv, rhs, stats if i else None, stats)


def first_stats(first, second, blocks):
    total = 2 * first.shape[0]
    return call(
        functools.partial(first_stats_kernel, len(blocks)),
        [sds((8, total), F32), sds((2 * total, 256), BF16)],
        [first, second, *blocks],
        "first_stats",
    )


def next_stats_kernel(kv, rhs, before, stats):
    stats_block(kv, rhs, before, stats)


def both_stats_kernel(kv, rhs_a, rhs_b, before_a, before_b, stats):
    stats_block(kv, rhs_a, before_a, stats.at[0:8])
    stats_block(kv, rhs_b, before_b, stats.at[8:16])


def merged(mine, theirs, a, b, i, j):
    for h in range(2):
        m1 = mine[i + h : i + h + 1, a]
        m2 = theirs[j + h : j + h + 1, b]
        peak = jnp.maximum(m1, m2)
        f1 = jnp.exp2(m1 - peak)
        f2 = jnp.exp2(m2 - peak)
        norm = f1 * mine[i + 2 + h : i + 3 + h, a] + f2 * theirs[j + 2 + h : j + 3 + h, b]
        mass = f1 * mine[i + 4 + h : i + 5 + h, a] + f2 * theirs[j + 4 + h : j + 5 + h, b]
        yield h, peak, norm, mass


def merge_cores_kernel(mine, theirs, out):
    half = mine.shape[1] // 2
    low, high = slice(0, half), slice(half, 2 * half)
    for i in (0, 8):
        for a, b in ((low, high), (high, low)):
            for h, peak, norm, mass in merged(mine, theirs, a, b, i, i):
                out[i + h : i + h + 1, a] = peak
                out[i + 2 + h : i + 3 + h, a] = norm
                out[i + 4 + h : i + 5 + h, a] = mass
        out[i + 6 : i + 8, :] = jnp.zeros((2, 2 * half), F32)


def merge_y_kernel(mine, theirs, out):
    whole = slice(0, mine.shape[1])
    for i, j in ((0, 8), (8, 0)):
        for h, peak, norm, mass in merged(mine, theirs, whole, whole, i, j):
            out[i + h : i + h + 1, whole] = peak + jnp.log(norm) * LOG2E
            out[i + 2 + h : i + 3 + h, whole] = mass / norm
        out[i + 4 : i + 8, :] = jnp.zeros((4, mine.shape[1]), F32)


def scores_kernel(has_before, is_last, *refs):
    kv, *rhs = refs[:3]
    stats = refs[3]
    refs = refs[4:]
    before = None
    if has_before:
        before, refs = refs[0], refs[1:]
    p_t, ds_t, *dq = refs
    total = rhs[0].shape[0] // 2
    half = total // 2
    n = kv.shape[0]
    keys_t = kv[:, 0:128].T
    step = STEP
    for g in range(2):
        for h in range(2):
            here = slice(h * total, (h + 1) * total)
            there = slice((2 * g + h) * total, (2 * g + h + 1) * total)
            lse = stats[8 * g + h : 8 * g + h + 1, :]
            delta = stats[8 * g + 2 + h : 8 * g + 3 + h, :]
            for c in range(0, n, step):
                s = dot(kv[c : c + step, 0:128], rhs[g][here, 0:128], 1, 1)
                p = jnp.exp2(s * LOG2E - lse)
                dp = dot(kv[c : c + step, 128:256], rhs[g][here, 128:256], 1, 1)
                ds = p * (dp - delta)
                p_t[c : c + step, there] = p.astype(BF16)
                ds_t[c : c + step, there] = ds.astype(BF16)
            out = slice(h * HEAD_DIM, (h + 1) * HEAD_DIM)
            cols = slice(g * total, (g + 1) * total)
            part = dot(keys_t[out, :], ds_t[:, there], 1, 0)
            if has_before:
                part += before[out, cols]
            if is_last:
                dq[2 * g][out, :] = part[:, :half].astype(dq[2 * g].dtype)
                dq[2 * g + 1][out, :] = part[:, half:].astype(BF16)
            else:
                dq[0][out, cols] = part


def scores(kv, rhs, stats, before, is_last, after=()):
    total = rhs[0].shape[0] // 2
    args = [kv, *rhs, stats] + ([] if before is None else [before])
    outs = [sds((kv.shape[0], 4 * total), BF16)] * 2
    if is_last:
        outs += [sds((128, total // 2), F32)] + [sds((128, total // 2), BF16)] * 3
    else:
        outs += [sds((128, 2 * total), F32)]
    return call(
        functools.partial(scores_kernel, before is not None, is_last),
        outs,
        args,
        "scores",
        after=after,
    )


def pair_kernel(first, p_t, ds_t, rhs_a, rhs_b, *outs):
    n = rhs_a.shape[0]
    rows = slice(first, first + sum(out.shape[0] for out in outs))
    for cols, weights in ((slice(0, 128), ds_t), (slice(128, 256), p_t)):
        total = dot(weights[rows, :n], rhs_a[:, cols], 1, 0)
        total += dot(weights[rows, n:], rhs_b[:, cols], 1, 0)
        lo = 0
        for out in outs:
            out[:, cols] = total[lo : lo + out.shape[0]].astype(out.dtype)
            lo += out.shape[0]


def pair(weights, rhs, first, outs, after=()):
    return call(
        functools.partial(pair_kernel, first), outs, [*weights, *rhs], "pair", after=after
    )


def pair_sum_kernel(own, a, b, c, *outs):
    n = outs[0].shape[0]
    for i, out in enumerate(outs):
        rows = slice(i * n, (i + 1) * n)
        more = (a[rows, :].astype(F32) + b[rows, :].astype(F32)) + c[rows, :].astype(F32)
        out[...] = (own[rows, :] + more).astype(BF16)


def weights_kernel(place, w_query, w_key, w_value, *outs):
    width = outs[0].shape[0]
    for r, out in enumerate(outs):
        lo = pl.multiple_of(lax.rem(place[0] + r, X) * width, width)
        for i, w in enumerate((w_query, w_key, w_value)):
            out[:, i * 128 : (i + 1) * 128] = w[pl.ds(lo, width), :]


def dq_sum_kernel(mine, a, b, c, dq):
    more = (a[...].astype(F32) + b[...].astype(F32)) + c[...].astype(F32)
    dq[...] = ((mine[...] + more) * SCALE).astype(BF16)


def piece_sum_kernel(a, b, out):
    out[...] = (a[...].astype(F32) + b[...].astype(F32)).astype(BF16)


def stack_weights(place, weights, cols, stacked, base):
    for r, w in enumerate(weights):
        for side in range(2):
            y_hi = place[1] if side == 0 else 1 - place[1]
            rows = pl.ds(pl.multiple_of(y_hi * 128, 128), 128)
            width = cols.stop - cols.start
            lo = base + r * width
            stacked[side * 128 : (side + 1) * 128, lo : lo + width] = w[rows, cols]


def cells_kernel(place, *refs):
    dqs, weights, (mine, theirs, dq, stacked) = refs[:X], refs[X : 2 * X], refs[2 * X :]
    na = dqs[0].shape[1] - mine.shape[0]
    for r, part in enumerate(dqs):
        dq[r * 128 : (r + 1) * 128, :] = part[:, na:]
    stack_weights(place, weights, slice(0, 128), stacked, 0)
    out = dot(dq[...], stacked[...], 0, 1)
    mine[...] = out[:, 0:128]
    theirs[...] = out[:, 128:256].astype(BF16)


def anchors_kernel(place, *refs):
    dqs, dkvs, weights = (refs[i * X : (i + 1) * X] for i in range(3))
    mine, theirs, rows, stacked = refs[3 * X :]
    na = mine.shape[0]
    for r, (dq, dkv) in enumerate(zip(dqs, dkvs)):
        rows[:, r * 128 : (r + 1) * 128] = dq[:, :na].T
        lo = X * 128 + r * 256
        rows[:, lo : lo + 256] = dkv[...]
    stack_weights(place, weights, slice(0, 128), stacked, 0)
    stack_weights(place, weights, slice(128, 384), stacked, X * 128)
    out = dot(rows[...], stacked[...], 1, 1)
    mine[...] = out[:, 0:128]
    theirs[...] = out[:, 128:256].astype(BF16)


def last_sum_kernel(mine, theirs, out):
    out[...] = (mine[...] + theirs[...].astype(F32)).astype(BF16)


def over_x(array):
    return [array] + [lax.ppermute(array, HEAD, SHIFT_X[r]) for r in range(1, X)]


def over_y(mine, theirs):
    (out,) = call(
        last_sum_kernel,
        [sds(mine.shape, BF16)],
        [mine, lax.ppermute(theirs, HEAD, SWAP_YH)],
        "last_sum",
    )
    return out


def per_device(anchors, cells, w_query, w_key, w_value, w_out, grad_a, grad_c):
    na, nc, d = anchors.shape[0], cells.shape[0], anchors.shape[1]
    rows = na + nc
    total = 2 * rows
    place = jnp.stack([lax.axis_index("x"), lax.axis_index("y_hi")]).astype(jnp.int32)

    (kv,) = call(
        kv_kernel,
        [sds((na, 256), BF16)],
        [anchors, w_key, w_value],
        "kv",
        scratch=[
            pltpu.VMEM((na, d), BF16),
            pltpu.VMEM((d, 128), BF16),
            pltpu.VMEM((d, 128), BF16),
            pltpu.SemaphoreType.DMA((3,)),
        ],
        hbm=(0, 1, 2),
        vmem=60,
    )
    block = jnp.concatenate([lax.ppermute(kv, TOK, perm) for perm in GATHER], axis=0)
    blocks = [block] + [lax.ppermute(block, TOK, FORTH[j]) for j in range(1, HOPS + 1)]

    (mine,) = call(
        qd_kernel,
        [sds((rows, 256), BF16)],
        [anchors, cells, grad_a, grad_c, w_query, w_out],
        "qd",
        after=[place, kv],
    )
    core_rows = lax.ppermute(mine, TOK, SWAP_CORE)
    y_rows = lax.ppermute(mine, TOK, SWAP_Y)
    both_rows = lax.ppermute(y_rows, TOK, SWAP_CORE)

    stats_a, rhs_a = first_stats(mine, core_rows, blocks[:1])
    x_weights = call(
        weights_kernel,
        [sds((d // X, 3 * 128), BF16)] * X,
        [place, w_query, w_key, w_value],
        "weights",
        smem=1,
        after=[stats_a],
    )
    x_weights = x_weights[:1] + tuple(
        lax.ppermute(x_weights[r], HEAD, SHIFT_X[r]) for r in range(1, X)
    )
    for j in range(1, HOPS):
        (stats_a,) = call(
            next_stats_kernel, [sds((8, total), F32)], [blocks[j], rhs_a, stats_a], "stats"
        )
    stats_b, rhs_b = first_stats(y_rows, both_rows, blocks[:HOPS])
    (stats,) = call(
        both_stats_kernel,
        [sds((16, total), F32)],
        [blocks[HOPS], rhs_a, rhs_b, stats_a, stats_b],
        "both_stats",
        after=x_weights[1:],
    )
    for merge_kernel, perm in ((merge_cores_kernel, SWAP_CORE), (merge_y_kernel, SWAP_Y)):
        (stats,) = call(
            merge_kernel,
            [sds((16, total), F32)],
            [stats, lax.ppermute(stats, TOK, perm)],
            "merge",
        )
    rhs = (rhs_a, rhs_b)
    n = block.shape[0]

    far = jnp.concatenate([blocks[3], blocks[2]], axis=0)
    near = jnp.concatenate([blocks[1], blocks[0]], axis=0)
    *weights, dq = scores(far, rhs, stats, None, False)
    dkv_3, dkv_2 = pair(weights, rhs, 0, [sds((n, 256), BF16)] * 2)
    sums = [lax.ppermute(dkv_3, TOK, BACK[3]), lax.ppermute(dkv_2, TOK, BACK[2])]
    *weights, dq_mine, dq_core, dq_y, dq_both = scores(
        near, rhs, stats, dq, True, after=[dkv_3]
    )
    dq_others = [
        lax.ppermute(part, TOK, perm)
        for part, perm in ((dq_y, SWAP_Y), (dq_both, SWAP_BOTH), (dq_core, SWAP_CORE))
    ]
    (dkv_1,) = pair(weights, rhs, 0, [sds((n, 256), BF16)], after=list(sums))
    sums.append(lax.ppermute(dkv_1, TOK, BACK[1]))
    (dkv,) = pair(weights, rhs, n, [sds((n, 256), F32)], after=[dkv_1])
    (dq,) = call(dq_sum_kernel, [sds((128, rows), BF16)], [dq_mine, *dq_others], "dq_sum")
    dqs = over_x(dq)
    pieces = call(
        pair_sum_kernel, [sds((na, 256), BF16)] * len(RETURN), [dkv, *sums], "pair_sum"
    )
    pieces = [lax.ppermute(piece, TOK, perm) for piece, perm in zip(pieces, RETURN)]
    cell_halves = call(
        cells_kernel,
        [sds((nc, 128), F32), sds((nc, 128), BF16)],
        [place, *dqs, *x_weights],
        "cells",
        scratch=[pltpu.VMEM((X * 128, nc), BF16), pltpu.VMEM((256, X * 128), BF16)],
        smem=1,
    )
    (dkv,) = call(piece_sum_kernel, [sds((na, 256), BF16)], pieces, "piece_sum")
    anchor_halves = call(
        anchors_kernel,
        [sds((na, 128), F32), sds((na, 128), BF16)],
        [place, *dqs, *over_x(dkv), *x_weights],
        "anchors",
        scratch=[pltpu.VMEM((na, X * 384), BF16), pltpu.VMEM((256, X * 384), BF16)],
        smem=1,
        after=cell_halves[:1],
    )
    return over_y(*anchor_halves), over_y(*cell_halves)


def solution(mesh):
    parts = jax.sharding.Mesh(mesh.devices.reshape(X, Y_HI, Y_LO, Z, CORES), (*HEAD, *TOK))
    return jax.shard_map(
        per_device,
        mesh=parts,
        in_specs=(
            P(TOK, None),
            P(TOK, None),
            P(None, HEAD),
            P(None, HEAD),
            P(None, HEAD),
            P(HEAD, None),
            P(TOK, None),
            P(TOK, None),
        ),
        out_specs=(P(TOK, HEAD), P(TOK, HEAD)),
        check_vma=False,
    )
```

```python
import functools

import jax
import jax.numpy as jnp
from jax import lax
from jax.experimental import pallas as pl
from jax.experimental.pallas import tpu as pltpu
from jax.sharding import PartitionSpec as P

HEAD_DIM = 64
SCALE = HEAD_DIM ** (-0.5)
LOG2E = 1.4426950408889634
Y_LO, Z, CORES = 2, 8, 2
X, Y_HI = 4, 2
HEAD = ("x", "y_hi")
TOK = ("y_lo", "z", "core")
STEP = 128
BF16 = jnp.bfloat16
F32 = jnp.float32
COST = {"scores": 15 * 10**8, "pair": 15 * 10**8, "anchors": 10**8}


def tok_perm(move):
    pairs = []
    for yl in range(Y_LO):
        for z in range(Z):
            for core in range(CORES):
                yl2, z2, core2 = move(yl, z, core)
                pairs.append(
                    ((yl * Z + z) * CORES + core, (yl2 * Z + z2 % Z) * CORES + core2)
                )
    return pairs


def head_perm(move):
    pairs = []
    for x in range(X):
        for yh in range(Y_HI):
            x2, yh2 = move(x, yh)
            pairs.append((x * Y_HI + yh, (x2 % X) * Y_HI + yh2))
    return pairs


SWAP_CORE = tok_perm(lambda yl, z, c: (yl, z, 1 - c))
SWAP_Y = tok_perm(lambda yl, z, c: (1 - yl, z, c))
SWAP_BOTH = tok_perm(lambda yl, z, c: (1 - yl, z, 1 - c))
GATHER = [
    tok_perm(lambda yl, z, c: (yl, z, 0) if c == 0 else (yl, z - 1, 1)),
    tok_perm(lambda yl, z, c: (yl, z - 1, 1) if c == 0 else (yl, z, 0)),
]
RETURN = [[(b, a) for a, b in perm] for perm in GATHER]
HOPS = 3
FORTH = [
    tok_perm(lambda yl, z, c, j=j: (yl, z + j, 0) if c == 0 else (yl, z - j, 1))
    for j in range(HOPS + 1)
]
BACK = [[(b, a) for a, b in perm] for perm in FORTH]
SHIFT_X = [head_perm(lambda x, yh, r=r: (x + r, yh)) for r in range(X)]
SWAP_YH = head_perm(lambda x, yh: (x, 1 - yh))


def dot(a, b, ca, cb):
    return lax.dot_general(a, b, (((ca,), (cb,)), ((), ())), preferred_element_type=F32)


def call(body, outs, args, name, scratch=(), smem=0, hbm=(), after=(), vmem=20):
    def spec(i):
        if i < smem:
            return pl.BlockSpec(memory_space=pltpu.SMEM)
        if i >= len(args):
            return pl.BlockSpec(memory_space=pl.ANY)
        return pl.BlockSpec(memory_space=pltpu.HBM if i in hbm else pltpu.VMEM)

    def kernel(*refs):
        body(*refs[: len(args)], *refs[len(args) + len(after) :])

    return pl.pallas_call(
        kernel,
        out_shape=tuple(outs),
        in_specs=[spec(i) for i in range(len(args) + len(after))],
        out_specs=tuple(pl.BlockSpec(memory_space=pltpu.VMEM) for _ in outs),
        scratch_shapes=list(scratch),
        compiler_params=pltpu.CompilerParams(vmem_limit_bytes=vmem << 20),
        cost_estimate=pl.CostEstimate(
            flops=COST.get(name, 10**10), bytes_accessed=10**6, transcendentals=0
        ),
        name=name,
    )(*args, *after)


def sds(shape, dtype):
    return jax.ShapeDtypeStruct(shape, dtype)


def kv_kernel(rows_hbm, w_key_hbm, w_value_hbm, out, rows, w_key, w_value, sems):
    copies = [
        pltpu.make_async_copy(src, dst, sems.at[i])
        for i, (src, dst) in enumerate(
            ((rows_hbm, rows), (w_key_hbm, w_key), (w_value_hbm, w_value))
        )
    ]
    for copy in copies:
        copy.start()
    copies[0].wait()
    copies[1].wait()
    out[:, 0:128] = dot(rows[...], w_key[...], 1, 0).astype(BF16)
    copies[2].wait()
    out[:, 128:256] = dot(rows[...], w_value[...], 1, 0).astype(BF16)


def qd_kernel(anchors, cells, grad_a, grad_c, w_query, w_out, out):
    na = anchors.shape[0]
    wq = w_query[...]
    wo = w_out[...]
    for lo, rows, grads in ((0, anchors, grad_a), (na, cells, grad_c)):
        hi = lo + rows.shape[0]
        out[lo:hi, 0:128] = dot(rows[...], wq, 1, 0).astype(BF16) * SCALE
        out[lo:hi, 128:256] = dot(grads[...], wo, 1, 1).astype(BF16)


def stats_block(kv, rhs, before, out):
    total = rhs.shape[0] // 2
    keys = kv[:, 0:128]
    values = kv[:, 128:256]
    for tile in range(0, total, 256):
        cols = slice(tile, tile + 256)
        for h in range(2):
            lo = h * total + tile
            s = dot(keys, rhs[lo : lo + 256, 0:128], 1, 1)
            peak = jnp.max(s, axis=0, keepdims=True) * LOG2E
            if before is not None:
                old_peak = before[h : h + 1, cols]
                peak = jnp.maximum(peak, old_peak)
            e = jnp.exp2(s * LOG2E - peak)
            dp = dot(values, rhs[lo : lo + 256, 128:256], 1, 1)
            norm = jnp.sum(e, axis=0, keepdims=True)
            mass = jnp.sum(e * dp, axis=0, keepdims=True)
            if before is not None:
                factor = jnp.exp2(old_peak - peak)
                norm += factor * before[2 + h : 3 + h, cols]
                mass += factor * before[4 + h : 5 + h, cols]
            out[h : h + 1, cols] = peak
            out[2 + h : 3 + h, cols] = norm
            out[4 + h : 5 + h, cols] = mass
    out[6:8, :] = jnp.zeros((2, total), F32)


def first_stats_kernel(count, *refs):
    first, second = refs[:2]
    blocks = refs[2 : 2 + count]
    stats, rhs = refs[2 + count :]
    half = first.shape[0]
    lane = lax.broadcasted_iota(jnp.int32, (1, 256), 1)
    for h in range(2):
        keep = lane // HEAD_DIM % 2 == h
        for part, rows in enumerate((first, second)):
            x = rows[...]
            lo = (2 * h + part) * half
            rhs[lo : lo + half, :] = jnp.where(keep, x, jnp.zeros_like(x))
    for i, kv in enumerate(blocks):
        stats_block(kv, rhs, stats if i else None, stats)


def first_stats(first, second, blocks):
    total = 2 * first.shape[0]
    return call(
        functools.partial(first_stats_kernel, len(blocks)),
        [sds((8, total), F32), sds((2 * total, 256), BF16)],
        [first, second, *blocks],
        "first_stats",
    )


def next_stats_kernel(kv, rhs, before, stats):
    stats_block(kv, rhs, before, stats)


def both_stats_kernel(kv, rhs_a, rhs_b, before_a, before_b, stats):
    stats_block(kv, rhs_a, before_a, stats.at[0:8])
    stats_block(kv, rhs_b, before_b, stats.at[8:16])


def merged(mine, theirs, a, b, i, j):
    for h in range(2):
        m1 = mine[i + h : i + h + 1, a]
        m2 = theirs[j + h : j + h + 1, b]
        peak = jnp.maximum(m1, m2)
        f1 = jnp.exp2(m1 - peak)
        f2 = jnp.exp2(m2 - peak)
        norm = f1 * mine[i + 2 + h : i + 3 + h, a] + f2 * theirs[j + 2 + h : j + 3 + h, b]
        mass = f1 * mine[i + 4 + h : i + 5 + h, a] + f2 * theirs[j + 4 + h : j + 5 + h, b]
        yield h, peak, norm, mass


def merge_cores_kernel(mine, theirs, out):
    half = mine.shape[1] // 2
    low, high = slice(0, half), slice(half, 2 * half)
    for i in (0, 8):
        for a, b in ((low, high), (high, low)):
            for h, peak, norm, mass in merged(mine, theirs, a, b, i, i):
                out[i + h : i + h + 1, a] = peak
                out[i + 2 + h : i + 3 + h, a] = norm
                out[i + 4 + h : i + 5 + h, a] = mass
        out[i + 6 : i + 8, :] = jnp.zeros((2, 2 * half), F32)


def merge_y_kernel(mine, theirs, out):
    whole = slice(0, mine.shape[1])
    for i, j in ((0, 8), (8, 0)):
        for h, peak, norm, mass in merged(mine, theirs, whole, whole, i, j):
            out[i + h : i + h + 1, whole] = peak + jnp.log(norm) * LOG2E
            out[i + 2 + h : i + 3 + h, whole] = mass / norm
        out[i + 4 : i + 8, :] = jnp.zeros((4, mine.shape[1]), F32)


def scores_kernel(has_before, is_last, *refs):
    kv, *rhs = refs[:3]
    stats = refs[3]
    refs = refs[4:]
    before = None
    if has_before:
        before, refs = refs[0], refs[1:]
    p_t, ds_t, *dq = refs
    total = rhs[0].shape[0] // 2
    half = total // 2
    n = kv.shape[0]
    keys_t = kv[:, 0:128].T
    step = STEP
    for g in range(2):
        for h in range(2):
            here = slice(h * total, (h + 1) * total)
            there = slice((2 * g + h) * total, (2 * g + h + 1) * total)
            lse = stats[8 * g + h : 8 * g + h + 1, :]
            delta = stats[8 * g + 2 + h : 8 * g + 3 + h, :]
            for c in range(0, n, step):
                s = dot(kv[c : c + step, 0:128], rhs[g][here, 0:128], 1, 1)
                p = jnp.exp2(s * LOG2E - lse)
                dp = dot(kv[c : c + step, 128:256], rhs[g][here, 128:256], 1, 1)
                ds = p * (dp - delta)
                p_t[c : c + step, there] = p.astype(BF16)
                ds_t[c : c + step, there] = ds.astype(BF16)
            out = slice(h * HEAD_DIM, (h + 1) * HEAD_DIM)
            cols = slice(g * total, (g + 1) * total)
            part = dot(keys_t[out, :], ds_t[:, there], 1, 0)
            if has_before:
                part += before[out, cols]
            if is_last:
                dq[2 * g][out, :] = part[:, :half].astype(dq[2 * g].dtype)
                dq[2 * g + 1][out, :] = part[:, half:].astype(BF16)
            else:
                dq[0][out, cols] = part


def scores(kv, rhs, stats, before, is_last, after=()):
    total = rhs[0].shape[0] // 2
    args = [kv, *rhs, stats] + ([] if before is None else [before])
    outs = [sds((kv.shape[0], 4 * total), BF16)] * 2
    if is_last:
        outs += [sds((128, total // 2), F32)] + [sds((128, total // 2), BF16)] * 3
    else:
        outs += [sds((128, 2 * total), F32)]
    return call(
        functools.partial(scores_kernel, before is not None, is_last),
        outs,
        args,
        "scores",
        after=after,
    )


def pair_kernel(first, p_t, ds_t, rhs_a, rhs_b, *outs):
    n = rhs_a.shape[0]
    rows = slice(first, first + sum(out.shape[0] for out in outs))
    for cols, weights in ((slice(0, 128), ds_t), (slice(128, 256), p_t)):
        total = dot(weights[rows, :n], rhs_a[:, cols], 1, 0)
        total += dot(weights[rows, n:], rhs_b[:, cols], 1, 0)
        lo = 0
        for out in outs:
            out[:, cols] = total[lo : lo + out.shape[0]].astype(out.dtype)
            lo += out.shape[0]


def pair(weights, rhs, first, outs, after=()):
    return call(
        functools.partial(pair_kernel, first), outs, [*weights, *rhs], "pair", after=after
    )


def pair_sum_kernel(own, a, b, c, *outs):
    n = outs[0].shape[0]
    for i, out in enumerate(outs):
        rows = slice(i * n, (i + 1) * n)
        more = (a[rows, :].astype(F32) + b[rows, :].astype(F32)) + c[rows, :].astype(F32)
        out[...] = (own[rows, :] + more).astype(BF16)


def stack_kernel(place, w_query, w_key, w_value, out, sems):
    depth = w_query.shape[0] // X
    copies = []
    for r in range(X):
        start = lax.rem(place[0] + X - r, X) * depth + place[0] * (depth // X)
        for side in range(2):
            y_hi = place[1] if side == 0 else 1 - place[1]
            rows = pl.ds(pl.multiple_of(start + y_hi * 128, 128), 128)
            for w, lo in ((w_query, r), (w_key, X + 2 * r), (w_value, X + 2 * r + 1)):
                to = out.at[side * 128 : (side + 1) * 128, lo * 128 : (lo + 1) * 128]
                copies.append(pltpu.make_async_copy(w.at[rows, :], to, sems.at[len(copies)]))
    for copy in copies:
        copy.start()
    for copy in copies:
        copy.wait()


def dq_sum_kernel(mine, a, b, c, dq, first):
    more = (a[...].astype(F32) + b[...].astype(F32)) + c[...].astype(F32)
    total = ((mine[...] + more) * SCALE).astype(BF16)
    dq[...] = total
    first[...] = total[:, : first.shape[1]]


def piece_sum_kernel(a, b, out):
    out[...] = (a[...].astype(F32) + b[...].astype(F32)).astype(BF16)


def cells_kernel(own, back_1, back_2a, back_2b, back_3, weights, mine, theirs, dq):
    na = own.shape[1] - mine.shape[0]
    cut = back_2a.shape[1]
    for r, part in ((0, own), (1, back_1), (3, back_3)):
        dq[r * 128 : (r + 1) * 128, :] = part[:, na:]
    dq[256:384, : cut - na] = back_2a[:, na:]
    dq[256:384, cut - na :] = back_2b[...]
    out = dot(dq[...], weights[:, : X * 128], 0, 1)
    mine[...] = out[:, 0:128]
    theirs[...] = out[:, 128:256].astype(BF16)


def anchors_kernel(*refs):
    dqs, dkvs, (weights, cells_mine, cells_theirs, mine, theirs, rows) = refs[:X], refs[X : 2 * X], refs[2 * X :]
    na = rows.shape[0]
    for r, (dq, dkv) in enumerate(zip(dqs, dkvs)):
        rows[:, r * 128 : (r + 1) * 128] = dq[:, :na].T
        lo = X * 128 + r * 256
        rows[:, lo : lo + 256] = dkv[...]
    out = dot(rows[...], weights[...], 1, 1)
    mine[:na, :] = out[:, 0:128]
    theirs[:na, :] = out[:, 128:256].astype(BF16)
    mine[na:, :] = cells_mine[...]
    theirs[na:, :] = cells_theirs[...]


def last_sum_kernel(mine, theirs, anchors, cells):
    na = anchors.shape[0]
    total = (mine[...] + theirs[...].astype(F32)).astype(BF16)
    anchors[...] = total[:na, :]
    cells[...] = total[na:, :]


def over_x(array):
    return [array] + [lax.ppermute(array, HEAD, SHIFT_X[r]) for r in range(1, X)]


def per_device(anchors, cells, w_query, w_key, w_value, w_out, grad_a, grad_c):
    na, nc, d = anchors.shape[0], cells.shape[0], anchors.shape[1]
    rows = na + nc
    total = 2 * rows
    place = jnp.stack([lax.axis_index("x"), lax.axis_index("y_hi")]).astype(jnp.int32)

    w_all = [lax.all_gather(w, "x", axis=0, tiled=True) for w in (w_query, w_key, w_value)]
    (kv,) = call(
        kv_kernel,
        [sds((na, 256), BF16)],
        [anchors, w_key, w_value],
        "kv",
        scratch=[
            pltpu.VMEM((na, d), BF16),
            pltpu.VMEM((d, 128), BF16),
            pltpu.VMEM((d, 128), BF16),
            pltpu.SemaphoreType.DMA((3,)),
        ],
        hbm=(0, 1, 2),
        vmem=60,
    )
    block = jnp.concatenate([lax.ppermute(kv, TOK, perm) for perm in GATHER], axis=0)
    blocks = [block] + [lax.ppermute(block, TOK, FORTH[j]) for j in range(1, HOPS + 1)]

    (mine,) = call(
        qd_kernel,
        [sds((rows, 256), BF16)],
        [anchors, cells, grad_a, grad_c, w_query, w_out],
        "qd",
        after=[place, kv],
    )
    core_rows = lax.ppermute(mine, TOK, SWAP_CORE)
    y_rows = lax.ppermute(mine, TOK, SWAP_Y)
    both_rows = lax.ppermute(y_rows, TOK, SWAP_CORE)

    stats_a, rhs_a = first_stats(mine, core_rows, blocks[:1])
    for j in range(1, HOPS):
        (stats_a,) = call(
            next_stats_kernel, [sds((8, total), F32)], [blocks[j], rhs_a, stats_a], "stats"
        )
    stats_b, rhs_b = first_stats(y_rows, both_rows, blocks[:HOPS])
    (stats,) = call(
        both_stats_kernel,
        [sds((16, total), F32)],
        [blocks[HOPS], rhs_a, rhs_b, stats_a, stats_b],
        "both_stats",
    )
    for merge_kernel, perm in ((merge_cores_kernel, SWAP_CORE), (merge_y_kernel, SWAP_Y)):
        (stats,) = call(
            merge_kernel,
            [sds((16, total), F32)],
            [stats, lax.ppermute(stats, TOK, perm)],
            "merge",
        )
    rhs = (rhs_a, rhs_b)
    n = block.shape[0]

    far = jnp.concatenate([blocks[3], blocks[2]], axis=0)
    near = jnp.concatenate([blocks[1], blocks[0]], axis=0)
    *weights, dq = scores(far, rhs, stats, None, False)
    dkv_3, dkv_2 = pair(weights, rhs, 0, [sds((n, 256), BF16)] * 2)
    sums = [lax.ppermute(dkv_3, TOK, BACK[3]), lax.ppermute(dkv_2, TOK, BACK[2])]
    *weights, dq_mine, dq_core, dq_y, dq_both = scores(
        near, rhs, stats, dq, True, after=[dkv_3]
    )
    dq_others = [
        lax.ppermute(part, TOK, perm)
        for part, perm in ((dq_y, SWAP_Y), (dq_both, SWAP_BOTH), (dq_core, SWAP_CORE))
    ]
    (dkv_1,) = pair(weights, rhs, 0, [sds((n, 256), BF16)], after=list(sums))
    sums.append(lax.ppermute(dkv_1, TOK, BACK[1]))
    (dkv,) = pair(weights, rhs, n, [sds((n, 256), F32)], after=[dkv_1])
    pieces = call(
        pair_sum_kernel, [sds((na, 256), BF16)] * len(RETURN), [dkv, *sums], "pair_sum"
    )
    pieces = [lax.ppermute(piece, TOK, perm) for piece, perm in zip(pieces, RETURN)]
    cut = 2 * 128
    dq, dq_first = call(
        dq_sum_kernel,
        [sds((128, rows), BF16), sds((128, cut), BF16)],
        [dq_mine, *dq_others],
        "dq_sum",
        after=[dkv],
    )
    (x_weights,) = call(
        stack_kernel,
        [sds((256, X * 384), BF16)],
        [place, *w_all],
        "stack",
        smem=1,
        hbm=(1, 2, 3),
        scratch=[pltpu.SemaphoreType.DMA((6 * X,))],
        after=[dq],
    )
    back_1 = lax.ppermute(dq, HEAD, SHIFT_X[1])
    back_3 = lax.ppermute(dq, HEAD, SHIFT_X[3])
    back_2a = lax.ppermute(dq_first, HEAD, SHIFT_X[2])
    back_2b = lax.ppermute(back_3[:, cut:], HEAD, SHIFT_X[3])
    cells_mine, cells_theirs = call(
        cells_kernel,
        [sds((nc, 128), F32), sds((nc, 128), BF16)],
        [dq, back_1, back_2a, back_2b, back_3, x_weights],
        "cells",
        scratch=[pltpu.VMEM((X * 128, nc), BF16)],
    )
    (dkv,) = call(
        piece_sum_kernel, [sds((na, 256), BF16)], pieces, "piece_sum", after=[x_weights]
    )
    mine, theirs = call(
        anchors_kernel,
        [sds((rows, 128), F32), sds((rows, 128), BF16)],
        [dq, back_1, back_2a, back_3, *over_x(dkv), x_weights, cells_mine, cells_theirs],
        "anchors",
        scratch=[pltpu.VMEM((na, X * 384), BF16)],
    )
    return call(
        last_sum_kernel,
        [sds((na, 128), BF16), sds((nc, 128), BF16)],
        [mine, lax.ppermute(theirs, HEAD, SWAP_YH)],
        "last_sum",
    )


def solution(mesh):
    parts = jax.sharding.Mesh(mesh.devices.reshape(X, Y_HI, Y_LO, Z, CORES), (*HEAD, *TOK))
    return jax.shard_map(
        per_device,
        mesh=parts,
        in_specs=(
            P(TOK, None),
            P(TOK, None),
            P(None, HEAD),
            P(None, HEAD),
            P(None, HEAD),
            P(HEAD, None),
            P(TOK, None),
            P(TOK, None),
        ),
        out_specs=(P(TOK, HEAD), P(TOK, HEAD)),
        check_vma=False,
    )
```

```python
import functools

import jax
import jax.numpy as jnp
from jax import lax
from jax.experimental import pallas as pl
from jax.experimental.pallas import tpu as pltpu
from jax.sharding import PartitionSpec as P

HEAD_DIM = 64
SCALE = HEAD_DIM ** (-0.5)
LOG2E = 1.4426950408889634
Y_LO, Z, CORES = 2, 8, 2
X, Y_HI = 4, 2
HEAD = ("x", "y_hi")
TOK = ("y_lo", "z", "core")
STEP = 128
BF16 = jnp.bfloat16
F32 = jnp.float32
COST = {"scores": 15 * 10**8, "pair": 15 * 10**8, "anchors": 10**8}


def tok_perm(move):
    pairs = []
    for yl in range(Y_LO):
        for z in range(Z):
            for core in range(CORES):
                yl2, z2, core2 = move(yl, z, core)
                pairs.append(
                    ((yl * Z + z) * CORES + core, (yl2 * Z + z2 % Z) * CORES + core2)
                )
    return pairs


def head_perm(move):
    pairs = []
    for x in range(X):
        for yh in range(Y_HI):
            x2, yh2 = move(x, yh)
            pairs.append((x * Y_HI + yh, (x2 % X) * Y_HI + yh2))
    return pairs


SWAP_CORE = tok_perm(lambda yl, z, c: (yl, z, 1 - c))
SWAP_Y = tok_perm(lambda yl, z, c: (1 - yl, z, c))
SWAP_BOTH = tok_perm(lambda yl, z, c: (1 - yl, z, 1 - c))
GATHER = [
    tok_perm(lambda yl, z, c: (yl, z, 0) if c == 0 else (yl, z - 1, 1)),
    tok_perm(lambda yl, z, c: (yl, z - 1, 1) if c == 0 else (yl, z, 0)),
]
RETURN = [[(b, a) for a, b in perm] for perm in GATHER]
HOPS = 3
FORTH = [
    tok_perm(lambda yl, z, c, j=j: (yl, z + j, 0) if c == 0 else (yl, z - j, 1))
    for j in range(HOPS + 1)
]
BACK = [[(b, a) for a, b in perm] for perm in FORTH]
SHIFT_X = [head_perm(lambda x, yh, r=r: (x + r, yh)) for r in range(X)]
SWAP_YH = head_perm(lambda x, yh: (x, 1 - yh))


def dot(a, b, ca, cb):
    return lax.dot_general(a, b, (((ca,), (cb,)), ((), ())), preferred_element_type=F32)


def call(body, outs, args, name, scratch=(), smem=0, hbm=(), after=(), vmem=20):
    def spec(i):
        if i < smem:
            return pl.BlockSpec(memory_space=pltpu.SMEM)
        if i >= len(args):
            return pl.BlockSpec(memory_space=pl.ANY)
        return pl.BlockSpec(memory_space=pltpu.HBM if i in hbm else pltpu.VMEM)

    def kernel(*refs):
        body(*refs[: len(args)], *refs[len(args) + len(after) :])

    return pl.pallas_call(
        kernel,
        out_shape=tuple(outs),
        in_specs=[spec(i) for i in range(len(args) + len(after))],
        out_specs=tuple(pl.BlockSpec(memory_space=pltpu.VMEM) for _ in outs),
        scratch_shapes=list(scratch),
        compiler_params=pltpu.CompilerParams(vmem_limit_bytes=vmem << 20),
        cost_estimate=pl.CostEstimate(
            flops=COST.get(name, 10**10), bytes_accessed=10**6, transcendentals=0
        ),
        name=name,
    )(*args, *after)


def sds(shape, dtype):
    return jax.ShapeDtypeStruct(shape, dtype)


def kv_kernel(rows_hbm, w_key_hbm, w_value_hbm, out, rows, w_key, w_value, sems):
    copies = [
        pltpu.make_async_copy(src, dst, sems.at[i])
        for i, (src, dst) in enumerate(
            ((rows_hbm, rows), (w_key_hbm, w_key), (w_value_hbm, w_value))
        )
    ]
    for copy in copies:
        copy.start()
    copies[0].wait()
    copies[1].wait()
    out[:, 0:128] = dot(rows[...], w_key[...], 1, 0).astype(BF16)
    copies[2].wait()
    out[:, 128:256] = dot(rows[...], w_value[...], 1, 0).astype(BF16)


def qd_kernel(anchors, cells, grad_a, grad_c, w_query, w_out, out):
    na = anchors.shape[0]
    wq = w_query[...]
    wo = w_out[...]
    for lo, rows, grads in ((0, anchors, grad_a), (na, cells, grad_c)):
        hi = lo + rows.shape[0]
        out[lo:hi, 0:128] = dot(rows[...], wq, 1, 0).astype(BF16) * SCALE
        out[lo:hi, 128:256] = dot(grads[...], wo, 1, 1).astype(BF16)


def stats_block(kv, rhs, before, out):
    total = rhs.shape[0] // 2
    keys = kv[:, 0:128]
    values = kv[:, 128:256]

    @pl.loop(0, total // 256)
    def _(index):
        tile = pl.multiple_of(index * 256, 256)
        cols = pl.ds(tile, 256)
        for h in range(2):
            rows = pl.ds(pl.multiple_of(h * total + tile, 256), 256)
            s = dot(keys, rhs[rows, 0:128], 1, 1)
            peak = jnp.max(s, axis=0, keepdims=True) * LOG2E
            if before is not None:
                old_peak = before[h : h + 1, cols]
                peak = jnp.maximum(peak, old_peak)
            e = jnp.exp2(s * LOG2E - peak)
            dp = dot(values, rhs[rows, 128:256], 1, 1)
            norm = jnp.sum(e, axis=0, keepdims=True)
            mass = jnp.sum(e * dp, axis=0, keepdims=True)
            if before is not None:
                factor = jnp.exp2(old_peak - peak)
                norm += factor * before[2 + h : 3 + h, cols]
                mass += factor * before[4 + h : 5 + h, cols]
            out[h : h + 1, cols] = peak
            out[2 + h : 3 + h, cols] = norm
            out[4 + h : 5 + h, cols] = mass

    out[6:8, :] = jnp.zeros((2, total), F32)


def first_stats_kernel(count, *refs):
    first, second = refs[:2]
    blocks = refs[2 : 2 + count]
    stats, rhs = refs[2 + count :]
    half = first.shape[0]
    lane = lax.broadcasted_iota(jnp.int32, (1, 256), 1)
    for h in range(2):
        keep = lane // HEAD_DIM % 2 == h
        for part, rows in enumerate((first, second)):
            x = rows[...]
            lo = (2 * h + part) * half
            rhs[lo : lo + half, :] = jnp.where(keep, x, jnp.zeros_like(x))
    for i, kv in enumerate(blocks):
        stats_block(kv, rhs, stats if i else None, stats)


def first_stats(first, second, blocks):
    total = 2 * first.shape[0]
    return call(
        functools.partial(first_stats_kernel, len(blocks)),
        [sds((8, total), F32), sds((2 * total, 256), BF16)],
        [first, second, *blocks],
        "first_stats",
    )


def next_stats_kernel(kv, rhs, before, stats):
    stats_block(kv, rhs, before, stats)


def both_stats_kernel(kv, rhs_a, rhs_b, before_a, before_b, stats):
    stats_block(kv, rhs_a, before_a, stats.at[0:8])
    stats_block(kv, rhs_b, before_b, stats.at[8:16])


def merged(mine, theirs, a, b, i, j):
    for h in range(2):
        m1 = mine[i + h : i + h + 1, a]
        m2 = theirs[j + h : j + h + 1, b]
        peak = jnp.maximum(m1, m2)
        f1 = jnp.exp2(m1 - peak)
        f2 = jnp.exp2(m2 - peak)
        norm = f1 * mine[i + 2 + h : i + 3 + h, a] + f2 * theirs[j + 2 + h : j + 3 + h, b]
        mass = f1 * mine[i + 4 + h : i + 5 + h, a] + f2 * theirs[j + 4 + h : j + 5 + h, b]
        yield h, peak, norm, mass


def merge_cores_kernel(mine, theirs, out):
    half = mine.shape[1] // 2
    low, high = slice(0, half), slice(half, 2 * half)
    for i in (0, 8):
        for a, b in ((low, high), (high, low)):
            for h, peak, norm, mass in merged(mine, theirs, a, b, i, i):
                out[i + h : i + h + 1, a] = peak
                out[i + 2 + h : i + 3 + h, a] = norm
                out[i + 4 + h : i + 5 + h, a] = mass
        out[i + 6 : i + 8, :] = jnp.zeros((2, 2 * half), F32)


def merge_y_kernel(mine, theirs, out):
    whole = slice(0, mine.shape[1])
    for i, j in ((0, 8), (8, 0)):
        for h, peak, norm, mass in merged(mine, theirs, whole, whole, i, j):
            out[i + h : i + h + 1, whole] = peak + jnp.log(norm) * LOG2E
            out[i + 2 + h : i + 3 + h, whole] = mass / norm
        out[i + 4 : i + 8, :] = jnp.zeros((4, mine.shape[1]), F32)


def scores_kernel(has_before, is_last, *refs):
    first, second, *rhs = refs[:4]
    stats = refs[4]
    refs = refs[5:]
    before = None
    if has_before:
        before, refs = refs[0], refs[1:]
    p_t, ds_t, *dq, kv, keys_t = refs
    kv[: first.shape[0], :] = first[...]
    kv[first.shape[0] :, :] = second[...]
    total = rhs[0].shape[0] // 2
    half = total // 2
    n = kv.shape[0]
    keys_t[...] = kv[:, 0:128].T

    @pl.loop(0, 2)
    def _(h):
        here = pl.ds(pl.multiple_of(h * total, 128), total)
        out = pl.ds(pl.multiple_of(h * HEAD_DIM, HEAD_DIM), HEAD_DIM)
        for g in range(2):
            there = pl.ds(pl.multiple_of((2 * g + h) * total, 128), total)
            lse = stats[pl.ds(8 * g + h, 1), :]
            delta = stats[pl.ds(8 * g + 2 + h, 1), :]
            for c in range(0, n, STEP):
                s = dot(kv[c : c + STEP, 0:128], rhs[g][here, 0:128], 1, 1)
                p = jnp.exp2(s * LOG2E - lse)
                dp = dot(kv[c : c + STEP, 128:256], rhs[g][here, 128:256], 1, 1)
                ds = p * (dp - delta)
                p_t[c : c + STEP, there] = p.astype(BF16)
                ds_t[c : c + STEP, there] = ds.astype(BF16)
            cols = slice(g * total, (g + 1) * total)
            part = dot(keys_t[out, :], ds_t[:, there], 1, 0)
            if has_before:
                part += before[out, cols]
            if is_last:
                dq[2 * g][out, :] = part[:, :half].astype(dq[2 * g].dtype)
                dq[2 * g + 1][out, :] = part[:, half:].astype(BF16)
            else:
                dq[0][out, cols] = part


def scores(blocks, rhs, stats, before, is_last, after=()):
    total = rhs[0].shape[0] // 2
    n = sum(block.shape[0] for block in blocks)
    args = [*blocks, *rhs, stats] + ([] if before is None else [before])
    outs = [sds((n, 4 * total), BF16)] * 2
    if is_last:
        outs += [sds((128, total // 2), F32)] + [sds((128, total // 2), BF16)] * 3
    else:
        outs += [sds((128, 2 * total), F32)]
    return call(
        functools.partial(scores_kernel, before is not None, is_last),
        outs,
        args,
        "scores",
        scratch=[pltpu.VMEM((n, 256), BF16), pltpu.VMEM((128, n), BF16)],
        after=after,
    )


def pair_kernel(first, p_t, ds_t, rhs_a, rhs_b, *outs):
    n = rhs_a.shape[0]
    rows = slice(first, first + sum(out.shape[0] for out in outs))
    for cols, weights in ((slice(0, 128), ds_t), (slice(128, 256), p_t)):
        total = dot(weights[rows, :n], rhs_a[:, cols], 1, 0)
        total += dot(weights[rows, n:], rhs_b[:, cols], 1, 0)
        lo = 0
        for out in outs:
            out[:, cols] = total[lo : lo + out.shape[0]].astype(out.dtype)
            lo += out.shape[0]


def pair(weights, rhs, first, outs, after=()):
    return call(
        functools.partial(pair_kernel, first), outs, [*weights, *rhs], "pair", after=after
    )


def pair_sum_kernel(own, a, b, c, *outs):
    n = outs[0].shape[0]
    for i, out in enumerate(outs):
        rows = slice(i * n, (i + 1) * n)
        more = (a[rows, :].astype(F32) + b[rows, :].astype(F32)) + c[rows, :].astype(F32)
        out[...] = (own[rows, :] + more).astype(BF16)


def weights_kernel(distances, place, w_query, w_key, w_value, *outs):
    width = outs[0].shape[0]
    for r, out in zip(distances, outs):
        lo = pl.multiple_of(lax.rem(place[0] + r, X) * width, width)
        for i, w in enumerate((w_query, w_key, w_value)):
            out[:, i * 128 : (i + 1) * 128] = w[pl.ds(lo, width), :]


def stack_kernel(place, *refs):
    *parts, out = refs
    for side in range(2):
        y_hi = place[1] if side == 0 else 1 - place[1]
        rows = pl.ds(pl.multiple_of(y_hi * 128, 128), 128)
        here = slice(side * 128, (side + 1) * 128)
        for r, part in enumerate(parts):
            out[here, r * 128 : (r + 1) * 128] = part[rows, 0:128]
            lo = (X + 2 * r) * 128
            out[here, lo : lo + 256] = part[rows, 128:384]


def dq_sum_kernel(mine, a, b, c, dq, first):
    more = (a[...].astype(F32) + b[...].astype(F32)) + c[...].astype(F32)
    total = ((mine[...] + more) * SCALE).astype(BF16)
    dq[...] = total
    first[...] = total[:, : first.shape[1]]


def piece_sum_kernel(a, b, out):
    out[...] = (a[...].astype(F32) + b[...].astype(F32)).astype(BF16)


def cells_kernel(own, back_1, back_2a, back_2b, back_3, weights, mine, theirs, dq):
    na = own.shape[1] - mine.shape[0]
    cut = back_2a.shape[1]
    for r, part in ((0, own), (1, back_1), (3, back_3)):
        dq[r * 128 : (r + 1) * 128, :] = part[:, na:]
    dq[256:384, : cut - na] = back_2a[:, na:]
    dq[256:384, cut - na :] = back_2b[...]
    out = dot(dq[...], weights[:, : X * 128], 0, 1)
    mine[...] = out[:, 0:128]
    theirs[...] = out[:, 128:256].astype(BF16)


def anchors_kernel(*refs):
    dqs, dkvs, (weights, cells_mine, cells_theirs, mine, theirs, rows) = refs[:X], refs[X : 2 * X], refs[2 * X :]
    na = rows.shape[0]
    for r, (dq, dkv) in enumerate(zip(dqs, dkvs)):
        rows[:, r * 128 : (r + 1) * 128] = dq[:, :na].T
        lo = X * 128 + r * 256
        rows[:, lo : lo + 256] = dkv[...]
    out = dot(rows[...], weights[...], 1, 1)
    mine[:na, :] = out[:, 0:128]
    theirs[:na, :] = out[:, 128:256].astype(BF16)
    mine[na:, :] = cells_mine[...]
    theirs[na:, :] = cells_theirs[...]


def last_sum_kernel(mine, theirs, anchors, cells):
    na = anchors.shape[0]
    total = (mine[...] + theirs[...].astype(F32)).astype(BF16)
    anchors[...] = total[:na, :]
    cells[...] = total[na:, :]


def over_x(array):
    return [array] + [lax.ppermute(array, HEAD, SHIFT_X[r]) for r in range(1, X)]


def per_device(anchors, cells, w_query, w_key, w_value, w_out, grad_a, grad_c):
    na, nc, d = anchors.shape[0], cells.shape[0], anchors.shape[1]
    rows = na + nc
    total = 2 * rows
    place = jnp.stack([lax.axis_index("x"), lax.axis_index("y_hi")]).astype(jnp.int32)

    (kv,) = call(
        kv_kernel,
        [sds((na, 256), BF16)],
        [anchors, w_key, w_value],
        "kv",
        scratch=[
            pltpu.VMEM((na, d), BF16),
            pltpu.VMEM((d, 128), BF16),
            pltpu.VMEM((d, 128), BF16),
            pltpu.SemaphoreType.DMA((3,)),
        ],
        hbm=(0, 1, 2),
        vmem=60,
    )
    block = jnp.concatenate([lax.ppermute(kv, TOK, perm) for perm in GATHER], axis=0)
    blocks = [block] + [lax.ppermute(block, TOK, FORTH[j]) for j in range(1, HOPS + 1)]

    (mine,) = call(
        qd_kernel,
        [sds((rows, 256), BF16)],
        [anchors, cells, grad_a, grad_c, w_query, w_out],
        "qd",
        after=[place, kv],
    )
    core_rows = lax.ppermute(mine, TOK, SWAP_CORE)
    y_rows = lax.ppermute(mine, TOK, SWAP_Y)
    both_rows = lax.ppermute(y_rows, TOK, SWAP_CORE)

    stats_a, rhs_a = first_stats(mine, core_rows, blocks[:1])
    def weight_rows(distances, after):
        return call(
            functools.partial(weights_kernel, distances),
            [sds((d // X, 3 * 128), BF16)] * len(distances),
            [place, w_query, w_key, w_value],
            "weights",
            smem=1,
            after=after,
        )

    for j in range(1, HOPS):
        (stats_a,) = call(
            next_stats_kernel, [sds((8, total), F32)], [blocks[j], rhs_a, stats_a], "stats"
        )
    stats_b, rhs_b = first_stats(y_rows, both_rows, blocks[:HOPS])
    (stats,) = call(
        both_stats_kernel,
        [sds((16, total), F32)],
        [blocks[HOPS], rhs_a, rhs_b, stats_a, stats_b],
        "both_stats",
    )
    x_weights = weight_rows(tuple(range(X)), [stats])
    x_weights = [x_weights[0]] + [
        lax.ppermute(x_weights[r], HEAD, SHIFT_X[r]) for r in range(1, X)
    ]
    for merge_kernel, perm in ((merge_cores_kernel, SWAP_CORE), (merge_y_kernel, SWAP_Y)):
        (stats,) = call(
            merge_kernel,
            [sds((16, total), F32)],
            [stats, lax.ppermute(stats, TOK, perm)],
            "merge",
        )
    rhs = (rhs_a, rhs_b)
    n = block.shape[0]

    *weights, dq = scores(blocks[3:1:-1], rhs, stats, None, False)
    dkv_3, dkv_2 = pair(weights, rhs, 0, [sds((n, 256), BF16)] * 2)
    sums = [lax.ppermute(dkv_3, TOK, BACK[3]), lax.ppermute(dkv_2, TOK, BACK[2])]
    *weights, dq_mine, dq_core, dq_y, dq_both = scores(
        blocks[1::-1], rhs, stats, dq, True, after=[dkv_3, *x_weights[1:]]
    )
    dq_others = [
        lax.ppermute(part, TOK, perm)
        for part, perm in ((dq_y, SWAP_Y), (dq_both, SWAP_BOTH), (dq_core, SWAP_CORE))
    ]
    (dkv_1,) = pair(weights, rhs, 0, [sds((n, 256), BF16)], after=list(sums))
    sums.append(lax.ppermute(dkv_1, TOK, BACK[1]))
    (dkv,) = pair(weights, rhs, n, [sds((n, 256), F32)], after=[dkv_1])
    pieces = call(
        pair_sum_kernel, [sds((na, 256), BF16)] * len(RETURN), [dkv, *sums], "pair_sum"
    )
    pieces = [lax.ppermute(piece, TOK, perm) for piece, perm in zip(pieces, RETURN)]
    cut = 2 * 128
    dq, dq_first = call(
        dq_sum_kernel,
        [sds((128, rows), BF16), sds((128, cut), BF16)],
        [dq_mine, *dq_others],
        "dq_sum",
        after=[dkv],
    )
    (x_weights,) = call(
        stack_kernel,
        [sds((256, X * 384), BF16)],
        [place, *x_weights],
        "stack",
        smem=1,
        after=[dq],
    )
    back_1 = lax.ppermute(dq, HEAD, SHIFT_X[1])
    back_3 = lax.ppermute(dq, HEAD, SHIFT_X[3])
    back_2a = lax.ppermute(dq_first, HEAD, SHIFT_X[2])
    back_2b = lax.ppermute(back_3[:, cut:], HEAD, SHIFT_X[3])
    cells_mine, cells_theirs = call(
        cells_kernel,
        [sds((nc, 128), F32), sds((nc, 128), BF16)],
        [dq, back_1, back_2a, back_2b, back_3, x_weights],
        "cells",
        scratch=[pltpu.VMEM((X * 128, nc), BF16)],
    )
    (dkv,) = call(
        piece_sum_kernel, [sds((na, 256), BF16)], pieces, "piece_sum", after=[x_weights]
    )
    mine, theirs = call(
        anchors_kernel,
        [sds((rows, 128), F32), sds((rows, 128), BF16)],
        [dq, back_1, back_2a, back_3, *over_x(dkv), x_weights, cells_mine, cells_theirs],
        "anchors",
        scratch=[pltpu.VMEM((na, X * 384), BF16)],
    )
    return call(
        last_sum_kernel,
        [sds((na, 128), BF16), sds((nc, 128), BF16)],
        [mine, lax.ppermute(theirs, HEAD, SWAP_YH)],
        "last_sum",
    )


def solution(mesh):
    parts = jax.sharding.Mesh(mesh.devices.reshape(X, Y_HI, Y_LO, Z, CORES), (*HEAD, *TOK))
    return jax.shard_map(
        per_device,
        mesh=parts,
        in_specs=(
            P(TOK, None),
            P(TOK, None),
            P(None, HEAD),
            P(None, HEAD),
            P(None, HEAD),
            P(HEAD, None),
            P(TOK, None),
            P(TOK, None),
        ),
        out_specs=(P(TOK, HEAD), P(TOK, HEAD)),
        check_vma=False,
    )
```

```python
import functools

import jax
import jax.numpy as jnp
from jax import lax
from jax.experimental import pallas as pl
from jax.experimental.pallas import tpu as pltpu
from jax.sharding import PartitionSpec as P

HEAD_DIM = 64
SCALE = HEAD_DIM ** (-0.5)
LOG2E = 1.4426950408889634
Y_LO, Z, CORES = 2, 8, 2
X, Y_HI = 4, 2
HEAD = ("x", "y_hi")
TOK = ("y_lo", "z", "core")
STEP = 128
BF16 = jnp.bfloat16
F32 = jnp.float32
COST = {"scores": 15 * 10**8, "pair": 15 * 10**8, "anchors": 10**8}


def tok_perm(move):
    pairs = []
    for yl in range(Y_LO):
        for z in range(Z):
            for core in range(CORES):
                yl2, z2, core2 = move(yl, z, core)
                pairs.append(
                    ((yl * Z + z) * CORES + core, (yl2 * Z + z2 % Z) * CORES + core2)
                )
    return pairs


def head_perm(move):
    pairs = []
    for x in range(X):
        for yh in range(Y_HI):
            x2, yh2 = move(x, yh)
            pairs.append((x * Y_HI + yh, (x2 % X) * Y_HI + yh2))
    return pairs


SWAP_CORE = tok_perm(lambda yl, z, c: (yl, z, 1 - c))
SWAP_Y = tok_perm(lambda yl, z, c: (1 - yl, z, c))
SWAP_BOTH = tok_perm(lambda yl, z, c: (1 - yl, z, 1 - c))
GATHER = [
    tok_perm(lambda yl, z, c: (yl, z, 0) if c == 0 else (yl, z - 1, 1)),
    tok_perm(lambda yl, z, c: (yl, z - 1, 1) if c == 0 else (yl, z, 0)),
]
RETURN = [[(b, a) for a, b in perm] for perm in GATHER]
HOPS = 3
FORTH = [
    tok_perm(lambda yl, z, c, j=j: (yl, z + j, 0) if c == 0 else (yl, z - j, 1))
    for j in range(HOPS + 1)
]
BACK = [[(b, a) for a, b in perm] for perm in FORTH]
SHIFT_X = [head_perm(lambda x, yh, r=r: (x + r, yh)) for r in range(X)]
SWAP_YH = head_perm(lambda x, yh: (x, 1 - yh))


def dot(a, b, ca, cb):
    return lax.dot_general(a, b, (((ca,), (cb,)), ((), ())), preferred_element_type=F32)


def call(body, outs, args, name, scratch=(), smem=0, hbm=(), after=(), vmem=20):
    def spec(i):
        if i < smem:
            return pl.BlockSpec(memory_space=pltpu.SMEM)
        if i >= len(args):
            return pl.BlockSpec(memory_space=pl.ANY)
        return pl.BlockSpec(memory_space=pltpu.HBM if i in hbm else pltpu.VMEM)

    def kernel(*refs):
        body(*refs[: len(args)], *refs[len(args) + len(after) :])

    return pl.pallas_call(
        kernel,
        out_shape=tuple(outs),
        in_specs=[spec(i) for i in range(len(args) + len(after))],
        out_specs=tuple(pl.BlockSpec(memory_space=pltpu.VMEM) for _ in outs),
        scratch_shapes=list(scratch),
        compiler_params=pltpu.CompilerParams(vmem_limit_bytes=vmem << 20),
        cost_estimate=pl.CostEstimate(
            flops=COST.get(name, 10**10), bytes_accessed=10**6, transcendentals=0
        ),
        name=name,
    )(*args, *after)


def sds(shape, dtype):
    return jax.ShapeDtypeStruct(shape, dtype)


def kv_kernel(rows_hbm, w_key_hbm, w_value_hbm, out, rows, w_key, w_value, sems):
    copies = [
        pltpu.make_async_copy(src, dst, sems.at[i])
        for i, (src, dst) in enumerate(
            ((rows_hbm, rows), (w_key_hbm, w_key), (w_value_hbm, w_value))
        )
    ]
    for copy in copies:
        copy.start()
    copies[0].wait()
    copies[1].wait()
    out[:, 0:128] = dot(rows[...], w_key[...], 1, 0).astype(BF16)
    copies[2].wait()
    out[:, 128:256] = dot(rows[...], w_value[...], 1, 0).astype(BF16)


def qd_kernel(anchors, cells, grad_a, grad_c, w_query, w_out, out):
    na = anchors.shape[0]
    wq = w_query[...]
    wo = w_out[...]
    for lo, rows, grads in ((0, anchors, grad_a), (na, cells, grad_c)):
        hi = lo + rows.shape[0]
        out[lo:hi, 0:128] = dot(rows[...], wq, 1, 0).astype(BF16) * SCALE
        out[lo:hi, 128:256] = dot(grads[...], wo, 1, 1).astype(BF16)


def stats_block(kv, rhs, before, out):
    total = rhs.shape[0] // 2
    keys = kv[:, 0:128]
    values = kv[:, 128:256]
    for tile in range(0, total, 256):
        cols = slice(tile, tile + 256)
        for h in range(2):
            lo = h * total + tile
            s = dot(keys, rhs[lo : lo + 256, 0:128], 1, 1)
            peak = jnp.max(s, axis=0, keepdims=True) * LOG2E
            if before is not None:
                old_peak = before[h : h + 1, cols]
                peak = jnp.maximum(peak, old_peak)
            e = jnp.exp2(s * LOG2E - peak)
            dp = dot(values, rhs[lo : lo + 256, 128:256], 1, 1)
            norm = jnp.sum(e, axis=0, keepdims=True)
            mass = jnp.sum(e * dp, axis=0, keepdims=True)
            if before is not None:
                factor = jnp.exp2(old_peak - peak)
                norm += factor * before[2 + h : 3 + h, cols]
                mass += factor * before[4 + h : 5 + h, cols]
            out[h : h + 1, cols] = peak
            out[2 + h : 3 + h, cols] = norm
            out[4 + h : 5 + h, cols] = mass


def first_stats_kernel(count, *refs):
    first, second = refs[:2]
    blocks = refs[2 : 2 + count]
    stats, rhs, kv = refs[2 + count :]
    half = first.shape[0]
    lane = lax.broadcasted_iota(jnp.int32, (1, 256), 1)
    for h in range(2):
        keep = lane // HEAD_DIM % 2 == h
        for part, rows in enumerate((first, second)):
            x = rows[...]
            lo = (2 * h + part) * half
            rhs[lo : lo + half, :] = jnp.where(keep, x, jnp.zeros_like(x))
    stats[0:2, :] = jnp.full((2, 2 * half), -1e30, F32)
    stats[2:8, :] = jnp.zeros((6, 2 * half), F32)
    if count == 1:
        stats_block(blocks[0], rhs, None, stats)
        return
    for i, block in enumerate(blocks):
        kv[i] = block[...]

    @pl.loop(0, count)
    def _(i):
        stats_block(kv.at[i], rhs, stats, stats)


def first_stats(first, second, blocks):
    total = 2 * first.shape[0]
    return call(
        functools.partial(first_stats_kernel, len(blocks)),
        [sds((8, total), F32), sds((2 * total, 256), BF16)],
        [first, second, *blocks],
        "first_stats",
        scratch=[pltpu.VMEM((len(blocks), *blocks[0].shape), BF16)],
    )


def next_stats_kernel(kv, rhs, before, stats):
    stats[6:8, :] = jnp.zeros((2, stats.shape[1]), F32)
    stats_block(kv, rhs, before, stats)


def both_stats_kernel(kv, rhs_a, rhs_b, before_a, before_b, stats):
    for lo in (6, 14):
        stats[lo : lo + 2, :] = jnp.zeros((2, stats.shape[1]), F32)
    stats_block(kv, rhs_a, before_a, stats.at[0:8])
    stats_block(kv, rhs_b, before_b, stats.at[8:16])


def merged(mine, theirs, a, b, i, j):
    for h in range(2):
        m1 = mine[i + h : i + h + 1, a]
        m2 = theirs[j + h : j + h + 1, b]
        peak = jnp.maximum(m1, m2)
        f1 = jnp.exp2(m1 - peak)
        f2 = jnp.exp2(m2 - peak)
        norm = f1 * mine[i + 2 + h : i + 3 + h, a] + f2 * theirs[j + 2 + h : j + 3 + h, b]
        mass = f1 * mine[i + 4 + h : i + 5 + h, a] + f2 * theirs[j + 4 + h : j + 5 + h, b]
        yield h, peak, norm, mass


def merge_cores_kernel(mine, theirs, out):
    half = mine.shape[1] // 2
    low, high = slice(0, half), slice(half, 2 * half)
    for i in (0, 8):
        for a, b in ((low, high), (high, low)):
            for h, peak, norm, mass in merged(mine, theirs, a, b, i, i):
                out[i + h : i + h + 1, a] = peak
                out[i + 2 + h : i + 3 + h, a] = norm
                out[i + 4 + h : i + 5 + h, a] = mass
        out[i + 6 : i + 8, :] = jnp.zeros((2, 2 * half), F32)


def merge_y_kernel(mine, theirs, out):
    whole = slice(0, mine.shape[1])
    for i, j in ((0, 8), (8, 0)):
        for h, peak, norm, mass in merged(mine, theirs, whole, whole, i, j):
            out[i + h : i + h + 1, whole] = peak + jnp.log(norm) * LOG2E
            out[i + 2 + h : i + 3 + h, whole] = mass / norm
        out[i + 4 : i + 8, :] = jnp.zeros((4, mine.shape[1]), F32)


def scores_kernel(has_before, is_last, *refs):
    first, second, *rhs = refs[:4]
    stats = refs[4]
    refs = refs[5:]
    before = None
    if has_before:
        before, refs = refs[0], refs[1:]
    p_t, ds_t, *dq, kv, keys_t = refs
    kv[: first.shape[0], :] = first[...]
    kv[first.shape[0] :, :] = second[...]
    total = rhs[0].shape[0] // 2
    half = total // 2
    n = kv.shape[0]
    keys_t[...] = kv[:, 0:128].T

    @pl.loop(0, 2)
    def _(h):
        here = pl.ds(pl.multiple_of(h * total, 128), total)
        out = pl.ds(pl.multiple_of(h * HEAD_DIM, HEAD_DIM), HEAD_DIM)
        for g in range(2):
            there = pl.ds(pl.multiple_of((2 * g + h) * total, 128), total)
            lse = stats[pl.ds(8 * g + h, 1), :]
            delta = stats[pl.ds(8 * g + 2 + h, 1), :]
            for c in range(0, n, STEP):
                s = dot(kv[c : c + STEP, 0:128], rhs[g][here, 0:128], 1, 1)
                p = jnp.exp2(s * LOG2E - lse)
                dp = dot(kv[c : c + STEP, 128:256], rhs[g][here, 128:256], 1, 1)
                ds = p * (dp - delta)
                p_t[c : c + STEP, there] = p.astype(BF16)
                ds_t[c : c + STEP, there] = ds.astype(BF16)
            cols = slice(g * total, (g + 1) * total)
            part = dot(keys_t[out, :], ds_t[:, there], 1, 0)
            if has_before:
                part += before[out, cols]
            if is_last:
                dq[2 * g][out, :] = part[:, :half].astype(dq[2 * g].dtype)
                dq[2 * g + 1][out, :] = part[:, half:].astype(BF16)
            else:
                dq[0][out, cols] = part


def scores(blocks, rhs, stats, before, is_last, after=()):
    total = rhs[0].shape[0] // 2
    n = sum(block.shape[0] for block in blocks)
    args = [*blocks, *rhs, stats] + ([] if before is None else [before])
    outs = [sds((n, 4 * total), BF16)] * 2
    if is_last:
        outs += [sds((128, total // 2), F32)] + [sds((128, total // 2), BF16)] * 3
    else:
        outs += [sds((128, 2 * total), F32)]
    return call(
        functools.partial(scores_kernel, before is not None, is_last),
        outs,
        args,
        "scores",
        scratch=[pltpu.VMEM((n, 256), BF16), pltpu.VMEM((128, n), BF16)],
        after=after,
    )


def pair_kernel(first, p_t, ds_t, rhs_a, rhs_b, *outs):
    n = rhs_a.shape[0]
    rows = slice(first, first + sum(out.shape[0] for out in outs))
    for cols, weights in ((slice(0, 128), ds_t), (slice(128, 256), p_t)):
        total = dot(weights[rows, :n], rhs_a[:, cols], 1, 0)
        total += dot(weights[rows, n:], rhs_b[:, cols], 1, 0)
        lo = 0
        for out in outs:
            out[:, cols] = total[lo : lo + out.shape[0]].astype(out.dtype)
            lo += out.shape[0]


def pair(weights, rhs, first, outs, after=()):
    return call(
        functools.partial(pair_kernel, first), outs, [*weights, *rhs], "pair", after=after
    )


def pair_sum_kernel(own, a, b, c, *outs):
    n = outs[0].shape[0]
    for i, out in enumerate(outs):
        rows = slice(i * n, (i + 1) * n)
        more = (a[rows, :].astype(F32) + b[rows, :].astype(F32)) + c[rows, :].astype(F32)
        out[...] = (own[rows, :] + more).astype(BF16)


def weights_kernel(distances, place, w_query, w_key, w_value, *outs):
    width = outs[0].shape[0]
    for r, out in zip(distances, outs):
        lo = pl.multiple_of(lax.rem(place[0] + r, X) * width, width)
        for i, w in enumerate((w_query, w_key, w_value)):
            out[:, i * 128 : (i + 1) * 128] = w[pl.ds(lo, width), :]


def stack_kernel(place, *refs):
    *parts, out = refs
    for side in range(2):
        y_hi = place[1] if side == 0 else 1 - place[1]
        rows = pl.ds(pl.multiple_of(y_hi * 128, 128), 128)
        here = slice(side * 128, (side + 1) * 128)
        for r, part in enumerate(parts):
            out[here, r * 128 : (r + 1) * 128] = part[rows, 0:128]
            lo = (X + 2 * r) * 128
            out[here, lo : lo + 256] = part[rows, 128:384]


def dq_sum_kernel(mine, a, b, c, dq, first):
    more = (a[...].astype(F32) + b[...].astype(F32)) + c[...].astype(F32)
    total = ((mine[...] + more) * SCALE).astype(BF16)
    dq[...] = total
    first[...] = total[:, : first.shape[1]]


def piece_sum_kernel(a, b, out):
    out[...] = (a[...].astype(F32) + b[...].astype(F32)).astype(BF16)


def cells_kernel(own, back_1, back_2a, back_2b, back_3, weights, mine, theirs, dq):
    na = own.shape[1] - mine.shape[0]
    cut = back_2a.shape[1]
    for r, part in ((0, own), (1, back_1), (3, back_3)):
        dq[r * 128 : (r + 1) * 128, :] = part[:, na:]
    dq[256:384, : cut - na] = back_2a[:, na:]
    dq[256:384, cut - na :] = back_2b[...]
    out = dot(dq[...], weights[:, : X * 128], 0, 1)
    mine[...] = out[:, 0:128]
    theirs[...] = out[:, 128:256].astype(BF16)


def anchors_kernel(*refs):
    dqs, dkvs, (weights, cells_mine, cells_theirs, mine, theirs, rows) = refs[:X], refs[X : 2 * X], refs[2 * X :]
    na = rows.shape[0]
    for r, (dq, dkv) in enumerate(zip(dqs, dkvs)):
        rows[:, r * 128 : (r + 1) * 128] = dq[:, :na].T
        lo = X * 128 + r * 256
        rows[:, lo : lo + 256] = dkv[...]
    out = dot(rows[...], weights[...], 1, 1)
    mine[:na, :] = out[:, 0:128]
    theirs[:na, :] = out[:, 128:256].astype(BF16)
    mine[na:, :] = cells_mine[...]
    theirs[na:, :] = cells_theirs[...]


def last_sum_kernel(mine, theirs, anchors, cells):
    na = anchors.shape[0]
    total = (mine[...] + theirs[...].astype(F32)).astype(BF16)
    anchors[...] = total[:na, :]
    cells[...] = total[na:, :]


def over_x(array):
    return [array] + [lax.ppermute(array, HEAD, SHIFT_X[r]) for r in range(1, X)]


def per_device(anchors, cells, w_query, w_key, w_value, w_out, grad_a, grad_c):
    na, nc, d = anchors.shape[0], cells.shape[0], anchors.shape[1]
    rows = na + nc
    total = 2 * rows
    place = jnp.stack([lax.axis_index("x"), lax.axis_index("y_hi")]).astype(jnp.int32)

    (kv,) = call(
        kv_kernel,
        [sds((na, 256), BF16)],
        [anchors, w_key, w_value],
        "kv",
        scratch=[
            pltpu.VMEM((na, d), BF16),
            pltpu.VMEM((d, 128), BF16),
            pltpu.VMEM((d, 128), BF16),
            pltpu.SemaphoreType.DMA((3,)),
        ],
        hbm=(0, 1, 2),
        vmem=60,
    )
    block = jnp.concatenate([lax.ppermute(kv, TOK, perm) for perm in GATHER], axis=0)
    blocks = [block] + [lax.ppermute(block, TOK, FORTH[j]) for j in range(1, HOPS + 1)]

    (mine,) = call(
        qd_kernel,
        [sds((rows, 256), BF16)],
        [anchors, cells, grad_a, grad_c, w_query, w_out],
        "qd",
        after=[place, kv],
    )
    core_rows = lax.ppermute(mine, TOK, SWAP_CORE)
    y_rows = lax.ppermute(mine, TOK, SWAP_Y)
    both_rows = lax.ppermute(y_rows, TOK, SWAP_CORE)

    stats_a, rhs_a = first_stats(mine, core_rows, blocks[:1])
    def weight_rows(distances, after):
        return call(
            functools.partial(weights_kernel, distances),
            [sds((d // X, 3 * 128), BF16)] * len(distances),
            [place, w_query, w_key, w_value],
            "weights",
            smem=1,
            after=after,
        )

    for j in range(1, HOPS):
        (stats_a,) = call(
            next_stats_kernel, [sds((8, total), F32)], [blocks[j], rhs_a, stats_a], "stats"
        )
    stats_b, rhs_b = first_stats(y_rows, both_rows, blocks[:HOPS])
    (stats,) = call(
        both_stats_kernel,
        [sds((16, total), F32)],
        [blocks[HOPS], rhs_a, rhs_b, stats_a, stats_b],
        "both_stats",
    )
    x_weights = weight_rows(tuple(range(X)), [stats])
    x_weights = [x_weights[0]] + [
        lax.ppermute(x_weights[r], HEAD, SHIFT_X[r]) for r in range(1, X)
    ]
    for merge_kernel, perm in ((merge_cores_kernel, SWAP_CORE), (merge_y_kernel, SWAP_Y)):
        (stats,) = call(
            merge_kernel,
            [sds((16, total), F32)],
            [stats, lax.ppermute(stats, TOK, perm)],
            "merge",
        )
    rhs = (rhs_a, rhs_b)
    n = block.shape[0]

    *weights, dq = scores(blocks[3:1:-1], rhs, stats, None, False)
    dkv_3, dkv_2 = pair(weights, rhs, 0, [sds((n, 256), BF16)] * 2)
    sums = [lax.ppermute(dkv_3, TOK, BACK[3]), lax.ppermute(dkv_2, TOK, BACK[2])]
    *weights, dq_mine, dq_core, dq_y, dq_both = scores(
        blocks[1::-1], rhs, stats, dq, True, after=[dkv_3, *x_weights[1:]]
    )
    dq_others = [
        lax.ppermute(part, TOK, perm)
        for part, perm in ((dq_y, SWAP_Y), (dq_both, SWAP_BOTH), (dq_core, SWAP_CORE))
    ]
    (dkv_1,) = pair(weights, rhs, 0, [sds((n, 256), BF16)], after=list(sums))
    sums.append(lax.ppermute(dkv_1, TOK, BACK[1]))
    (dkv,) = pair(weights, rhs, n, [sds((n, 256), F32)], after=[dkv_1])
    pieces = call(
        pair_sum_kernel, [sds((na, 256), BF16)] * len(RETURN), [dkv, *sums], "pair_sum"
    )
    pieces = [lax.ppermute(piece, TOK, perm) for piece, perm in zip(pieces, RETURN)]
    cut = 2 * 128
    dq, dq_first = call(
        dq_sum_kernel,
        [sds((128, rows), BF16), sds((128, cut), BF16)],
        [dq_mine, *dq_others],
        "dq_sum",
        after=[dkv],
    )
    (x_weights,) = call(
        stack_kernel,
        [sds((256, X * 384), BF16)],
        [place, *x_weights],
        "stack",
        smem=1,
        after=[dq],
    )
    back_1 = lax.ppermute(dq, HEAD, SHIFT_X[1])
    back_3 = lax.ppermute(dq, HEAD, SHIFT_X[3])
    back_2a = lax.ppermute(dq_first, HEAD, SHIFT_X[2])
    back_2b = lax.ppermute(back_3[:, cut:], HEAD, SHIFT_X[3])
    cells_mine, cells_theirs = call(
        cells_kernel,
        [sds((nc, 128), F32), sds((nc, 128), BF16)],
        [dq, back_1, back_2a, back_2b, back_3, x_weights],
        "cells",
        scratch=[pltpu.VMEM((X * 128, nc), BF16)],
    )
    (dkv,) = call(
        piece_sum_kernel, [sds((na, 256), BF16)], pieces, "piece_sum", after=[x_weights]
    )
    mine, theirs = call(
        anchors_kernel,
        [sds((rows, 128), F32), sds((rows, 128), BF16)],
        [dq, back_1, back_2a, back_3, *over_x(dkv), x_weights, cells_mine, cells_theirs],
        "anchors",
        scratch=[pltpu.VMEM((na, X * 384), BF16)],
    )
    return call(
        last_sum_kernel,
        [sds((na, 128), BF16), sds((nc, 128), BF16)],
        [mine, lax.ppermute(theirs, HEAD, SWAP_YH)],
        "last_sum",
    )


def solution(mesh):
    parts = jax.sharding.Mesh(mesh.devices.reshape(X, Y_HI, Y_LO, Z, CORES), (*HEAD, *TOK))
    return jax.shard_map(
        per_device,
        mesh=parts,
        in_specs=(
            P(TOK, None),
            P(TOK, None),
            P(None, HEAD),
            P(None, HEAD),
            P(None, HEAD),
            P(HEAD, None),
            P(TOK, None),
            P(TOK, None),
        ),
        out_specs=(P(TOK, HEAD), P(TOK, HEAD)),
        check_vma=False,
    )
```

```python
import functools

import jax
import jax.numpy as jnp
from jax import lax
from jax.experimental import pallas as pl
from jax.experimental.pallas import tpu as pltpu
from jax.sharding import PartitionSpec as P

HEAD_DIM = 64
SCALE = HEAD_DIM ** (-0.5)
LOG2E = 1.4426950408889634
Y_LO, Z, CORES = 2, 8, 2
X, Y_HI = 4, 2
HEAD = ("x", "y_hi")
TOK = ("y_lo", "z", "core")
STEP = 128
BF16 = jnp.bfloat16
F32 = jnp.float32
COST = {"scores": 15 * 10**8, "pair": 15 * 10**8, "anchors": 10**8}


def tok_perm(move):
    pairs = []
    for yl in range(Y_LO):
        for z in range(Z):
            for core in range(CORES):
                yl2, z2, core2 = move(yl, z, core)
                pairs.append(
                    ((yl * Z + z) * CORES + core, (yl2 * Z + z2 % Z) * CORES + core2)
                )
    return pairs


def head_perm(move):
    pairs = []
    for x in range(X):
        for yh in range(Y_HI):
            x2, yh2 = move(x, yh)
            pairs.append((x * Y_HI + yh, (x2 % X) * Y_HI + yh2))
    return pairs


SWAP_CORE = tok_perm(lambda yl, z, c: (yl, z, 1 - c))
SWAP_Y = tok_perm(lambda yl, z, c: (1 - yl, z, c))
SWAP_BOTH = tok_perm(lambda yl, z, c: (1 - yl, z, 1 - c))
GATHER = [
    tok_perm(lambda yl, z, c: (yl, z, 0) if c == 0 else (yl, z - 1, 1)),
    tok_perm(lambda yl, z, c: (yl, z - 1, 1) if c == 0 else (yl, z, 0)),
]
RETURN = [[(b, a) for a, b in perm] for perm in GATHER]
HOPS = 3
FORTH = [
    tok_perm(lambda yl, z, c, j=j: (yl, z + j, 0) if c == 0 else (yl, z - j, 1))
    for j in range(HOPS + 1)
]
BACK = [[(b, a) for a, b in perm] for perm in FORTH]
SHIFT_X = [head_perm(lambda x, yh, r=r: (x + r, yh)) for r in range(X)]
SWAP_YH = head_perm(lambda x, yh: (x, 1 - yh))


def dot(a, b, ca, cb):
    return lax.dot_general(a, b, (((ca,), (cb,)), ((), ())), preferred_element_type=F32)


def call(body, outs, args, name, scratch=(), smem=0, hbm=(), after=(), vmem=20):
    def spec(i):
        if i < smem:
            return pl.BlockSpec(memory_space=pltpu.SMEM)
        if i >= len(args):
            return pl.BlockSpec(memory_space=pl.ANY)
        return pl.BlockSpec(memory_space=pltpu.HBM if i in hbm else pltpu.VMEM)

    def kernel(*refs):
        body(*refs[: len(args)], *refs[len(args) + len(after) :])

    return pl.pallas_call(
        kernel,
        out_shape=tuple(outs),
        in_specs=[spec(i) for i in range(len(args) + len(after))],
        out_specs=tuple(pl.BlockSpec(memory_space=pltpu.VMEM) for _ in outs),
        scratch_shapes=list(scratch),
        compiler_params=pltpu.CompilerParams(vmem_limit_bytes=vmem << 20),
        cost_estimate=pl.CostEstimate(
            flops=COST.get(name, 10**10), bytes_accessed=10**6, transcendentals=0
        ),
        name=name,
    )(*args, *after)


def sds(shape, dtype):
    return jax.ShapeDtypeStruct(shape, dtype)


def kv_kernel(rows_hbm, w_key_hbm, w_value_hbm, out, rows, w_key, w_value, sems):
    copies = [
        pltpu.make_async_copy(src, dst, sems.at[i])
        for i, (src, dst) in enumerate(
            ((rows_hbm, rows), (w_key_hbm, w_key), (w_value_hbm, w_value))
        )
    ]
    for copy in copies:
        copy.start()
    copies[0].wait()
    copies[1].wait()
    out[:, 0:128] = dot(rows[...], w_key[...], 1, 0).astype(BF16)
    copies[2].wait()
    out[:, 128:256] = dot(rows[...], w_value[...], 1, 0).astype(BF16)


def qd_kernel(anchors, cells, grad_a, grad_c, w_query, w_out, out):
    na = anchors.shape[0]
    wq = w_query[...]
    wo = w_out[...]
    for lo, rows, grads in ((0, anchors, grad_a), (na, cells, grad_c)):
        hi = lo + rows.shape[0]
        out[lo:hi, 0:128] = dot(rows[...], wq, 1, 0).astype(BF16) * SCALE
        out[lo:hi, 128:256] = dot(grads[...], wo, 1, 1).astype(BF16)


def stats_block(kv, rhs, before, out):
    total = rhs.shape[0] // 2
    keys = kv[:, 0:128]
    values = kv[:, 128:256]
    for tile in range(0, total, 256):
        cols = slice(tile, tile + 256)
        for h in range(2):
            lo = h * total + tile
            s = dot(keys, rhs[lo : lo + 256, 0:128], 1, 1)
            peak = jnp.max(s, axis=0, keepdims=True) * LOG2E
            if before is not None:
                old_peak = before[h : h + 1, cols]
                peak = jnp.maximum(peak, old_peak)
            e = jnp.exp2(s * LOG2E - peak)
            dp = dot(values, rhs[lo : lo + 256, 128:256], 1, 1)
            norm = jnp.sum(e, axis=0, keepdims=True)
            mass = jnp.sum(e * dp, axis=0, keepdims=True)
            if before is not None:
                factor = jnp.exp2(old_peak - peak)
                norm += factor * before[2 + h : 3 + h, cols]
                mass += factor * before[4 + h : 5 + h, cols]
            out[h : h + 1, cols] = peak
            out[2 + h : 3 + h, cols] = norm
            out[4 + h : 5 + h, cols] = mass


def first_stats_kernel(count, *refs):
    first, second = refs[:2]
    blocks = refs[2 : 2 + count]
    stats, rhs, kv = refs[2 + count :]
    half = first.shape[0]
    lane = lax.broadcasted_iota(jnp.int32, (1, 256), 1)
    for h in range(2):
        keep = lane // HEAD_DIM % 2 == h
        for part, rows in enumerate((first, second)):
            x = rows[...]
            lo = (2 * h + part) * half
            rhs[lo : lo + half, :] = jnp.where(keep, x, jnp.zeros_like(x))
    stats[0:2, :] = jnp.full((2, 2 * half), -1e30, F32)
    stats[2:8, :] = jnp.zeros((6, 2 * half), F32)
    if count == 1:
        stats_block(blocks[0], rhs, None, stats)
        return
    for i, block in enumerate(blocks):
        kv[i] = block[...]

    @pl.loop(0, count)
    def _(i):
        stats_block(kv.at[i], rhs, stats, stats)


def first_stats(first, second, blocks):
    total = 2 * first.shape[0]
    return call(
        functools.partial(first_stats_kernel, len(blocks)),
        [sds((8, total), F32), sds((2 * total, 256), BF16)],
        [first, second, *blocks],
        "first_stats",
        scratch=[pltpu.VMEM((len(blocks), *blocks[0].shape), BF16)],
    )


def next_stats_kernel(kv, rhs, before, stats):
    stats[6:8, :] = jnp.zeros((2, stats.shape[1]), F32)
    stats_block(kv, rhs, before, stats)


def both_stats_kernel(kv, rhs_a, rhs_b, before_a, before_b, stats):
    for lo in (6, 14):
        stats[lo : lo + 2, :] = jnp.zeros((2, stats.shape[1]), F32)
    stats_block(kv, rhs_a, before_a, stats.at[0:8])
    stats_block(kv, rhs_b, before_b, stats.at[8:16])


def merged(mine, theirs, a, b, i, j):
    for h in range(2):
        m1 = mine[i + h : i + h + 1, a]
        m2 = theirs[j + h : j + h + 1, b]
        peak = jnp.maximum(m1, m2)
        f1 = jnp.exp2(m1 - peak)
        f2 = jnp.exp2(m2 - peak)
        norm = f1 * mine[i + 2 + h : i + 3 + h, a] + f2 * theirs[j + 2 + h : j + 3 + h, b]
        mass = f1 * mine[i + 4 + h : i + 5 + h, a] + f2 * theirs[j + 4 + h : j + 5 + h, b]
        yield h, peak, norm, mass


def merge_cores_kernel(mine, theirs, out):
    half = mine.shape[1] // 2
    low, high = slice(0, half), slice(half, 2 * half)
    for i in (0, 8):
        for a, b in ((low, high), (high, low)):
            for h, peak, norm, mass in merged(mine, theirs, a, b, i, i):
                out[i + h : i + h + 1, a] = peak
                out[i + 2 + h : i + 3 + h, a] = norm
                out[i + 4 + h : i + 5 + h, a] = mass
        out[i + 6 : i + 8, :] = jnp.zeros((2, 2 * half), F32)


def merge_y_kernel(mine, theirs, out):
    whole = slice(0, mine.shape[1])
    for i, j in ((0, 8), (8, 0)):
        for h, peak, norm, mass in merged(mine, theirs, whole, whole, i, j):
            out[i + h : i + h + 1, whole] = peak + jnp.log(norm) * LOG2E
            out[i + 2 + h : i + 3 + h, whole] = mass / norm
        out[i + 4 : i + 8, :] = jnp.zeros((4, mine.shape[1]), F32)


def scores_kernel(has_before, is_last, *refs):
    first, second, *rhs = refs[:4]
    stats = refs[4]
    refs = refs[5:]
    before = None
    if has_before:
        before, refs = refs[0], refs[1:]
    p_t, ds_t, *dq, kv, keys_t = refs
    kv[: first.shape[0], :] = first[...]
    kv[first.shape[0] :, :] = second[...]
    total = rhs[0].shape[0] // 2
    half = total // 2
    n = kv.shape[0]
    keys_t[...] = kv[:, 0:128].T

    @pl.loop(0, 2)
    def _(h):
        here = pl.ds(pl.multiple_of(h * total, 128), total)
        out = pl.ds(pl.multiple_of(h * HEAD_DIM, HEAD_DIM), HEAD_DIM)
        for g in range(2):
            there = pl.ds(pl.multiple_of((2 * g + h) * total, 128), total)
            lse = stats[pl.ds(8 * g + h, 1), :]
            delta = stats[pl.ds(8 * g + 2 + h, 1), :]
            for c in range(0, n, STEP):
                s = dot(kv[c : c + STEP, 0:128], rhs[g][here, 0:128], 1, 1)
                p = jnp.exp2(s * LOG2E - lse)
                dp = dot(kv[c : c + STEP, 128:256], rhs[g][here, 128:256], 1, 1)
                ds = p * (dp - delta)
                p_t[c : c + STEP, there] = p.astype(BF16)
                ds_t[c : c + STEP, there] = ds.astype(BF16)
            cols = slice(g * total, (g + 1) * total)
            part = dot(keys_t[out, :], ds_t[:, there], 1, 0)
            if has_before:
                part += before[out, cols]
            if is_last:
                dq[2 * g][out, :] = part[:, :half].astype(dq[2 * g].dtype)
                dq[2 * g + 1][out, :] = part[:, half:].astype(BF16)
            else:
                dq[0][out, cols] = part


def scores(blocks, rhs, stats, before, is_last, after=()):
    total = rhs[0].shape[0] // 2
    n = sum(block.shape[0] for block in blocks)
    args = [*blocks, *rhs, stats] + ([] if before is None else [before])
    outs = [sds((n, 4 * total), BF16)] * 2
    if is_last:
        outs += [sds((128, total // 2), F32)] + [sds((128, total // 2), BF16)] * 3
    else:
        outs += [sds((128, 2 * total), F32)]
    return call(
        functools.partial(scores_kernel, before is not None, is_last),
        outs,
        args,
        "scores",
        scratch=[pltpu.VMEM((n, 256), BF16), pltpu.VMEM((128, n), BF16)],
        after=after,
    )


def pair_kernel(first, p_t, ds_t, rhs_a, rhs_b, *outs):
    n = rhs_a.shape[0]
    rows = slice(first, first + sum(out.shape[0] for out in outs))
    for cols, weights in ((slice(0, 128), ds_t), (slice(128, 256), p_t)):
        total = dot(weights[rows, :n], rhs_a[:, cols], 1, 0)
        total += dot(weights[rows, n:], rhs_b[:, cols], 1, 0)
        lo = 0
        for out in outs:
            out[:, cols] = total[lo : lo + out.shape[0]].astype(out.dtype)
            lo += out.shape[0]


def pair(weights, rhs, first, outs, after=()):
    return call(
        functools.partial(pair_kernel, first), outs, [*weights, *rhs], "pair", after=after
    )


def pair_sum_kernel(own, a, b, c, *outs):
    n = outs[0].shape[0]
    for i, out in enumerate(outs):
        rows = slice(i * n, (i + 1) * n)
        more = (a[rows, :].astype(F32) + b[rows, :].astype(F32)) + c[rows, :].astype(F32)
        out[...] = (own[rows, :] + more).astype(BF16)


def weights_kernel(distances, place, w_query, w_key, w_value, *outs):
    width = outs[0].shape[0]
    for r, out in zip(distances, outs):
        lo = pl.multiple_of(lax.rem(place[0] + r, X) * width, width)
        for i, w in enumerate((w_query, w_key, w_value)):
            out[:, i * 128 : (i + 1) * 128] = w[pl.ds(lo, width), :]


def stack_kernel(place, *refs):
    *parts, out = refs
    for side in range(2):
        y_hi = place[1] if side == 0 else 1 - place[1]
        rows = pl.ds(pl.multiple_of(y_hi * 128, 128), 128)
        here = slice(side * 128, (side + 1) * 128)
        for r, part in enumerate(parts):
            out[here, r * 128 : (r + 1) * 128] = part[rows, 0:128]
            lo = (X + 2 * r) * 128
            out[here, lo : lo + 256] = part[rows, 128:384]


def dq_sum_kernel(mine, a, b, c, dq, first):
    more = (a[...].astype(F32) + b[...].astype(F32)) + c[...].astype(F32)
    total = ((mine[...] + more) * SCALE).astype(BF16)
    dq[...] = total
    first[...] = total[:, : first.shape[1]]


def piece_sum_kernel(a, b, out):
    out[...] = (a[...].astype(F32) + b[...].astype(F32)).astype(BF16)


def cells_kernel(own, back_1, back_2a, back_2b, back_3, weights, mine, theirs, dq):
    na = own.shape[1] - mine.shape[0]
    cut = back_2a.shape[1]
    for r, part in ((0, own), (1, back_1), (3, back_3)):
        dq[r * 128 : (r + 1) * 128, :] = part[:, na:]
    dq[256:384, : cut - na] = back_2a[:, na:]
    dq[256:384, cut - na :] = back_2b[...]
    out = dot(dq[...], weights[:, : X * 128], 0, 1)
    mine[...] = out[:, 0:128]
    theirs[...] = out[:, 128:256].astype(BF16)


def anchors_kernel(*refs):
    dqs, dkvs, (weights, cells_mine, cells_theirs, mine, theirs, rows) = refs[:X], refs[X : 2 * X], refs[2 * X :]
    na = rows.shape[0]
    for r, (dq, dkv) in enumerate(zip(dqs, dkvs)):
        rows[:, r * 128 : (r + 1) * 128] = dq[:, :na].T
        lo = X * 128 + r * 256
        rows[:, lo : lo + 256] = dkv[...]
    out = dot(rows[...], weights[...], 1, 1)
    mine[:na, :] = out[:, 0:128]
    theirs[:na, :] = out[:, 128:256].astype(BF16)
    mine[na:, :] = cells_mine[...]
    theirs[na:, :] = cells_theirs[...]


def last_sum_kernel(mine, theirs, anchors, cells):
    na = anchors.shape[0]
    total = (mine[...] + theirs[...].astype(F32)).astype(BF16)
    anchors[...] = total[:na, :]
    cells[...] = total[na:, :]


def over_x(array):
    return [array] + [lax.ppermute(array, HEAD, SHIFT_X[r]) for r in range(1, X)]


def per_device(anchors, cells, w_query, w_key, w_value, w_out, grad_a, grad_c):
    na, nc, d = anchors.shape[0], cells.shape[0], anchors.shape[1]
    rows = na + nc
    total = 2 * rows
    place = jnp.stack([lax.axis_index("x"), lax.axis_index("y_hi")]).astype(jnp.int32)

    (kv,) = call(
        kv_kernel,
        [sds((na, 256), BF16)],
        [anchors, w_key, w_value],
        "kv",
        scratch=[
            pltpu.VMEM((na, d), BF16),
            pltpu.VMEM((d, 128), BF16),
            pltpu.VMEM((d, 128), BF16),
            pltpu.SemaphoreType.DMA((3,)),
        ],
        hbm=(0, 1, 2),
        vmem=60,
    )
    block = jnp.concatenate([lax.ppermute(kv, TOK, perm) for perm in GATHER], axis=0)
    blocks = [block] + [lax.ppermute(block, TOK, FORTH[j]) for j in range(1, HOPS + 1)]

    (mine,) = call(
        qd_kernel,
        [sds((rows, 256), BF16)],
        [anchors, cells, grad_a, grad_c, w_query, w_out],
        "qd",
        after=[place, kv],
    )
    core_rows = lax.ppermute(mine, TOK, SWAP_CORE)
    y_rows = lax.ppermute(mine, TOK, SWAP_Y)
    both_rows = lax.ppermute(y_rows, TOK, SWAP_CORE)

    stats_a, rhs_a = first_stats(mine, core_rows, blocks[:1])
    def weight_rows(distances, after):
        return call(
            functools.partial(weights_kernel, distances),
            [sds((d // X, 3 * 128), BF16)] * len(distances),
            [place, w_query, w_key, w_value],
            "weights",
            smem=1,
            after=after,
        )

    for j in range(1, HOPS):
        (stats_a,) = call(
            next_stats_kernel, [sds((8, total), F32)], [blocks[j], rhs_a, stats_a], "stats"
        )
        if j == 1:
            own_weights, part = weight_rows((0, 1), [stats_a])
            x_weights = [own_weights, lax.ppermute(part, HEAD, SHIFT_X[1])]
    stats_b, rhs_b = first_stats(y_rows, both_rows, blocks[:HOPS])
    (stats,) = call(
        both_stats_kernel,
        [sds((16, total), F32)],
        [blocks[HOPS], rhs_a, rhs_b, stats_a, stats_b],
        "both_stats",
        after=x_weights[1:],
    )
    x_weights += [
        lax.ppermute(part, HEAD, SHIFT_X[r])
        for r, part in zip((2, 3), weight_rows((2, 3), [stats]))
    ]
    for merge_kernel, perm in ((merge_cores_kernel, SWAP_CORE), (merge_y_kernel, SWAP_Y)):
        (stats,) = call(
            merge_kernel,
            [sds((16, total), F32)],
            [stats, lax.ppermute(stats, TOK, perm)],
            "merge",
        )
    rhs = (rhs_a, rhs_b)
    n = block.shape[0]

    *weights, dq = scores(blocks[3:1:-1], rhs, stats, None, False)
    dkv_3, dkv_2 = pair(weights, rhs, 0, [sds((n, 256), BF16)] * 2)
    sums = [lax.ppermute(dkv_3, TOK, BACK[3]), lax.ppermute(dkv_2, TOK, BACK[2])]
    *weights, dq_mine, dq_core, dq_y, dq_both = scores(
        blocks[1::-1], rhs, stats, dq, True, after=[dkv_3, *x_weights[1:]]
    )
    dq_others = [
        lax.ppermute(part, TOK, perm)
        for part, perm in ((dq_y, SWAP_Y), (dq_both, SWAP_BOTH), (dq_core, SWAP_CORE))
    ]
    (dkv_1,) = pair(weights, rhs, 0, [sds((n, 256), BF16)])
    sums.append(lax.ppermute(dkv_1, TOK, BACK[1]))
    (dkv,) = pair(weights, rhs, n, [sds((n, 256), F32)], after=[dkv_1, *sums[:2]])
    cut = 2 * 128
    dq, dq_first = call(
        dq_sum_kernel,
        [sds((128, rows), BF16), sds((128, cut), BF16)],
        [dq_mine, *dq_others],
        "dq_sum",
        after=[dkv],
    )
    pieces = call(
        pair_sum_kernel, [sds((na, 256), BF16)] * len(RETURN), [dkv, *sums], "pair_sum", after=[dq]
    )
    pieces = [lax.ppermute(piece, TOK, perm) for piece, perm in zip(pieces, RETURN)]
    (x_weights,) = call(
        stack_kernel,
        [sds((256, X * 384), BF16)],
        [place, *x_weights],
        "stack",
        smem=1,
        after=[dq],
    )
    back_1 = lax.ppermute(dq, HEAD, SHIFT_X[1])
    back_3 = lax.ppermute(dq, HEAD, SHIFT_X[3])
    back_2a = lax.ppermute(dq_first, HEAD, SHIFT_X[2])
    back_2b = lax.ppermute(back_3[:, cut:], HEAD, SHIFT_X[3])
    cells_mine, cells_theirs = call(
        cells_kernel,
        [sds((nc, 128), F32), sds((nc, 128), BF16)],
        [dq, back_1, back_2a, back_2b, back_3, x_weights],
        "cells",
        scratch=[pltpu.VMEM((X * 128, nc), BF16)],
    )
    (dkv,) = call(
        piece_sum_kernel, [sds((na, 256), BF16)], pieces, "piece_sum", after=[x_weights]
    )
    mine, theirs = call(
        anchors_kernel,
        [sds((rows, 128), F32), sds((rows, 128), BF16)],
        [dq, back_1, back_2a, back_3, *over_x(dkv), x_weights, cells_mine, cells_theirs],
        "anchors",
        scratch=[pltpu.VMEM((na, X * 384), BF16)],
    )
    return call(
        last_sum_kernel,
        [sds((na, 128), BF16), sds((nc, 128), BF16)],
        [mine, lax.ppermute(theirs, HEAD, SWAP_YH)],
        "last_sum",
    )


def solution(mesh):
    parts = jax.sharding.Mesh(mesh.devices.reshape(X, Y_HI, Y_LO, Z, CORES), (*HEAD, *TOK))
    return jax.shard_map(
        per_device,
        mesh=parts,
        in_specs=(
            P(TOK, None),
            P(TOK, None),
            P(None, HEAD),
            P(None, HEAD),
            P(None, HEAD),
            P(HEAD, None),
            P(TOK, None),
            P(TOK, None),
        ),
        out_specs=(P(TOK, HEAD), P(TOK, HEAD)),
        check_vma=False,
    )
```

```python
import functools

import jax
import jax.numpy as jnp
from jax import lax
from jax.experimental import pallas as pl
from jax.experimental.pallas import tpu as pltpu
from jax.sharding import PartitionSpec as P

HEAD_DIM = 64
SCALE = HEAD_DIM ** (-0.5)
LOG2E = 1.4426950408889634
Y_LO, Z, CORES = 2, 8, 2
X, Y_HI = 4, 2
HEAD = ("x", "y_hi")
TOK = ("y_lo", "z", "core")
STEP = 128
BF16 = jnp.bfloat16
F32 = jnp.float32
COST = {"scores": 15 * 10**8, "pair": 15 * 10**8, "anchors": 10**8}


def tok_perm(move):
    pairs = []
    for yl in range(Y_LO):
        for z in range(Z):
            for core in range(CORES):
                yl2, z2, core2 = move(yl, z, core)
                pairs.append(
                    ((yl * Z + z) * CORES + core, (yl2 * Z + z2 % Z) * CORES + core2)
                )
    return pairs


def head_perm(move):
    pairs = []
    for x in range(X):
        for yh in range(Y_HI):
            x2, yh2 = move(x, yh)
            pairs.append((x * Y_HI + yh, (x2 % X) * Y_HI + yh2))
    return pairs


SWAP_CORE = tok_perm(lambda yl, z, c: (yl, z, 1 - c))
SWAP_Y = tok_perm(lambda yl, z, c: (1 - yl, z, c))
SWAP_BOTH = tok_perm(lambda yl, z, c: (1 - yl, z, 1 - c))
GATHER = [
    tok_perm(lambda yl, z, c: (yl, z, 0) if c == 0 else (yl, z - 1, 1)),
    tok_perm(lambda yl, z, c: (yl, z - 1, 1) if c == 0 else (yl, z, 0)),
]
RETURN = [[(b, a) for a, b in perm] for perm in GATHER]
HOPS = 3
FORTH = [
    tok_perm(lambda yl, z, c, j=j: (yl, z + j, 0) if c == 0 else (yl, z - j, 1))
    for j in range(HOPS + 1)
]
BACK = [[(b, a) for a, b in perm] for perm in FORTH]
SHIFT_X = [head_perm(lambda x, yh, r=r: (x + r, yh)) for r in range(X)]
SWAP_YH = head_perm(lambda x, yh: (x, 1 - yh))


def dot(a, b, ca, cb):
    return lax.dot_general(a, b, (((ca,), (cb,)), ((), ())), preferred_element_type=F32)


def call(body, outs, args, name, scratch=(), smem=0, hbm=(), after=(), vmem=20):
    def spec(i):
        if i < smem:
            return pl.BlockSpec(memory_space=pltpu.SMEM)
        if i >= len(args):
            return pl.BlockSpec(memory_space=pl.ANY)
        return pl.BlockSpec(memory_space=pltpu.HBM if i in hbm else pltpu.VMEM)

    def kernel(*refs):
        body(*refs[: len(args)], *refs[len(args) + len(after) :])

    return pl.pallas_call(
        kernel,
        out_shape=tuple(outs),
        in_specs=[spec(i) for i in range(len(args) + len(after))],
        out_specs=tuple(pl.BlockSpec(memory_space=pltpu.VMEM) for _ in outs),
        scratch_shapes=list(scratch),
        compiler_params=pltpu.CompilerParams(vmem_limit_bytes=vmem << 20),
        cost_estimate=pl.CostEstimate(
            flops=COST.get(name, 10**10), bytes_accessed=10**6, transcendentals=0
        ),
        name=name,
    )(*args, *after)


def sds(shape, dtype):
    return jax.ShapeDtypeStruct(shape, dtype)


def kv_kernel(rows_hbm, w_key_hbm, w_value_hbm, out, rows, w_key, w_value, sems):
    copies = [
        pltpu.make_async_copy(src, dst, sems.at[i])
        for i, (src, dst) in enumerate(
            ((rows_hbm, rows), (w_key_hbm, w_key), (w_value_hbm, w_value))
        )
    ]
    for copy in copies:
        copy.start()
    copies[0].wait()
    copies[1].wait()
    out[:, 0:128] = dot(rows[...], w_key[...], 1, 0).astype(BF16)
    copies[2].wait()
    out[:, 128:256] = dot(rows[...], w_value[...], 1, 0).astype(BF16)


def qd_kernel(anchors, cells, grad_a, grad_c, w_query, w_out, out):
    na = anchors.shape[0]
    wq = w_query[...]
    wo = w_out[...]
    for lo, rows, grads in ((0, anchors, grad_a), (na, cells, grad_c)):
        hi = lo + rows.shape[0]
        out[lo:hi, 0:128] = dot(rows[...], wq, 1, 0).astype(BF16) * SCALE
        out[lo:hi, 128:256] = dot(grads[...], wo, 1, 1).astype(BF16)


def stats_block(kv, rhs, before, out):
    total = rhs.shape[0] // 2
    keys = kv[:, 0:128]
    values = kv[:, 128:256]
    for tile in range(0, total, 256):
        cols = slice(tile, tile + 256)
        for h in range(2):
            lo = h * total + tile
            s = dot(keys, rhs[lo : lo + 256, 0:128], 1, 1)
            peak = jnp.max(s, axis=0, keepdims=True) * LOG2E
            if before is not None:
                old_peak = before[h : h + 1, cols]
                peak = jnp.maximum(peak, old_peak)
            e = jnp.exp2(s * LOG2E - peak)
            dp = dot(values, rhs[lo : lo + 256, 128:256], 1, 1)
            norm = jnp.sum(e, axis=0, keepdims=True)
            mass = jnp.sum(e * dp, axis=0, keepdims=True)
            if before is not None:
                factor = jnp.exp2(old_peak - peak)
                norm += factor * before[2 + h : 3 + h, cols]
                mass += factor * before[4 + h : 5 + h, cols]
            out[h : h + 1, cols] = peak
            out[2 + h : 3 + h, cols] = norm
            out[4 + h : 5 + h, cols] = mass


def first_stats_kernel(count, *refs):
    first, second = refs[:2]
    blocks = refs[2 : 2 + count]
    stats, rhs, kv = refs[2 + count :]
    half = first.shape[0]
    lane = lax.broadcasted_iota(jnp.int32, (1, 256), 1)
    for h in range(2):
        keep = lane // HEAD_DIM % 2 == h
        for part, rows in enumerate((first, second)):
            x = rows[...]
            lo = (2 * h + part) * half
            rhs[lo : lo + half, :] = jnp.where(keep, x, jnp.zeros_like(x))
    stats[0:2, :] = jnp.full((2, 2 * half), -1e30, F32)
    stats[2:8, :] = jnp.zeros((6, 2 * half), F32)
    if count == 1:
        stats_block(blocks[0], rhs, None, stats)
        return
    for i, block in enumerate(blocks):
        kv[i] = block[...]

    @pl.loop(0, count)
    def _(i):
        stats_block(kv.at[i], rhs, stats, stats)


def first_stats(first, second, blocks):
    total = 2 * first.shape[0]
    return call(
        functools.partial(first_stats_kernel, len(blocks)),
        [sds((8, total), F32), sds((2 * total, 256), BF16)],
        [first, second, *blocks],
        "first_stats",
        scratch=[pltpu.VMEM((len(blocks), *blocks[0].shape), BF16)],
    )


def next_stats_kernel(kv, rhs, before, stats):
    stats[6:8, :] = jnp.zeros((2, stats.shape[1]), F32)
    stats_block(kv, rhs, before, stats)


def both_stats_kernel(kv, rhs_a, rhs_b, before_a, before_b, stats):
    for lo in (6, 14):
        stats[lo : lo + 2, :] = jnp.zeros((2, stats.shape[1]), F32)
    stats_block(kv, rhs_a, before_a, stats.at[0:8])
    stats_block(kv, rhs_b, before_b, stats.at[8:16])


def merged(mine, theirs, a, b, i, j):
    for h in range(2):
        m1 = mine[i + h : i + h + 1, a]
        m2 = theirs[j + h : j + h + 1, b]
        peak = jnp.maximum(m1, m2)
        f1 = jnp.exp2(m1 - peak)
        f2 = jnp.exp2(m2 - peak)
        norm = f1 * mine[i + 2 + h : i + 3 + h, a] + f2 * theirs[j + 2 + h : j + 3 + h, b]
        mass = f1 * mine[i + 4 + h : i + 5 + h, a] + f2 * theirs[j + 4 + h : j + 5 + h, b]
        yield h, peak, norm, mass


def merge_cores_kernel(mine, theirs, out):
    half = mine.shape[1] // 2
    low, high = slice(0, half), slice(half, 2 * half)
    for i in (0, 8):
        for a, b in ((low, high), (high, low)):
            for h, peak, norm, mass in merged(mine, theirs, a, b, i, i):
                out[i + h : i + h + 1, a] = peak
                out[i + 2 + h : i + 3 + h, a] = norm
                out[i + 4 + h : i + 5 + h, a] = mass
        out[i + 6 : i + 8, :] = jnp.zeros((2, 2 * half), F32)


def merge_y_kernel(mine, theirs, out):
    whole = slice(0, mine.shape[1])
    for i, j in ((0, 8), (8, 0)):
        for h, peak, norm, mass in merged(mine, theirs, whole, whole, i, j):
            out[i + h : i + h + 1, whole] = peak + jnp.log(norm) * LOG2E
            out[i + 2 + h : i + 3 + h, whole] = mass / norm
        out[i + 4 : i + 8, :] = jnp.zeros((4, mine.shape[1]), F32)


def scores_kernel(has_before, is_last, *refs):
    first, second, *rhs = refs[:4]
    stats = refs[4]
    refs = refs[5:]
    before = None
    if has_before:
        before, refs = refs[0], refs[1:]
    p_t, ds_t, *dq, kv, keys_t = refs
    kv[: first.shape[0], :] = first[...]
    kv[first.shape[0] :, :] = second[...]
    total = rhs[0].shape[0] // 2
    half = total // 2
    n = kv.shape[0]
    keys_t[...] = kv[:, 0:128].T

    @pl.loop(0, 2)
    def _(h):
        here = pl.ds(pl.multiple_of(h * total, 128), total)
        out = pl.ds(pl.multiple_of(h * HEAD_DIM, HEAD_DIM), HEAD_DIM)
        for g in range(2):
            there = pl.ds(pl.multiple_of((2 * g + h) * total, 128), total)
            lse = stats[pl.ds(8 * g + h, 1), :]
            delta = stats[pl.ds(8 * g + 2 + h, 1), :]
            for c in range(0, n, STEP):
                s = dot(kv[c : c + STEP, 0:128], rhs[g][here, 0:128], 1, 1)
                p = jnp.exp2(s * LOG2E - lse)
                dp = dot(kv[c : c + STEP, 128:256], rhs[g][here, 128:256], 1, 1)
                ds = p * (dp - delta)
                p_t[c : c + STEP, there] = p.astype(BF16)
                ds_t[c : c + STEP, there] = ds.astype(BF16)
            cols = slice(g * total, (g + 1) * total)
            part = dot(keys_t[out, :], ds_t[:, there], 1, 0)
            if has_before:
                part += before[out, cols]
            if is_last:
                dq[2 * g][out, :] = part[:, :half].astype(dq[2 * g].dtype)
                dq[2 * g + 1][out, :] = part[:, half:].astype(BF16)
            else:
                dq[0][out, cols] = part


def scores(blocks, rhs, stats, before, is_last, after=()):
    total = rhs[0].shape[0] // 2
    n = sum(block.shape[0] for block in blocks)
    args = [*blocks, *rhs, stats] + ([] if before is None else [before])
    outs = [sds((n, 4 * total), BF16)] * 2
    if is_last:
        outs += [sds((128, total // 2), F32)] + [sds((128, total // 2), BF16)] * 3
    else:
        outs += [sds((128, 2 * total), F32)]
    return call(
        functools.partial(scores_kernel, before is not None, is_last),
        outs,
        args,
        "scores",
        scratch=[pltpu.VMEM((n, 256), BF16), pltpu.VMEM((128, n), BF16)],
        after=after,
    )


def pair_kernel(first, p_t, ds_t, rhs_a, rhs_b, *outs):
    n = rhs_a.shape[0]
    rows = slice(first, first + sum(out.shape[0] for out in outs))
    for cols, weights in ((slice(0, 128), ds_t), (slice(128, 256), p_t)):
        total = dot(weights[rows, :n], rhs_a[:, cols], 1, 0)
        total += dot(weights[rows, n:], rhs_b[:, cols], 1, 0)
        lo = 0
        for out in outs:
            out[:, cols] = total[lo : lo + out.shape[0]].astype(out.dtype)
            lo += out.shape[0]


def pair(weights, rhs, first, outs, after=()):
    return call(
        functools.partial(pair_kernel, first), outs, [*weights, *rhs], "pair", after=after
    )


def pair_sum_kernel(own, a, b, c, *outs):
    n = outs[0].shape[0]
    for i, out in enumerate(outs):
        rows = slice(i * n, (i + 1) * n)
        more = (a[rows, :].astype(F32) + b[rows, :].astype(F32)) + c[rows, :].astype(F32)
        out[...] = (own[rows, :] + more).astype(BF16)


def weights_kernel(distances, place, w_query, w_key, w_value, *outs):
    width = outs[0].shape[0]
    for r, out in zip(distances, outs):
        lo = pl.multiple_of(lax.rem(place[0] + r, X) * width, width)
        for i, w in enumerate((w_query, w_key, w_value)):
            out[:, i * 128 : (i + 1) * 128] = w[pl.ds(lo, width), :]


def stack_kernel(place, *refs):
    *parts, out = refs
    for side in range(2):
        y_hi = place[1] if side == 0 else 1 - place[1]
        rows = pl.ds(pl.multiple_of(y_hi * 128, 128), 128)
        here = slice(side * 128, (side + 1) * 128)
        for r, part in enumerate(parts):
            out[here, r * 128 : (r + 1) * 128] = part[rows, 0:128]
            lo = (X + 2 * r) * 128
            out[here, lo : lo + 256] = part[rows, 128:384]


def dq_sum_kernel(mine, a, b, c, dq, first):
    more = (a[...].astype(F32) + b[...].astype(F32)) + c[...].astype(F32)
    total = ((mine[...] + more) * SCALE).astype(BF16)
    dq[...] = total
    first[...] = total[:, : first.shape[1]]


def piece_sum_kernel(a, b, out):
    out[...] = (a[...].astype(F32) + b[...].astype(F32)).astype(BF16)


def cells_kernel(own, back_1, back_2a, back_2b, back_3, weights, mine, theirs, dq):
    na = own.shape[1] - mine.shape[0]
    cut = back_2a.shape[1]
    for r, part in ((0, own), (1, back_1), (3, back_3)):
        dq[r * 128 : (r + 1) * 128, :] = part[:, na:]
    dq[256:384, : cut - na] = back_2a[:, na:]
    dq[256:384, cut - na :] = back_2b[...]
    out = dot(dq[...], weights[:, : X * 128], 0, 1)
    mine[...] = out[:, 0:128]
    theirs[...] = out[:, 128:256].astype(BF16)


def anchors_kernel(*refs):
    dqs, dkvs, (weights, cells_mine, cells_theirs, mine, theirs, rows) = refs[:X], refs[X : 2 * X], refs[2 * X :]
    na = rows.shape[0]
    for r, (dq, dkv) in enumerate(zip(dqs, dkvs)):
        rows[:, r * 128 : (r + 1) * 128] = dq[:, :na].T
        lo = X * 128 + r * 256
        rows[:, lo : lo + 256] = dkv[...]
    out = dot(rows[...], weights[...], 1, 1)
    mine[:na, :] = out[:, 0:128]
    theirs[:na, :] = out[:, 128:256].astype(BF16)
    mine[na:, :] = cells_mine[...]
    theirs[na:, :] = cells_theirs[...]


def last_sum_kernel(mine, theirs, anchors, cells):
    na = anchors.shape[0]
    total = (mine[...] + theirs[...].astype(F32)).astype(BF16)
    anchors[...] = total[:na, :]
    cells[...] = total[na:, :]


def over_x(array):
    return [array] + [lax.ppermute(array, HEAD, SHIFT_X[r]) for r in range(1, X)]


def per_device(anchors, cells, w_query, w_key, w_value, w_out, grad_a, grad_c):
    na, nc, d = anchors.shape[0], cells.shape[0], anchors.shape[1]
    rows = na + nc
    total = 2 * rows
    place = jnp.stack([lax.axis_index("x"), lax.axis_index("y_hi")]).astype(jnp.int32)

    (kv,) = call(
        kv_kernel,
        [sds((na, 256), BF16)],
        [anchors, w_key, w_value],
        "kv",
        scratch=[
            pltpu.VMEM((na, d), BF16),
            pltpu.VMEM((d, 128), BF16),
            pltpu.VMEM((d, 128), BF16),
            pltpu.SemaphoreType.DMA((3,)),
        ],
        hbm=(0, 1, 2),
        vmem=60,
    )
    block = jnp.concatenate([lax.ppermute(kv, TOK, perm) for perm in GATHER], axis=0)
    blocks = [block] + [lax.ppermute(block, TOK, FORTH[j]) for j in range(1, HOPS + 1)]

    (mine,) = call(
        qd_kernel,
        [sds((rows, 256), BF16)],
        [anchors, cells, grad_a, grad_c, w_query, w_out],
        "qd",
        after=[place, kv],
    )
    core_rows = lax.ppermute(mine, TOK, SWAP_CORE)
    y_rows = lax.ppermute(mine, TOK, SWAP_Y)
    both_rows = lax.ppermute(y_rows, TOK, SWAP_CORE)

    stats_a, rhs_a = first_stats(mine, core_rows, blocks[:1])
    def weight_rows(distances, after):
        return call(
            functools.partial(weights_kernel, distances),
            [sds((d // X, 3 * 128), BF16)] * len(distances),
            [place, w_query, w_key, w_value],
            "weights",
            smem=1,
            after=after,
        )

    for j in range(1, HOPS):
        (stats_a,) = call(
            next_stats_kernel, [sds((8, total), F32)], [blocks[j], rhs_a, stats_a], "stats"
        )
        if j == 1:
            own_weights, part = weight_rows((0, 1), [stats_a])
            x_weights = [own_weights, lax.ppermute(part, HEAD, SHIFT_X[1])]
    stats_b, rhs_b = first_stats(y_rows, both_rows, blocks[:HOPS])
    (stats,) = call(
        both_stats_kernel,
        [sds((16, total), F32)],
        [blocks[HOPS], rhs_a, rhs_b, stats_a, stats_b],
        "both_stats",
        after=x_weights[1:],
    )
    x_weights += [
        lax.ppermute(part, HEAD, SHIFT_X[r])
        for r, part in zip((2, 3), weight_rows((2, 3), [stats]))
    ]
    for merge_kernel, perm in ((merge_cores_kernel, SWAP_CORE), (merge_y_kernel, SWAP_Y)):
        (stats,) = call(
            merge_kernel,
            [sds((16, total), F32)],
            [stats, lax.ppermute(stats, TOK, perm)],
            "merge",
        )
    rhs = (rhs_a, rhs_b)
    n = block.shape[0]

    *weights, dq = scores(blocks[3:1:-1], rhs, stats, None, False)
    dkv_3, dkv_2 = pair(weights, rhs, 0, [sds((n, 256), BF16)] * 2)
    sums = [lax.ppermute(dkv_3, TOK, BACK[3]), lax.ppermute(dkv_2, TOK, BACK[2])]
    *weights, dq_mine, dq_core, dq_y, dq_both = scores(
        blocks[1::-1], rhs, stats, dq, True, after=[dkv_3, *x_weights[1:]]
    )
    dq_others = [
        lax.ppermute(part, TOK, perm)
        for part, perm in ((dq_y, SWAP_Y), (dq_both, SWAP_BOTH), (dq_core, SWAP_CORE))
    ]
    (dkv_1,) = pair(weights, rhs, 0, [sds((n, 256), BF16)])
    sums.append(lax.ppermute(dkv_1, TOK, BACK[1]))
    (dkv,) = pair(weights, rhs, n, [sds((n, 256), F32)], after=[dkv_1, *sums[:2]])
    (x_weights,) = call(
        stack_kernel,
        [sds((256, X * 384), BF16)],
        [place, *x_weights],
        "stack",
        smem=1,
        after=[dkv],
    )
    cut = 2 * 128
    dq, dq_first = call(
        dq_sum_kernel,
        [sds((128, rows), BF16), sds((128, cut), BF16)],
        [dq_mine, *dq_others],
        "dq_sum",
        after=[dkv, x_weights],
    )
    pieces = call(
        pair_sum_kernel, [sds((na, 256), BF16)] * len(RETURN), [dkv, *sums], "pair_sum", after=[dq]
    )
    pieces = [lax.ppermute(piece, TOK, perm) for piece, perm in zip(pieces, RETURN)]
    back_1 = lax.ppermute(dq, HEAD, SHIFT_X[1])
    back_3 = lax.ppermute(dq, HEAD, SHIFT_X[3])
    back_2a = lax.ppermute(dq_first, HEAD, SHIFT_X[2])
    back_2b = lax.ppermute(back_3[:, cut:], HEAD, SHIFT_X[3])
    cells_mine, cells_theirs = call(
        cells_kernel,
        [sds((nc, 128), F32), sds((nc, 128), BF16)],
        [dq, back_1, back_2a, back_2b, back_3, x_weights],
        "cells",
        scratch=[pltpu.VMEM((X * 128, nc), BF16)],
    )
    (dkv,) = call(
        piece_sum_kernel, [sds((na, 256), BF16)], pieces, "piece_sum", after=[x_weights]
    )
    mine, theirs = call(
        anchors_kernel,
        [sds((rows, 128), F32), sds((rows, 128), BF16)],
        [dq, back_1, back_2a, back_3, *over_x(dkv), x_weights, cells_mine, cells_theirs],
        "anchors",
        scratch=[pltpu.VMEM((na, X * 384), BF16)],
    )
    return call(
        last_sum_kernel,
        [sds((na, 128), BF16), sds((nc, 128), BF16)],
        [mine, lax.ppermute(theirs, HEAD, SWAP_YH)],
        "last_sum",
    )


def solution(mesh):
    parts = jax.sharding.Mesh(mesh.devices.reshape(X, Y_HI, Y_LO, Z, CORES), (*HEAD, *TOK))
    return jax.shard_map(
        per_device,
        mesh=parts,
        in_specs=(
            P(TOK, None),
            P(TOK, None),
            P(None, HEAD),
            P(None, HEAD),
            P(None, HEAD),
            P(HEAD, None),
            P(TOK, None),
            P(TOK, None),
        ),
        out_specs=(P(TOK, HEAD), P(TOK, HEAD)),
        check_vma=False,
    )
```
